32 devices in a mesh: section: 4 (over y, x), seq: 2 (over core), dp: 4 (over z).
Axes of the slice: x: 2, y: 2, z: 4, core: 2. Of those that a mesh axis runs over, the one named last changes fastest.
Arguments:
- bases: int32 [8, 3072, 128], P('dp', 'seq'), may hold values from 0 to 3
- targets: int32 [8, 3072, 4096], P('dp', 'seq', 'section'), may hold values from 0 to 2
- stem_weight: bfloat16 [512, 384], replicated, may hold values from -0.5 to 0.5
- conv_weight: bfloat16 [4, 3, 384, 192], P('section'), may hold values from -0.1875 to 0.1875
- proj_weight: bfloat16 [4, 192, 384], P('section'), may hold values from -0.4375 to 0.4375
- head_weight: bfloat16 [384, 4096], P(None, 'section'), may hold values from -0.078125 to 0.078125
Outputs:
- conv_grad: float32 [4, 3, 384, 192], P('section')
- proj_grad: float32 [4, 192, 384], P('section')
- head_grad: float32 [384, 4096], P(None, 'section')
The draws below stay inside these ranges and needn't reach their ends.
All inputs are finite; a program needn't handle non-finite values.
Results may differ from the reference program's by a relative error of at most 0.0014.
Values may be sent and summed in bfloat16 or wider, within the bound.
A program may use at most 128 MiB of HBM per device.

```python
import math
import jax
import jax.numpy as jnp
from jax import lax

CHANNELS = 384
INNER = 192
BIN_BASES = 128
LEN = 3072
DILATION_START = 192
LAYERS = 4
OUTPUT_TRACKS = 4096
BATCH = 8
N_SECTION = 4


def touch_ends(result, key, least, high):
    place = [jax.random.randint(jax.random.fold_in(key, axis), (), 0, length) for axis, length in enumerate(result.shape)]
    longest = result.shape.index(max(result.shape))
    neighbour = place[:longest] + [(place[longest] + 1) % result.shape[longest]] + place[longest + 1:]
    return result.at[tuple(place)].set(least).at[tuple(neighbour)].set(high)


def level_of(stream_key, extent, split, smallest, largest):
    gain, own = 1.0, jax.random.fold_in(stream_key, 6)
    for dim, blocks in split:
        heights = jnp.exp(jax.random.uniform(jax.random.fold_in(own, dim), (blocks,), jnp.float32, smallest / len(split), largest / len(split)))
        gain = gain * jnp.repeat(heights, extent[dim] // blocks).reshape([-1 if axis == dim else 1 for axis in range(len(extent))])
    return gain


def normal_values(rng, dims, spread, most, pieces=(), held_as=jnp.bfloat16):
    drawn = jax.random.normal(rng, dims, jnp.float32) * spread
    if len(pieces) > 0:
        drawn = level_of(rng, dims, pieces, -0.22, 0.18) * drawn
    return jnp.clip(drawn, min=-most, max=most).astype(held_as)


def setup_inputs(seed: int = 0) -> dict:
    key_list = jax.random.split(jax.random.key(seed), 7)
    bases = touch_ends(jax.random.randint(key_list[0], (BATCH, LEN, BIN_BASES), 0, 4), jax.random.fold_in(key_list[0], 1), 0, 3).astype(jnp.int32)
    targets = touch_ends(jax.random.randint(key_list[1], (BATCH, LEN, OUTPUT_TRACKS), 0, 3), jax.random.fold_in(key_list[1], 1), 0, 2).astype(jnp.int32)
    stem_weight = normal_values(key_list[2], (4 * BIN_BASES, CHANNELS), BIN_BASES ** -0.5, 0.5)
    conv_weight = normal_values(key_list[3], (LAYERS, 3, CHANNELS, INNER), (3 * CHANNELS) ** -0.5, 0.1875, ((0, 4),))
    proj_weight = normal_values(key_list[4], (LAYERS, INNER, CHANNELS), INNER ** -0.5, 0.4375, ((0, 4),))
    head_weight = normal_values(key_list[5], (CHANNELS, OUTPUT_TRACKS), (16 * CHANNELS) ** -0.5, 0.078125, ((1, 4),))
    return dict(bases=bases, targets=targets, stem_weight=stem_weight, conv_weight=conv_weight, proj_weight=proj_weight, head_weight=head_weight)


SQRT_TWO_OVER_PI = 0.7978845608028654
CUBIC_TERM = 0.044715

def gelu_value(inputs):
    return 0.5 * inputs * (1.0 + jnp.tanh(SQRT_TWO_OVER_PI * (inputs + CUBIC_TERM * inputs * inputs * inputs)))

def gelu_slope(inputs):
    tangent = jnp.tanh(SQRT_TWO_OVER_PI * (inputs + CUBIC_TERM * inputs * inputs * inputs))
    return 0.5 * (1.0 + tangent) + 0.5 * inputs * (1.0 - tangent * tangent) * SQRT_TWO_OVER_PI * (1.0 + 3.0 * CUBIC_TERM * inputs * inputs)

def flatten(values):
    return values.reshape(-1, values.shape[-1])

def contract_rows(left_side, right_side):
    return lax.dot_general(flatten(left_side), flatten(right_side), (((0,), (0,)), ((), ())), preferred_element_type=jnp.float32)

def times_transposed(left_side, right_side):
    return lax.dot_general(left_side, right_side, (((1,), (1,)), ((), ())), preferred_element_type=jnp.float32)

def shifted(values, dilation_rate):
    padding = jnp.zeros((values.shape[0], dilation_rate, values.shape[2]), values.dtype)
    behind = jnp.concatenate([padding, values[:, :-dilation_rate]], 1)
    forward = jnp.concatenate([values[:, dilation_rate:], padding], 1)
    return (behind, forward)

def reference(bases, targets, stem_weight, conv_weight, proj_weight, head_weight):
    batch_count, seq_len, bin_width = bases.shape
    channels = stem_weight.shape[1]
    inner_width = proj_weight.shape[1]
    letters = jnp.arange(4, dtype=jnp.int32)
    onehot = (bases[..., None] == letters).astype(jnp.bfloat16).reshape(batch_count * seq_len, bin_width * 4)
    state = jnp.dot(onehot, stem_weight, preferred_element_type=jnp.float32).astype(jnp.bfloat16)
    state = state.reshape(batch_count, seq_len, channels)
    saved_list = []
    for layer_position in range(N_SECTION):
        dilation_rate = DILATION_START * 2 ** layer_position
        kernel = conv_weight[layer_position]
        hidden = gelu_value(state.astype(jnp.float32)).astype(jnp.bfloat16)
        behind, forward = shifted(hidden, dilation_rate)
        inner_sum = jnp.dot(flatten(behind), kernel[0], preferred_element_type=jnp.float32)
        inner_sum = inner_sum + jnp.dot(flatten(hidden), kernel[1], preferred_element_type=jnp.float32)
        inner_sum = inner_sum + jnp.dot(flatten(forward), kernel[2], preferred_element_type=jnp.float32)
        active = gelu_value(inner_sum).astype(jnp.bfloat16)
        saved_list.append((state, hidden, behind, forward, inner_sum))
        update = jnp.dot(active, proj_weight[layer_position], preferred_element_type=jnp.float32)
        state = (flatten(state).astype(jnp.float32) + update).astype(jnp.bfloat16).reshape(batch_count, seq_len, channels)
    lifted = gelu_value(state.astype(jnp.float32)).astype(jnp.bfloat16)
    factor = 1.0 / math.sqrt(batch_count * seq_len)

    def head_step(running, item_pair):
        lifted_one, target_one = item_pair
        logits = jnp.dot(lifted_one, head_weight, preferred_element_type=jnp.float32)
        slope = ((jnp.exp(logits) - target_one.astype(jnp.float32)) * factor).astype(jnp.bfloat16)
        return (running + contract_rows(lifted_one, slope), times_transposed(slope, head_weight))
    head_grad, lift_grad = lax.scan(head_step, jnp.zeros((channels, head_weight.shape[1]), jnp.float32), (lifted, targets))
    cotangent = (lift_grad * gelu_slope(state.astype(jnp.float32))).astype(jnp.bfloat16)
    conv_list = []
    proj_list = []
    for layer_position in reversed(range(N_SECTION)):
        dilation_rate = DILATION_START * 2 ** layer_position
        kernel = conv_weight[layer_position]
        start_state, hidden, behind, forward, inner_sum = saved_list[layer_position]
        active = gelu_value(inner_sum).astype(jnp.bfloat16)
        proj_list.append(contract_rows(active, cotangent))
        active_grad = times_transposed(flatten(cotangent), proj_weight[layer_position])
        inner_grad = (active_grad * gelu_slope(inner_sum)).astype(jnp.bfloat16)
        inner_grad = inner_grad.reshape(batch_count, seq_len, inner_width)
        conv_list.append(jnp.stack([contract_rows(behind, inner_grad), contract_rows(hidden, inner_grad), contract_rows(forward, inner_grad)]))
        grad_behind, grad_forward = shifted(inner_grad, dilation_rate)
        hidden_grad = times_transposed(flatten(inner_grad), kernel[1])
        hidden_grad = hidden_grad + times_transposed(flatten(grad_forward), kernel[0])
        hidden_grad = hidden_grad + times_transposed(flatten(grad_behind), kernel[2])
        merged = flatten(cotangent).astype(jnp.float32) + hidden_grad * gelu_slope(flatten(start_state).astype(jnp.float32))
        cotangent = merged.astype(jnp.bfloat16).reshape(batch_count, seq_len, channels)
    conv_grad = jnp.stack(conv_list[::-1])
    proj_grad = jnp.stack(proj_list[::-1])
    return (conv_grad, proj_grad, head_grad)
```

```python
import math

import jax
import jax.numpy as jnp
from jax import lax
from jax.experimental import pallas as pl
from jax.experimental.pallas import tpu as pltpu
from jax.sharding import PartitionSpec as P

SQRT_TWO_OVER_PI = 0.7978845608028654
CUBIC_TERM = 0.044715


def gelu_value(inputs):
    return (
        0.5
        * inputs
        * (1.0 + jnp.tanh(SQRT_TWO_OVER_PI * (inputs + CUBIC_TERM * inputs * inputs * inputs)))
    )


def gelu_slope(inputs):
    tangent = jnp.tanh(SQRT_TWO_OVER_PI * (inputs + CUBIC_TERM * inputs * inputs * inputs))
    return 0.5 * (1.0 + tangent) + 0.5 * inputs * (1.0 - tangent * tangent) * SQRT_TWO_OVER_PI * (
        1.0 + 3.0 * CUBIC_TERM * inputs * inputs
    )


def contract_rows(left_side, right_side):
    return lax.dot_general(
        left_side, right_side, (((0,), (0,)), ((), ())), preferred_element_type=jnp.float32
    )


def times_transposed(left_side, right_side):
    return lax.dot_general(
        left_side, right_side, (((1,), (1,)), ((), ())), preferred_element_type=jnp.float32
    )


def shift_rows(value, by):
    if abs(by) >= value.shape[0]:
        return jnp.zeros_like(value)
    pad = jnp.zeros((abs(by),) + value.shape[1:], value.dtype)
    if by > 0:
        return jnp.concatenate([pad, value[:-by]], 0)
    return jnp.concatenate([value[-by:], pad], 0)


MESH = pl.DeviceIdType.MESH
ANY = pl.BlockSpec(memory_space=pl.ANY)


def greet(peers):
    barrier = pltpu.get_barrier_semaphore()
    for peer in peers:
        pl.semaphore_signal(barrier, inc=1, device_id=peer, device_id_type=MESH)
    pl.semaphore_wait(barrier, len(peers))


def remote(src, dst, send, recv, peer):
    return pltpu.make_async_remote_copy(
        src_ref=src, dst_ref=dst, send_sem=send, recv_sem=recv, device_id=peer, device_id_type=MESH
    )


def both_gelu(inputs):
    square = inputs * inputs
    tangent = jnp.tanh(
        inputs * (SQRT_TWO_OVER_PI + (SQRT_TWO_OVER_PI * CUBIC_TERM) * square)
    )
    gate = 0.5 + 0.5 * tangent
    value = inputs * gate
    inside = 2.0 * SQRT_TWO_OVER_PI + (6.0 * SQRT_TWO_OVER_PI * CUBIC_TERM) * square
    return value, gate + value * (1.0 - gate) * inside


def tile_of(rows):
    for size in (512, 384, 256, 192, 128, 96, 64, 48, 32, 16):
        if rows % size == 0:
            return size
    return rows


def forward_tower(bases, stem, taps, proj, sections, unit):
    seqs, half, width = bases.shape
    length = seqs * half
    channels = stem.shape[1]
    inner = proj.shape[0]
    rows = taps.shape[0] + inner
    part = rows // 2
    tile = tile_of(half)
    steps = half // tile
    shifts = [unit * 2**k for k in range(sections)]

    def kernel(*refs):
        bases_ref, stem_ref, taps_ref, proj_ref = refs[:4]
        refs = refs[4:]
        top_ref, weights_ref = refs[:2]
        hidden_out, slope_out = refs[2 : 2 + sections], refs[2 + sections : 1 + 2 * sections]
        refs = refs[1 + 2 * sections :]
        active_out, bend_out = refs[:sections], refs[sections : 2 * sections]
        refs = refs[2 * sections :]
        full, held, turned, state = refs[:4]
        refs = refs[4:]
        hidden, slope = refs[:sections], refs[sections : 2 * sections - 1]
        refs = refs[2 * sections - 1 :]
        active, bend = refs[:sections], refs[sections : 2 * sections]
        refs = refs[2 * sections :]
        bsend, brecv, send, recv, send2, recv2, tsend, trecv, own_sem, out_sem = refs

        s, c = lax.axis_index("section"), lax.axis_index("seq")
        partner = {"section": s, "seq": 1 - c}
        peers = [{"section": lax.rem(s + k, sections), "seq": c} for k in range(1, sections)]
        loads = [
            pltpu.make_async_copy(bases_ref.at[c], full.at[c], own_sem.at[0]),
            pltpu.make_async_copy(
                taps_ref, held.at[s, pl.ds(0, taps.shape[0])], own_sem.at[1]
            ),
            pltpu.make_async_copy(
                proj_ref, held.at[s, pl.ds(taps.shape[0], inner)], own_sem.at[2]
            ),
        ]
        for copy in loads:
            copy.start()
        greet(peers + [partner])
        across = remote(bases_ref.at[1 - c], full.at[c], bsend, brecv, partner)
        across.start()
        loads[1].wait()
        loads[2].wait()
        mine = held.at[s, pl.ds(pl.multiple_of(c * part, 16), part)]
        first = []
        for k, peer in enumerate(peers):
            first.append(remote(mine, mine, send.at[k], recv.at[k], peer))
            first[-1].start()
        for k in range(sections):
            edge = jnp.zeros((shifts[k], channels), jnp.bfloat16)
            hidden[k][pl.ds(0, shifts[k]), :] = edge
            hidden[k][pl.ds(shifts[k] + length, shifts[k]), :] = edge

        def begin(number):
            def step(i, carry):
                at = i * tile
                codes = full[number, pl.ds(pl.multiple_of(at, 16), tile), :]
                onehot = jnp.concatenate(
                    [(codes == k).astype(jnp.bfloat16) for k in range(4)], 1
                )
                start = jnp.dot(onehot, stem_ref[...], preferred_element_type=jnp.float32)
                start = start.astype(jnp.bfloat16)
                place = pl.multiple_of(number * half + at, 16)
                state[pl.ds(place, tile), :] = start
                value = gelu_value(start.astype(jnp.float32)).astype(jnp.bfloat16)
                hidden[0][pl.ds(pl.multiple_of(shifts[0] + place, 16), tile), :] = value
                return carry

            lax.fori_loop(0, steps, step, 0)

        loads[0].wait()
        begin(c)
        across.wait_recv()
        begin(1 - c)

        second = []
        for k in range(sections - 1):
            first[k].wait_recv()
            source = lax.rem(s + sections - 1 - k, sections)
            piece = held.at[source, pl.ds(pl.multiple_of(c * part, 16), part)]
            second.append(remote(piece, piece, send2.at[k], recv2.at[k], partner))
            second[-1].start()
        for copy in second:
            copy.wait_recv()

        outs = []

        def keep(src, dst):
            outs.append(pltpu.make_async_copy(src, dst, out_sem.at[len(outs)]))
            outs[-1].start()

        keep(held, weights_ref)
        keep(hidden[0].at[pl.ds(shifts[0], length)], hidden_out[0])

        for k in range(sections):
            by = shifts[k]
            for j in range(3):
                tap = held[k, pl.ds(j * inner, inner), :]
                turned[pl.ds(j * channels, channels), :] = tap.T

            def step_at(place, k=k, by=by):
                wide = jnp.concatenate(
                    [
                        hidden[k][pl.ds(pl.multiple_of(place + j * by, 16), tile), :]
                        for j in range(3)
                    ],
                    1,
                )
                total = jnp.dot(wide, turned[...], preferred_element_type=jnp.float32)
                value, bent = both_gelu(total)
                value = value.astype(jnp.bfloat16)
                active[k][pl.ds(place, tile), :] = value
                bend[k][pl.ds(place, tile), :] = bent.astype(jnp.bfloat16)
                update = jnp.dot(
                    value,
                    held[k, pl.ds(3 * inner, inner), :],
                    preferred_element_type=jnp.float32,
                )
                return (state[pl.ds(place, tile), :].astype(jnp.float32) + update).astype(
                    jnp.bfloat16
                )

            if k < sections - 1:

                def step(i, carry, k=k):
                    place = pl.multiple_of(i * tile, 16)
                    new = step_at(place)
                    state[pl.ds(place, tile), :] = new
                    value, bent = both_gelu(new.astype(jnp.float32))
                    ahead = pl.multiple_of(shifts[k + 1] + place, 16)
                    hidden[k + 1][pl.ds(ahead, tile), :] = value.astype(jnp.bfloat16)
                    slope[k][pl.ds(place, tile), :] = bent.astype(jnp.bfloat16)
                    return carry

                lax.fori_loop(0, length // tile, step, 0)
                keep(hidden[k + 1].at[pl.ds(shifts[k + 1], length)], hidden_out[k + 1])
                keep(slope[k], slope_out[k])
            else:

                def away(i, carry):
                    place = pl.multiple_of((1 - c) * half + i * tile, 16)
                    state[pl.ds(place, tile), :] = step_at(place)
                    return carry

                lax.fori_loop(0, steps, away, 0)
                theirs = state.at[pl.ds(pl.multiple_of((1 - c) * half, 16), half)]
                last = remote(theirs, top_ref.at[c], tsend, trecv, partner)
                last.start()

                def here(i, carry):
                    at = pl.multiple_of(i * tile, 16)
                    place = pl.multiple_of(c * half + at, 16)
                    top_ref[c, pl.ds(at, tile), :] = step_at(place)
                    return carry

                lax.fori_loop(0, steps, here, 0)
            keep(active[k], active_out[k])
            keep(bend[k], bend_out[k])
        for copy in outs:
            copy.wait()
        last.wait()
        across.wait_send()
        for copy in first + second:
            copy.wait_send()

    bf16 = jnp.bfloat16
    long = jax.ShapeDtypeStruct((length, channels), bf16)
    thin = jax.ShapeDtypeStruct((length, inner), bf16)
    dma = pltpu.SemaphoreType.DMA
    copies = 4 * sections
    out = pl.pallas_call(
        kernel,
        out_shape=[
            jax.ShapeDtypeStruct((seqs, half, channels), bf16),
            jax.ShapeDtypeStruct((sections, rows, channels), bf16),
        ]
        + [long] * (2 * sections - 1)
        + [thin] * (2 * sections),
        in_specs=[ANY, pl.BlockSpec(memory_space=pltpu.VMEM), ANY, ANY],
        out_specs=[pl.BlockSpec(memory_space=pltpu.VMEM)] + [ANY] * (4 * sections),
        scratch_shapes=[
            pltpu.VMEM((seqs, half, width), jnp.int32),
            pltpu.VMEM((sections, rows, channels), bf16),
            pltpu.VMEM((3 * channels, inner), bf16),
            pltpu.VMEM((length, channels), bf16),
        ]
        + [pltpu.VMEM((length + 2 * by, channels), bf16) for by in shifts]
        + [pltpu.VMEM((length, channels), bf16)] * (sections - 1)
        + [pltpu.VMEM((length, inner), bf16)] * (2 * sections)
        + [dma, dma]
        + [dma((sections - 1,))] * 4
        + [dma, dma, dma((3,)), dma((copies,))],
        compiler_params=pltpu.CompilerParams(
            collective_id=0, has_side_effects=True, vmem_limit_bytes=54 * 2**20
        ),
        name="forward_tower",
    )(bases, stem, taps, proj)
    top, weights = out[:2]
    hidden, slope = out[2 : 2 + sections], out[2 + sections : 1 + 2 * sections]
    active = out[1 + 2 * sections : 1 + 3 * sections]
    bend = out[1 + 3 * sections :]
    return top, weights, hidden, slope, active, bend


def head(top, targets, head_weight, factor):
    seqs, half, channels = top.shape
    tracks = head_weight.shape[1]
    tile = tile_of(half)
    steps = half // tile

    def kernel(
        top_ref, targets_ref, weight_ref, grad_ref, cot_ref, counts, stage, load, send, recv
    ):
        s, c = lax.axis_index("section"), lax.axis_index("seq")
        partner = {"section": s, "seq": 1 - c}
        loads = []
        for n, b in enumerate((1 - c, c)):
            for i in range(steps):
                loads.append(
                    pltpu.make_async_copy(
                        targets_ref.at[b, pl.ds(i * tile, tile)],
                        counts.at[n * steps + i],
                        load.at[n * steps + i],
                    )
                )
                loads[-1].start()
        greet([partner])
        grad_ref[...] = jnp.zeros_like(grad_ref)

        def run(b, n, store):
            def step(i, carry):
                at = pl.multiple_of(i * tile, 16)
                pltpu.make_async_copy(
                    targets_ref.at[b, pl.ds(at, tile)], counts.at[n + i], load.at[n + i]
                ).wait()
                value, bent = both_gelu(top_ref[b, pl.ds(at, tile), :].astype(jnp.float32))
                lifted = value.astype(jnp.bfloat16)
                logits = jnp.dot(lifted, weight_ref[...], preferred_element_type=jnp.float32)
                drop = jnp.exp(logits) - counts[n + i].astype(jnp.float32)
                drop = (drop * factor).astype(jnp.bfloat16)
                grad_ref[...] += contract_rows(lifted, drop)
                lift = times_transposed(drop, weight_ref[...])
                store(at, (lift * bent).astype(jnp.bfloat16))
                return carry

            lax.fori_loop(0, steps, step, 0)

        def away(at, value):
            stage[pl.ds(at, tile), :] = value

        def here(at, value):
            cot_ref[c, pl.ds(at, tile), :] = value

        run(1 - c, 0, away)
        copy = remote(stage, cot_ref.at[c], send, recv, partner)
        copy.start()
        run(c, steps, here)
        copy.wait()

    vmem = pl.BlockSpec(memory_space=pltpu.VMEM)
    dma = pltpu.SemaphoreType.DMA
    return pl.pallas_call(
        kernel,
        out_shape=[
            jax.ShapeDtypeStruct((channels, tracks), jnp.float32),
            jax.ShapeDtypeStruct(top.shape, jnp.bfloat16),
        ],
        in_specs=[vmem, ANY, vmem],
        out_specs=[vmem, vmem],
        scratch_shapes=[
            pltpu.VMEM((seqs * steps, tile, tracks), jnp.int32),
            pltpu.VMEM((half, channels), jnp.bfloat16),
            dma((seqs * steps,)),
            dma,
            dma,
        ],
        compiler_params=pltpu.CompilerParams(
            collective_id=1, has_side_effects=True, vmem_limit_bytes=48 * 2**20
        ),
        name="head",
    )(top, targets, head_weight)


def backward_tower(cot, weights, hidden, slope, active, bend, sections, unit):
    length, channels = hidden[0].shape
    inner = active[0].shape[1]
    tile = tile_of(length)
    most = unit * 2 ** (sections - 1)

    def kernel(*refs):
        cot_in, weights_ref = refs[:2]
        refs = refs[2:]
        hidden_in, slope_in = refs[:sections], refs[sections : 2 * sections - 1]
        refs = refs[2 * sections - 1 :]
        active_in, bend_in = refs[:sections], refs[sections : 2 * sections]
        out = refs[2 * sections]
        refs = refs[2 * sections + 1 :]
        hidden, slope = refs[:sections], refs[sections : 2 * sections - 1]
        refs = refs[2 * sections - 1 :]
        active, bend = refs[:sections], refs[sections : 2 * sections]
        held, grad, pull, sems = refs[2 * sections :]
        count = [0]

        def fetch(src, dst):
            copy = pltpu.make_async_copy(src, dst, sems.at[count[0]])
            count[0] += 1
            copy.start()
            return copy

        bring = {}
        for k in reversed(range(sections)):
            early = [fetch(weights_ref.at[k], held.at[k])]
            if k == sections - 1:
                early.append(fetch(cot_in, grad))
            early.append(fetch(bend_in[k], bend[k]))
            early.append(fetch(active_in[k], active[k]))
            late = [fetch(hidden_in[k], hidden[k])]
            if k:
                late.append(fetch(slope_in[k - 1], slope[k - 1]))
            bring[k] = (early, late)
        pull[pl.ds(0, most), :] = jnp.zeros((most, inner), jnp.bfloat16)
        pull[pl.ds(most + length, most), :] = jnp.zeros((most, inner), jnp.bfloat16)
        out[...] = jnp.zeros_like(out)

        for k in reversed(range(sections)):
            by = unit * 2**k
            for copy in bring[k][0]:
                copy.wait()

            def inward(i, carry, k=k):
                place = pl.multiple_of(i * tile, 16)
                here = grad[pl.ds(place, tile), :]
                back = times_transposed(here, held[k, pl.ds(3 * inner, inner), :])
                back = back * bend[k][pl.ds(place, tile), :].astype(jnp.float32)
                pull[pl.ds(pl.multiple_of(most + place, 16), tile), :] = back.astype(jnp.bfloat16)
                out[k, pl.ds(3 * inner, inner), :] += contract_rows(
                    active[k][pl.ds(place, tile), :], here
                )
                return carry

            lax.fori_loop(0, length // tile, inward, 0)
            for copy in bring[k][1]:
                copy.wait()

            def outward(i, carry, k=k, by=by):
                place = pl.multiple_of(i * tile, 16)
                there = hidden[k][pl.ds(place, tile), :]
                total = None
                for j in range(3):
                    piece = pull[pl.ds(pl.multiple_of(most + place + (1 - j) * by, 16), tile), :]
                    rows = pl.ds(j * inner, inner)
                    out[k, rows, :] += contract_rows(piece, there)
                    if k:
                        term = jnp.dot(
                            piece, held[k, rows, :], preferred_element_type=jnp.float32
                        )
                        total = term if total is None else total + term
                if k:
                    total = total * slope[k - 1][pl.ds(place, tile), :].astype(jnp.float32)
                    total = total + grad[pl.ds(place, tile), :].astype(jnp.float32)
                    grad[pl.ds(place, tile), :] = total.astype(jnp.bfloat16)
                return carry

            lax.fori_loop(0, length // tile, outward, 0)

    bf16 = jnp.bfloat16
    return pl.pallas_call(
        kernel,
        out_shape=jax.ShapeDtypeStruct(
            (sections, weights.shape[1], channels), jnp.float32
        ),
        in_specs=[ANY] * (2 + 4 * sections - 1),
        out_specs=pl.BlockSpec(memory_space=pltpu.VMEM),
        scratch_shapes=[pltpu.VMEM((length, channels), bf16)] * (2 * sections - 1)
        + [pltpu.VMEM((length, inner), bf16)] * (2 * sections)
        + [
            pltpu.VMEM(weights.shape, bf16),
            pltpu.VMEM((length, channels), bf16),
            pltpu.VMEM((length + 2 * most, inner), bf16),
            pltpu.SemaphoreType.DMA((5 * sections,)),
        ],
        compiler_params=pltpu.CompilerParams(vmem_limit_bytes=56 * 2**20),
        name="backward_tower",
    )(cot, weights, *hidden, *slope, *active, *bend)


def sum_gradients(value, sections, zones):
    rows, width = value.shape[1:]
    half = rows // 2
    piece = half // zones

    def kernel(
        src, out, met, wire, came, total, zcame, s0, r0, s1, r1, s2, r2, s3, r3, s4, r4
    ):
        s, c, d = (lax.axis_index(name) for name in ("section", "seq", "dp"))
        partner = {"section": s, "seq": 1 - c, "dp": d}
        order = [lax.rem(s + k, sections) for k in range(1, sections + 1)]
        across = [{"section": o, "seq": c, "dp": d} for o in order[:-1]]
        levels = [lax.rem(d + k, zones) for k in range(1, zones)]
        along = [{"section": s, "seq": c, "dp": z} for z in levels]
        greet([partner] + across + along)

        def strip(z):
            return pl.ds(pl.multiple_of(z * piece, 8), piece)

        def far(o):
            return src.at[o, pl.ds(pl.multiple_of((1 - c) * half, 8), half), :]

        def near(o):
            return src[o, pl.ds(pl.multiple_of(c * half, 8), half), :]

        pair = [remote(far(o), met.at[k], s0.at[k], r0.at[k], partner) for k, o in enumerate(order)]
        for copy in pair:
            copy.start()
        hops = []
        for k, peer in enumerate(across):
            pair[k].wait_recv()
            wire[k] = (met[k] + near(order[k])).astype(wire.dtype)
            hops.append(remote(wire.at[k], came.at[k], s1.at[k], r1.at[k], peer))
            hops[-1].start()
        pair[sections - 1].wait_recv()
        total[...] = met[sections - 1] + near(order[sections - 1])
        for k, copy in enumerate(hops):
            copy.wait_recv()
            total[...] += came[k].astype(jnp.float32)
        climbs = []
        for k, peer in enumerate(along):
            climbs.append(
                remote(total.at[strip(levels[k])], zcame.at[k], s2.at[k], r2.at[k], peer)
            )
            climbs[-1].start()
        done = total[strip(d), :]
        for k, copy in enumerate(climbs):
            copy.wait_recv()
            done = done + zcame[k]
        out[c, strip(d), :] = done

        mine = out.at[c, strip(d)]
        backs = [remote(mine, mine, s3.at[k], r3.at[k], peer) for k, peer in enumerate(along)]
        for copy in backs:
            copy.start()
        ends = [remote(mine, mine, s4.at[0], r4.at[0], partner)]
        ends[0].start()
        for k in range(zones - 1):
            backs[k].wait_recv()
            landed = out.at[c, strip(lax.rem(d + zones - 1 - k, zones))]
            ends.append(remote(landed, landed, s4.at[k + 1], r4.at[k + 1], partner))
            ends[-1].start()
        for copy in ends:
            copy.wait()
        for copy in pair + hops + climbs + backs:
            copy.wait_send()

    def dma(count):
        return [pltpu.SemaphoreType.DMA((count,))] * 2

    out = pl.pallas_call(
        kernel,
        out_shape=jax.ShapeDtypeStruct((2, half, width), jnp.float32),
        in_specs=[pl.BlockSpec(memory_space=pltpu.VMEM)],
        out_specs=pl.BlockSpec(memory_space=pltpu.VMEM),
        scratch_shapes=[
            pltpu.VMEM((sections, half, width), jnp.float32),
            pltpu.VMEM((sections - 1, half, width), jnp.bfloat16),
            pltpu.VMEM((sections - 1, half, width), jnp.bfloat16),
            pltpu.VMEM((half, width), jnp.float32),
            pltpu.VMEM((zones - 1, piece, width), jnp.float32),
        ]
        + dma(sections) + dma(sections - 1) + dma(zones - 1) + dma(zones - 1) + dma(zones),
        compiler_params=pltpu.CompilerParams(
            collective_id=3, has_side_effects=True, vmem_limit_bytes=40 * 2**20
        ),
    )(value)
    return out.reshape(rows, width)


def plain_body(bases, targets, stem_weight, conv_weight, proj_weight, head_weight):
    sections = lax.axis_size("section")
    seqs = lax.axis_size("seq")
    section_number = lax.axis_index("section")
    batches, row_count, bin_width = bases.shape
    channels = stem_weight.shape[1]
    length = row_count * seqs
    factor = 1.0 / math.sqrt(batches * lax.axis_size("dp") * length)
    unit = length // 2**sections
    local_q = row_count // unit
    blocks = length // unit
    columns = batches * unit // (seqs * sections)

    conv_all = lax.all_gather(conv_weight, "section", axis=0, tiled=True)
    proj_all = lax.all_gather(proj_weight, "section", axis=0, tiled=True)

    def to_chains(value):
        value = lax.all_to_all(value, "seq", split_axis=1, concat_axis=0, tiled=True)
        return value.reshape(blocks * columns, value.shape[-1])

    own = bases.reshape(batches, local_q, unit, bin_width).transpose(1, 0, 2, 3)
    own = own.reshape(local_q, seqs, sections, columns, bin_width)
    own = lax.dynamic_index_in_dim(own, section_number, 2, keepdims=False)
    picked = to_chains(own.astype(jnp.bfloat16))
    onehot = jnp.concatenate([(picked == c).astype(jnp.bfloat16) for c in range(4)], 1)
    stem = stem_weight.reshape(bin_width, 4, channels).transpose(1, 0, 2).reshape(-1, channels)
    state = jnp.dot(onehot, stem, preferred_element_type=jnp.float32).astype(jnp.bfloat16)

    saved = []
    for layer in range(sections):
        by = columns * 2**layer
        taps = conv_all[layer].reshape(-1, conv_all.shape[-1])
        hidden = gelu_value(state.astype(jnp.float32)).astype(jnp.bfloat16)
        wide = jnp.concatenate([shift_rows(hidden, by), hidden, shift_rows(hidden, -by)], 1)
        inner_sum = jnp.dot(wide, taps, preferred_element_type=jnp.float32)
        active = gelu_value(inner_sum).astype(jnp.bfloat16)
        update = jnp.dot(active, proj_all[layer], preferred_element_type=jnp.float32)
        saved.append((state, wide, inner_sum, active))
        state = (state.astype(jnp.float32) + update).astype(jnp.bfloat16)

    lifted = gelu_value(state.astype(jnp.float32)).astype(jnp.bfloat16)
    lifted = lifted.reshape(seqs, local_q, 1, columns, channels)
    lifted = lax.all_to_all(lifted, "seq", split_axis=0, concat_axis=2, tiled=True)
    lifted = lifted.reshape(local_q, seqs, 1, columns, channels)
    lifted = lax.all_gather(lifted, "section", axis=2, tiled=True)
    lifted = lifted.reshape(local_q, batches, unit, channels).transpose(1, 0, 2, 3)
    lifted = lifted.reshape(batches * row_count, channels)

    logits = jnp.dot(lifted, head_weight, preferred_element_type=jnp.float32)
    counts = targets.reshape(batches * row_count, targets.shape[2]).astype(jnp.float32)
    slope = ((jnp.exp(logits) - counts) * factor).astype(jnp.bfloat16)
    head_sum = lax.psum(contract_rows(lifted, slope), ("seq", "dp"))
    lift_part = times_transposed(slope, head_weight)

    lift_part = lift_part.reshape(batches, local_q, unit, channels).transpose(1, 0, 2, 3)
    lift_part = lift_part.reshape(local_q, seqs, sections, columns, channels)
    lift_part = lax.psum_scatter(lift_part, "section", scatter_dimension=2, tiled=True)
    lift_grad = to_chains(lift_part.reshape(local_q, seqs, columns, channels))


    grad = (lift_grad * gelu_slope(state.astype(jnp.float32))).astype(jnp.bfloat16)
    parts = []
    for layer in reversed(range(sections)):
        by = columns * 2**layer
        start_state, wide, inner_sum, active = saved[layer]
        kernel = conv_all[layer]
        proj_part = contract_rows(active, grad)
        active_grad = times_transposed(grad, proj_all[layer])
        inner_grad = (active_grad * gelu_slope(inner_sum)).astype(jnp.bfloat16)
        parts.append(jnp.concatenate([contract_rows(inner_grad, wide), proj_part], 1))
        wide_grad = jnp.concatenate(
            [shift_rows(inner_grad, -by), inner_grad, shift_rows(inner_grad, by)], 1
        )
        turned = kernel.transpose(0, 2, 1).reshape(-1, channels)
        hidden_grad = jnp.dot(wide_grad, turned, preferred_element_type=jnp.float32)
        grad = (
            grad.astype(jnp.float32) + hidden_grad * gelu_slope(start_state.astype(jnp.float32))
        ).astype(jnp.bfloat16)
    parts = jnp.stack(parts[::-1])
    total = lax.psum_scatter(parts, "section", scatter_dimension=0, tiled=True)
    total = lax.psum(total[0], ("seq", "dp"))
    taps_width = total.shape[1] - channels
    conv_sum = total[:, :taps_width].T.reshape(conv_weight.shape)
    return conv_sum, total[:, taps_width:][None], head_sum


def paired_body(bases, targets, stem_weight, conv_weight, proj_weight, head_weight):
    sections = lax.axis_size("section")
    zones = lax.axis_size("dp")
    batches, half, bin_width = bases.shape
    channels = stem_weight.shape[1]
    inner = proj_weight.shape[1]
    length = batches * half
    unit = length // 2**sections
    factor = 1.0 / math.sqrt(batches * zones * length)
    stem = stem_weight.reshape(bin_width, 4, channels).transpose(1, 0, 2).reshape(-1, channels)
    taps = conv_weight[0].transpose(0, 2, 1).reshape(3 * inner, channels)
    top, weights, hidden, slope, active, bend = forward_tower(
        bases, stem, taps, proj_weight[0], sections, unit
    )
    head_part, cot = head(top, targets, head_weight, factor)
    head_sum = lax.psum(head_part, ("seq", "dp"))
    cot = cot.reshape(length, channels)
    parts = backward_tower(cot, weights, hidden, slope, active, bend, sections, unit)
    total = sum_gradients(parts, sections, zones)
    conv_sum = total[: 3 * inner].reshape(3, inner, channels).transpose(0, 2, 1)
    return conv_sum[None], total[3 * inner :][None], head_sum


def body(bases, targets, stem_weight, conv_weight, proj_weight, head_weight):
    sections, zones = lax.axis_size("section"), lax.axis_size("dp")
    batches, half = bases.shape[:2]
    inner = proj_weight.shape[1]
    unit = batches * half // 2**sections
    paired = lax.axis_size("seq") == 2 and batches == 2 and zones > 1 and sections > 1
    paired = paired and unit % 16 == 0 and half % 16 == 0 and inner % 16 == 0
    paired = paired and (4 * inner) % (16 * zones) == 0
    run = paired_body if paired else plain_body
    return run(bases, targets, stem_weight, conv_weight, proj_weight, head_weight)


def solution(mesh):
    in_specs = (
        P("dp", "seq", None),
        P("dp", "seq", "section"),
        P(),
        P("section", None, None, None),
        P("section", None, None),
        P(None, "section"),
    )
    out_specs = (P("section", None, None, None), P("section", None, None), P(None, "section"))
    return jax.shard_map(body, mesh=mesh, in_specs=in_specs, out_specs=out_specs, check_vma=False)
```

```python
import math

import jax
import jax.numpy as jnp
from jax import lax
from jax.experimental import pallas as pl
from jax.experimental.pallas import tpu as pltpu
from jax.sharding import PartitionSpec as P

SQRT_TWO_OVER_PI = 0.7978845608028654
CUBIC_TERM = 0.044715


def gelu_value(inputs):
    return (
        0.5
        * inputs
        * (1.0 + jnp.tanh(SQRT_TWO_OVER_PI * (inputs + CUBIC_TERM * inputs * inputs * inputs)))
    )


def gelu_slope(inputs):
    tangent = jnp.tanh(SQRT_TWO_OVER_PI * (inputs + CUBIC_TERM * inputs * inputs * inputs))
    return 0.5 * (1.0 + tangent) + 0.5 * inputs * (1.0 - tangent * tangent) * SQRT_TWO_OVER_PI * (
        1.0 + 3.0 * CUBIC_TERM * inputs * inputs
    )


def contract_rows(left_side, right_side):
    return lax.dot_general(
        left_side, right_side, (((0,), (0,)), ((), ())), preferred_element_type=jnp.float32
    )


def times_transposed(left_side, right_side):
    return lax.dot_general(
        left_side, right_side, (((1,), (1,)), ((), ())), preferred_element_type=jnp.float32
    )


def shift_rows(value, by):
    if abs(by) >= value.shape[0]:
        return jnp.zeros_like(value)
    pad = jnp.zeros((abs(by),) + value.shape[1:], value.dtype)
    if by > 0:
        return jnp.concatenate([pad, value[:-by]], 0)
    return jnp.concatenate([value[-by:], pad], 0)


MESH = pl.DeviceIdType.MESH
ANY = pl.BlockSpec(memory_space=pl.ANY)


def greet(peers):
    barrier = pltpu.get_barrier_semaphore()
    for peer in peers:
        pl.semaphore_signal(barrier, inc=1, device_id=peer, device_id_type=MESH)
    pl.semaphore_wait(barrier, len(peers))


def remote(src, dst, send, recv, peer):
    return pltpu.make_async_remote_copy(
        src_ref=src, dst_ref=dst, send_sem=send, recv_sem=recv, device_id=peer, device_id_type=MESH
    )


def both_gelu(inputs):
    square = inputs * inputs
    tangent = jnp.tanh(
        inputs * (SQRT_TWO_OVER_PI + (SQRT_TWO_OVER_PI * CUBIC_TERM) * square)
    )
    gate = 0.5 + 0.5 * tangent
    value = inputs * gate
    inside = 2.0 * SQRT_TWO_OVER_PI + (6.0 * SQRT_TWO_OVER_PI * CUBIC_TERM) * square
    return value, gate + value * (1.0 - gate) * inside


def tile_of(rows):
    for size in (512, 384, 256, 192, 128, 96, 64, 48, 32, 16):
        if rows % size == 0:
            return size
    return rows


def forward_tower(bases, stem, taps, proj, sections, unit):
    seqs, half, width = bases.shape
    length = seqs * half
    channels = stem.shape[1]
    inner = proj.shape[0]
    rows = taps.shape[0] + inner
    part = rows // 2
    tile = tile_of(half)
    steps = half // tile
    shifts = [unit * 2**k for k in range(sections)]

    def kernel(*refs):
        bases_ref, stem_ref, taps_ref, proj_ref = refs[:4]
        refs = refs[4:]
        top_ref, weights_ref = refs[:2]
        hidden_out, slope_out = refs[2 : 2 + sections], refs[2 + sections : 1 + 2 * sections]
        refs = refs[1 + 2 * sections :]
        active_out, bend_out = refs[:sections], refs[sections : 2 * sections]
        refs = refs[2 * sections :]
        full, held, turned, state = refs[:4]
        refs = refs[4:]
        hidden, slope = refs[:sections], refs[sections : 2 * sections - 1]
        refs = refs[2 * sections - 1 :]
        active, bend = refs[:sections], refs[sections : 2 * sections]
        refs = refs[2 * sections :]
        bsend, brecv, send, recv, send2, recv2, tsend, trecv, own_sem, out_sem = refs

        s, c = lax.axis_index("section"), lax.axis_index("seq")
        partner = {"section": s, "seq": 1 - c}
        peers = [{"section": lax.rem(s + k, sections), "seq": c} for k in range(1, sections)]
        loads = [
            pltpu.make_async_copy(bases_ref.at[c], full.at[c], own_sem.at[0]),
            pltpu.make_async_copy(
                taps_ref, held.at[s, pl.ds(0, taps.shape[0])], own_sem.at[1]
            ),
            pltpu.make_async_copy(
                proj_ref, held.at[s, pl.ds(taps.shape[0], inner)], own_sem.at[2]
            ),
        ]
        for copy in loads:
            copy.start()
        greet(peers + [partner])
        across = remote(bases_ref.at[1 - c], full.at[c], bsend, brecv, partner)
        across.start()
        loads[1].wait()
        loads[2].wait()
        mine = held.at[s, pl.ds(pl.multiple_of(c * part, 16), part)]
        first = []
        for k, peer in enumerate(peers):
            first.append(remote(mine, mine, send.at[k], recv.at[k], peer))
            first[-1].start()
        for k in range(sections):
            edge = jnp.zeros((shifts[k], channels), jnp.bfloat16)
            hidden[k][pl.ds(0, shifts[k]), :] = edge
            hidden[k][pl.ds(shifts[k] + length, shifts[k]), :] = edge

        def begin(number):
            def step(i, carry):
                at = i * tile
                codes = full[number, pl.ds(pl.multiple_of(at, 16), tile), :]
                onehot = jnp.concatenate(
                    [(codes == k).astype(jnp.bfloat16) for k in range(4)], 1
                )
                start = jnp.dot(onehot, stem_ref[...], preferred_element_type=jnp.float32)
                start = start.astype(jnp.bfloat16)
                place = pl.multiple_of(number * half + at, 16)
                state[pl.ds(place, tile), :] = start
                value = gelu_value(start.astype(jnp.float32)).astype(jnp.bfloat16)
                hidden[0][pl.ds(pl.multiple_of(shifts[0] + place, 16), tile), :] = value
                return carry

            lax.fori_loop(0, steps, step, 0)

        loads[0].wait()
        begin(c)
        across.wait_recv()
        begin(1 - c)

        second = []
        for k in range(sections - 1):
            first[k].wait_recv()
            source = lax.rem(s + sections - 1 - k, sections)
            piece = held.at[source, pl.ds(pl.multiple_of(c * part, 16), part)]
            second.append(remote(piece, piece, send2.at[k], recv2.at[k], partner))
            second[-1].start()
        for copy in second:
            copy.wait_recv()

        outs = []

        def keep(src, dst):
            outs.append(pltpu.make_async_copy(src, dst, out_sem.at[len(outs)]))
            outs[-1].start()

        keep(held, weights_ref)
        keep(hidden[0].at[pl.ds(shifts[0], length)], hidden_out[0])

        for k in range(sections):
            by = shifts[k]
            for j in range(3):
                tap = held[k, pl.ds(j * inner, inner), :]
                turned[pl.ds(j * channels, channels), :] = tap.T

            def step_at(place, k=k, by=by):
                wide = jnp.concatenate(
                    [
                        hidden[k][pl.ds(pl.multiple_of(place + j * by, 16), tile), :]
                        for j in range(3)
                    ],
                    1,
                )
                total = jnp.dot(wide, turned[...], preferred_element_type=jnp.float32)
                value, bent = both_gelu(total)
                value = value.astype(jnp.bfloat16)
                active[k][pl.ds(place, tile), :] = value
                bend[k][pl.ds(place, tile), :] = bent.astype(jnp.bfloat16)
                update = jnp.dot(
                    value,
                    held[k, pl.ds(3 * inner, inner), :],
                    preferred_element_type=jnp.float32,
                )
                return (state[pl.ds(place, tile), :].astype(jnp.float32) + update).astype(
                    jnp.bfloat16
                )

            if k < sections - 1:

                def step(i, carry, k=k):
                    place = pl.multiple_of(i * tile, 16)
                    new = step_at(place)
                    state[pl.ds(place, tile), :] = new
                    value, bent = both_gelu(new.astype(jnp.float32))
                    ahead = pl.multiple_of(shifts[k + 1] + place, 16)
                    hidden[k + 1][pl.ds(ahead, tile), :] = value.astype(jnp.bfloat16)
                    slope[k][pl.ds(place, tile), :] = bent.astype(jnp.bfloat16)
                    return carry

                lax.fori_loop(0, length // tile, step, 0)
                keep(hidden[k + 1].at[pl.ds(shifts[k + 1], length)], hidden_out[k + 1])
                keep(slope[k], slope_out[k])
            else:

                def away(i, carry):
                    place = pl.multiple_of((1 - c) * half + i * tile, 16)
                    state[pl.ds(place, tile), :] = step_at(place)
                    return carry

                lax.fori_loop(0, steps, away, 0)
                theirs = state.at[pl.ds(pl.multiple_of((1 - c) * half, 16), half)]
                last = remote(theirs, top_ref.at[c], tsend, trecv, partner)
                last.start()

                def here(i, carry):
                    at = pl.multiple_of(i * tile, 16)
                    place = pl.multiple_of(c * half + at, 16)
                    top_ref[c, pl.ds(at, tile), :] = step_at(place)
                    return carry

                lax.fori_loop(0, steps, here, 0)
            keep(active[k], active_out[k])
            keep(bend[k], bend_out[k])
        for copy in outs:
            copy.wait()
        last.wait()
        across.wait_send()
        for copy in first + second:
            copy.wait_send()

    bf16 = jnp.bfloat16
    long = jax.ShapeDtypeStruct((length, channels), bf16)
    thin = jax.ShapeDtypeStruct((length, inner), bf16)
    dma = pltpu.SemaphoreType.DMA
    copies = 4 * sections
    out = pl.pallas_call(
        kernel,
        out_shape=[
            jax.ShapeDtypeStruct((seqs, half, channels), bf16),
            jax.ShapeDtypeStruct((sections, rows, channels), bf16),
        ]
        + [long] * (2 * sections - 1)
        + [thin] * (2 * sections),
        in_specs=[ANY, pl.BlockSpec(memory_space=pltpu.VMEM), ANY, ANY],
        out_specs=[pl.BlockSpec(memory_space=pltpu.VMEM)] + [ANY] * (4 * sections),
        scratch_shapes=[
            pltpu.VMEM((seqs, half, width), jnp.int32),
            pltpu.VMEM((sections, rows, channels), bf16),
            pltpu.VMEM((3 * channels, inner), bf16),
            pltpu.VMEM((length, channels), bf16),
        ]
        + [pltpu.VMEM((length + 2 * by, channels), bf16) for by in shifts]
        + [pltpu.VMEM((length, channels), bf16)] * (sections - 1)
        + [pltpu.VMEM((length, inner), bf16)] * (2 * sections)
        + [dma, dma]
        + [dma((sections - 1,))] * 4
        + [dma, dma, dma((3,)), dma((copies,))],
        compiler_params=pltpu.CompilerParams(
            collective_id=0, has_side_effects=True, vmem_limit_bytes=54 * 2**20
        ),
        name="forward_tower",
    )(bases, stem, taps, proj)
    top, weights = out[:2]
    hidden, slope = out[2 : 2 + sections], out[2 + sections : 1 + 2 * sections]
    active = out[1 + 2 * sections : 1 + 3 * sections]
    bend = out[1 + 3 * sections :]
    return top, weights, hidden, slope, active, bend


def head(top, targets, head_weight, factor):
    seqs, half, channels = top.shape
    tracks = head_weight.shape[1]
    tile = tile_of(half)
    steps = half // tile

    def kernel(
        top_ref, targets_ref, weight_ref, grad_ref, cot_ref, counts, stage, load, send, recv
    ):
        s, c = lax.axis_index("section"), lax.axis_index("seq")
        partner = {"section": s, "seq": 1 - c}
        loads = []
        for n, b in enumerate((1 - c, c)):
            for i in range(steps):
                loads.append(
                    pltpu.make_async_copy(
                        targets_ref.at[b, pl.ds(i * tile, tile)],
                        counts.at[n * steps + i],
                        load.at[n * steps + i],
                    )
                )
                loads[-1].start()
        greet([partner])
        grad_ref[...] = jnp.zeros_like(grad_ref)

        def run(b, n, store):
            def step(i, carry):
                at = pl.multiple_of(i * tile, 16)
                pltpu.make_async_copy(
                    targets_ref.at[b, pl.ds(at, tile)], counts.at[n + i], load.at[n + i]
                ).wait()
                value, bent = both_gelu(top_ref[b, pl.ds(at, tile), :].astype(jnp.float32))
                lifted = value.astype(jnp.bfloat16)
                logits = jnp.dot(lifted, weight_ref[...], preferred_element_type=jnp.float32)
                drop = jnp.exp(logits) - counts[n + i].astype(jnp.float32)
                drop = (drop * factor).astype(jnp.bfloat16)
                grad_ref[...] += contract_rows(lifted, drop)
                lift = times_transposed(drop, weight_ref[...])
                store(at, (lift * bent).astype(jnp.bfloat16))
                return carry

            lax.fori_loop(0, steps, step, 0)

        def away(at, value):
            stage[pl.ds(at, tile), :] = value

        def here(at, value):
            cot_ref[c, pl.ds(at, tile), :] = value

        run(1 - c, 0, away)
        copy = remote(stage, cot_ref.at[c], send, recv, partner)
        copy.start()
        run(c, steps, here)
        copy.wait()

    vmem = pl.BlockSpec(memory_space=pltpu.VMEM)
    dma = pltpu.SemaphoreType.DMA
    return pl.pallas_call(
        kernel,
        out_shape=[
            jax.ShapeDtypeStruct((channels, tracks), jnp.float32),
            jax.ShapeDtypeStruct(top.shape, jnp.bfloat16),
        ],
        in_specs=[vmem, ANY, vmem],
        out_specs=[vmem, vmem],
        scratch_shapes=[
            pltpu.VMEM((seqs * steps, tile, tracks), jnp.int32),
            pltpu.VMEM((half, channels), jnp.bfloat16),
            dma((seqs * steps,)),
            dma,
            dma,
        ],
        compiler_params=pltpu.CompilerParams(
            collective_id=1, has_side_effects=True, vmem_limit_bytes=48 * 2**20
        ),
        name="head",
    )(top, targets, head_weight)


def backward_tower(head_part, cot, weights, hidden, slope, active, bend, sections, zones, unit):
    length, channels = hidden[0].shape
    inner = active[0].shape[1]
    rows = weights.shape[1]
    part = rows // 2
    quarter = part // sections
    strip = quarter // zones
    tracks = head_part.shape[1]
    side = head_part.shape[0] // 2
    band = side // zones
    tile = length // 2
    most = unit * 2 ** (sections - 1)
    f32, bf16 = jnp.float32, jnp.bfloat16

    def kernel(*refs):
        head_ref, cot_ref, weights_ref = refs[:3]
        refs = refs[3:]
        hidden_in, slope_in = refs[:sections], refs[sections : 2 * sections - 1]
        refs = refs[2 * sections - 1 :]
        active_in, bend_in = refs[:sections], refs[sections : 2 * sections]
        refs = refs[2 * sections :]
        out, head_out = refs[:2]
        hidden, slope, active, bend = refs[2:4], refs[4:6], refs[6:8], refs[8:10]
        held, grad, pull, sums, load = refs[10:15]
        met, wire, came, total, zcame, final = refs[15:21]
        hmet, hsum, hcame = refs[21:24]
        sems = refs[24:]

        s, c, d = (lax.axis_index(name) for name in ("section", "seq", "dp"))
        partner = {"section": s, "seq": 1 - c, "dp": d}
        order = [lax.rem(s + k, sections) for k in range(1, sections)]
        across = [{"section": o, "seq": c, "dp": d} for o in order]
        levels = [lax.rem(d + k, zones) for k in range(1, zones)]
        along = [{"section": s, "seq": c, "dp": z} for z in levels]
        count = [0]

        def fetch(src, dst):
            copy = pltpu.make_async_copy(src, dst, load.at[count[0]])
            count[0] += 1
            copy.start()
            return copy

        bring = {}

        def prefetch(k):
            slot = k % 2
            early = [
                fetch(weights_ref.at[k], held.at[k]),
                fetch(bend_in[k], bend[slot]),
                fetch(active_in[k], active[slot]),
            ]
            late = [fetch(hidden_in[k], hidden[slot])]
            if k:
                late.append(fetch(slope_in[k - 1], slope[slot]))
            bring[k] = (early, late)

        prefetch(sections - 1)
        greet([partner] + across + along)

        sends = []

        def launch(src, dst, pair, index, peer):
            copy = remote(src, dst, sems[2 * pair].at[index], sems[2 * pair + 1].at[index], peer)
            copy.start()
            sends.append(copy)
            return copy

        def block(base, size, number):
            return pl.ds(pl.multiple_of(base + number * size, 8), size)

        flight = {}

        def swap(k):
            far = sums.at[k, block(0, part, 1 - c)]
            flight[k] = [launch(far, met.at[k], 0, k, partner)]

        def spread(k):
            flight[k][0].wait_recv()
            flight[k] = []

            def both(o):
                return met[k, block(0, quarter, o), :] + sums[k, block(c * part, quarter, o), :]

            for n, o in enumerate(order):
                wire[k, n] = both(o).astype(bf16)
                flight[k].append(
                    launch(wire.at[k, n], came.at[k, n], 1, k * (sections - 1) + n, across[n])
                )
            total[k] = both(s)

        def climb(k):
            for n, copy in enumerate(flight[k]):
                copy.wait_recv()
            value = total[k]
            for n in range(sections - 1):
                value = value + came[k, n].astype(f32)
            total[k] = value
            flight[k] = []
            for n, z in enumerate(levels):
                piece = total.at[k, block(0, strip, z)]
                flight[k].append(
                    launch(piece, zcame.at[k, n], 2, k * (zones - 1) + n, along[n])
                )

        def level(k):
            for copy in flight[k]:
                copy.wait_recv()
            value = total[k, block(0, strip, d), :]
            for n in range(zones - 1):
                value = value + zcame[k, n]
            final[k, block(0, strip, d), :] = value
            mine = final.at[k, block(0, strip, d)]
            flight[k] = [
                launch(mine, mine, 3, k * (zones - 1) + n, peer) for n, peer in enumerate(along)
            ]

        def home(k):
            owner = {"section": k, "seq": c, "dp": d}
            index = lax.rem(s + 2 * sections - k - 1, sections)
            place = out.at[block(c * part, quarter, s)]
            return remote(final.at[k], place, sems[8].at[k], sems[9].at[index], owner)

        def deliver(k):
            for copy in flight[k]:
                copy.wait_recv()

            @pl.when(s != k)
            def _():
                home(k).start()

            @pl.when(s == k)
            def _():
                out[block(c * part, quarter, s), :] = final[k]
                relay(0, s).start()

        def relay(n, source):
            piece = out.at[block(c * part, quarter, source)]
            return remote(piece, piece, sems[10].at[n], sems[11].at[n], partner)

        def hand(k):
            @pl.when(s == k)
            def _():
                for n, o in enumerate(order):
                    piece = out.at[block(c * part, quarter, o)]
                    remote(final.at[k], piece, sems[8].at[k], sems[9].at[n], across[n]).wait_recv()
                    relay(n + 1, o).start()

        def settle(k):
            @pl.when(s != k)
            def _():
                home(k).wait_send()

            @pl.when(s == k)
            def _():
                for n, o in enumerate([s] + order):
                    relay(n, o).wait()

        def head_swap():
            far = head_ref.at[block(0, side, 1 - c)]
            flight["h"] = [launch(far, hmet, 6, 0, partner)]

        def head_climb():
            flight["h"][0].wait_recv()
            hsum[...] = hmet[...] + head_ref[block(0, side, c), :]
            flight["h"] = [
                launch(hsum.at[block(0, band, z)], hcame.at[n], 7, n, along[n])
                for n, z in enumerate(levels)
            ]

        def head_level():
            for copy in flight["h"]:
                copy.wait_recv()
            value = hsum[block(0, band, d), :]
            for n in range(zones - 1):
                value = value + hcame[n]
            head_out[block(c * side, band, d), :] = value
            mine = head_out.at[block(c * side, band, d)]
            flight["h"] = [launch(mine, mine, 8, n, peer) for n, peer in enumerate(along)]
            flight["r"] = [launch(mine, mine, 9, 0, partner)]

        def head_hand():
            for n, copy in enumerate(flight["h"]):
                copy.wait_recv()
                source = lax.rem(d + zones - 1 - n, zones)
                piece = head_out.at[block(c * side, band, source)]
                flight["r"].append(launch(piece, piece, 9, n + 1, partner))

        head_swap()
        pull[pl.ds(0, most), :] = jnp.zeros((most, inner), bf16)
        pull[pl.ds(most + length, most), :] = jnp.zeros((most, inner), bf16)
        sums[...] = jnp.zeros_like(sums)

        top = sections - 1
        for k in reversed(range(sections)):
            by = unit * 2**k
            slot = k % 2
            above = cot_ref if k == top else grad
            if k:
                prefetch(k - 1)
            for copy in bring[k][0]:
                copy.wait()

            def inward(i, carry, k=k, slot=slot, above=above):
                place = pl.multiple_of(i * tile, 16)
                here = above[pl.ds(place, tile), :]
                back = times_transposed(here, held[k, pl.ds(3 * inner, inner), :])
                back = back * bend[slot][pl.ds(place, tile), :].astype(f32)
                pull[pl.ds(pl.multiple_of(most + place, 16), tile), :] = back.astype(bf16)
                sums[k, pl.ds(3 * inner, inner), :] += contract_rows(
                    active[slot][pl.ds(place, tile), :], here
                )
                return carry

            lax.fori_loop(0, length // tile, inward, 0)
            if k == top:
                head_climb()
            else:
                if k + 3 <= top:
                    hand(k + 3)
                if k + 2 <= top:
                    level(k + 2)
                spread(k + 1)
                if k == top - 2:
                    head_level()
            for copy in bring[k][1]:
                copy.wait()

            def outward(i, carry, k=k, by=by, slot=slot, above=above):
                place = pl.multiple_of(i * tile, 16)
                there = hidden[slot][pl.ds(place, tile), :]
                value = None
                for j in range(3):
                    piece = pull[pl.ds(pl.multiple_of(most + place + (1 - j) * by, 16), tile), :]
                    span = pl.ds(j * inner, inner)
                    sums[k, span, :] += contract_rows(piece, there)
                    if k:
                        term = jnp.dot(piece, held[k, span, :], preferred_element_type=f32)
                        value = term if value is None else value + term
                if k:
                    value = value * slope[slot][pl.ds(place, tile), :].astype(f32)
                    value = value + above[pl.ds(place, tile), :].astype(f32)
                    grad[pl.ds(place, tile), :] = value.astype(bf16)
                return carry

            lax.fori_loop(0, length // tile, outward, 0)
            swap(k)
            if k + 1 <= top:
                climb(k + 1)
            if k + 2 <= top:
                deliver(k + 2)

        spread(0)
        level(1)
        hand(2)
        climb(0)
        deliver(1)
        level(0)
        hand(1)
        deliver(0)
        head_hand()
        hand(0)
        for copy in flight["r"]:
            copy.wait_recv()
        for k in range(sections):
            settle(k)
        for copy in sends:
            copy.wait_send()

    dma = pltpu.SemaphoreType.DMA

    def pair(count):
        return [dma((count,))] * 2

    long, thin = pltpu.VMEM((length, channels), bf16), pltpu.VMEM((length, inner), bf16)
    vmem = pl.BlockSpec(memory_space=pltpu.VMEM)
    return pl.pallas_call(
        kernel,
        out_shape=[
            jax.ShapeDtypeStruct((rows, channels), f32),
            jax.ShapeDtypeStruct(head_part.shape, f32),
        ],
        in_specs=[vmem, vmem] + [ANY] * (4 * sections),
        out_specs=[vmem, vmem],
        scratch_shapes=[long] * 4
        + [thin] * 4
        + [
            pltpu.VMEM(weights.shape, bf16),
            long,
            pltpu.VMEM((length + 2 * most, inner), bf16),
            pltpu.VMEM((sections, rows, channels), f32),
            dma((5 * sections,)),
            pltpu.VMEM((sections, part, channels), f32),
            pltpu.VMEM((sections, sections - 1, quarter, channels), bf16),
            pltpu.VMEM((sections, sections - 1, quarter, channels), bf16),
            pltpu.VMEM((sections, quarter, channels), f32),
            pltpu.VMEM((sections, zones - 1, strip, channels), f32),
            pltpu.VMEM((sections, quarter, channels), f32),
            pltpu.VMEM((side, tracks), f32),
            pltpu.VMEM((side, tracks), f32),
            pltpu.VMEM((zones - 1, band, tracks), f32),
        ]
        + pair(sections)
        + pair(sections * (sections - 1))
        + pair(sections * (zones - 1))
        + pair(sections * (zones - 1))
        + [dma((sections,)), dma((sections,))]
        + pair(sections)
        + pair(1)
        + pair(zones - 1)
        + pair(zones - 1)
        + pair(zones),
        compiler_params=pltpu.CompilerParams(
            collective_id=2, has_side_effects=True, vmem_limit_bytes=56 * 2**20
        ),
        name="backward_tower",
    )(head_part, cot, weights, *hidden, *slope, *active, *bend)


def plain_body(bases, targets, stem_weight, conv_weight, proj_weight, head_weight):
    sections = lax.axis_size("section")
    seqs = lax.axis_size("seq")
    section_number = lax.axis_index("section")
    batches, row_count, bin_width = bases.shape
    channels = stem_weight.shape[1]
    length = row_count * seqs
    factor = 1.0 / math.sqrt(batches * lax.axis_size("dp") * length)
    unit = length // 2**sections
    local_q = row_count // unit
    blocks = length // unit
    columns = batches * unit // (seqs * sections)

    conv_all = lax.all_gather(conv_weight, "section", axis=0, tiled=True)
    proj_all = lax.all_gather(proj_weight, "section", axis=0, tiled=True)

    def to_chains(value):
        value = lax.all_to_all(value, "seq", split_axis=1, concat_axis=0, tiled=True)
        return value.reshape(blocks * columns, value.shape[-1])

    own = bases.reshape(batches, local_q, unit, bin_width).transpose(1, 0, 2, 3)
    own = own.reshape(local_q, seqs, sections, columns, bin_width)
    own = lax.dynamic_index_in_dim(own, section_number, 2, keepdims=False)
    picked = to_chains(own.astype(jnp.bfloat16))
    onehot = jnp.concatenate([(picked == c).astype(jnp.bfloat16) for c in range(4)], 1)
    stem = stem_weight.reshape(bin_width, 4, channels).transpose(1, 0, 2).reshape(-1, channels)
    state = jnp.dot(onehot, stem, preferred_element_type=jnp.float32).astype(jnp.bfloat16)

    saved = []
    for layer in range(sections):
        by = columns * 2**layer
        taps = conv_all[layer].reshape(-1, conv_all.shape[-1])
        hidden = gelu_value(state.astype(jnp.float32)).astype(jnp.bfloat16)
        wide = jnp.concatenate([shift_rows(hidden, by), hidden, shift_rows(hidden, -by)], 1)
        inner_sum = jnp.dot(wide, taps, preferred_element_type=jnp.float32)
        active = gelu_value(inner_sum).astype(jnp.bfloat16)
        update = jnp.dot(active, proj_all[layer], preferred_element_type=jnp.float32)
        saved.append((state, wide, inner_sum, active))
        state = (state.astype(jnp.float32) + update).astype(jnp.bfloat16)

    lifted = gelu_value(state.astype(jnp.float32)).astype(jnp.bfloat16)
    lifted = lifted.reshape(seqs, local_q, 1, columns, channels)
    lifted = lax.all_to_all(lifted, "seq", split_axis=0, concat_axis=2, tiled=True)
    lifted = lifted.reshape(local_q, seqs, 1, columns, channels)
    lifted = lax.all_gather(lifted, "section", axis=2, tiled=True)
    lifted = lifted.reshape(local_q, batches, unit, channels).transpose(1, 0, 2, 3)
    lifted = lifted.reshape(batches * row_count, channels)

    logits = jnp.dot(lifted, head_weight, preferred_element_type=jnp.float32)
    counts = targets.reshape(batches * row_count, targets.shape[2]).astype(jnp.float32)
    slope = ((jnp.exp(logits) - counts) * factor).astype(jnp.bfloat16)
    head_sum = lax.psum(contract_rows(lifted, slope), ("seq", "dp"))
    lift_part = times_transposed(slope, head_weight)

    lift_part = lift_part.reshape(batches, local_q, unit, channels).transpose(1, 0, 2, 3)
    lift_part = lift_part.reshape(local_q, seqs, sections, columns, channels)
    lift_part = lax.psum_scatter(lift_part, "section", scatter_dimension=2, tiled=True)
    lift_grad = to_chains(lift_part.reshape(local_q, seqs, columns, channels))


    grad = (lift_grad * gelu_slope(state.astype(jnp.float32))).astype(jnp.bfloat16)
    parts = []
    for layer in reversed(range(sections)):
        by = columns * 2**layer
        start_state, wide, inner_sum, active = saved[layer]
        kernel = conv_all[layer]
        proj_part = contract_rows(active, grad)
        active_grad = times_transposed(grad, proj_all[layer])
        inner_grad = (active_grad * gelu_slope(inner_sum)).astype(jnp.bfloat16)
        parts.append(jnp.concatenate([contract_rows(inner_grad, wide), proj_part], 1))
        wide_grad = jnp.concatenate(
            [shift_rows(inner_grad, -by), inner_grad, shift_rows(inner_grad, by)], 1
        )
        turned = kernel.transpose(0, 2, 1).reshape(-1, channels)
        hidden_grad = jnp.dot(wide_grad, turned, preferred_element_type=jnp.float32)
        grad = (
            grad.astype(jnp.float32) + hidden_grad * gelu_slope(start_state.astype(jnp.float32))
        ).astype(jnp.bfloat16)
    parts = jnp.stack(parts[::-1])
    total = lax.psum_scatter(parts, "section", scatter_dimension=0, tiled=True)
    total = lax.psum(total[0], ("seq", "dp"))
    taps_width = total.shape[1] - channels
    conv_sum = total[:, :taps_width].T.reshape(conv_weight.shape)
    return conv_sum, total[:, taps_width:][None], head_sum


def paired_body(bases, targets, stem_weight, conv_weight, proj_weight, head_weight):
    sections = lax.axis_size("section")
    zones = lax.axis_size("dp")
    batches, half, bin_width = bases.shape
    channels = stem_weight.shape[1]
    inner = proj_weight.shape[1]
    length = batches * half
    unit = length // 2**sections
    factor = 1.0 / math.sqrt(batches * zones * length)
    stem = stem_weight.reshape(bin_width, 4, channels).transpose(1, 0, 2).reshape(-1, channels)
    taps = conv_weight[0].transpose(0, 2, 1).reshape(3 * inner, channels)
    top, weights, hidden, slope, active, bend = forward_tower(
        bases, stem, taps, proj_weight[0], sections, unit
    )
    head_part, cot = head(top, targets, head_weight, factor)
    cot = cot.reshape(length, channels)
    total, head_sum = backward_tower(
        head_part, cot, weights, hidden, slope, active, bend, sections, zones, unit
    )
    conv_sum = total[: 3 * inner].reshape(3, inner, channels).transpose(0, 2, 1)
    return conv_sum[None], total[3 * inner :][None], head_sum


def body(bases, targets, stem_weight, conv_weight, proj_weight, head_weight):
    sections, zones = lax.axis_size("section"), lax.axis_size("dp")
    batches, half = bases.shape[:2]
    inner = proj_weight.shape[1]
    unit = batches * half // 2**sections
    paired = lax.axis_size("seq") == 2 and batches == 2 and zones > 1 and sections > 1
    paired = paired and unit % 16 == 0 and half % 16 == 0 and inner % 16 == 0
    paired = paired and (2 * inner) % (16 * sections) == 0
    paired = paired and (2 * inner) % (8 * sections * zones) == 0
    paired = paired and stem_weight.shape[1] % (16 * zones) == 0
    run = paired_body if paired else plain_body
    return run(bases, targets, stem_weight, conv_weight, proj_weight, head_weight)


def solution(mesh):
    in_specs = (
        P("dp", "seq", None),
        P("dp", "seq", "section"),
        P(),
        P("section", None, None, None),
        P("section", None, None),
        P(None, "section"),
    )
    out_specs = (P("section", None, None, None), P("section", None, None), P(None, "section"))
    return jax.shard_map(body, mesh=mesh, in_specs=in_specs, out_specs=out_specs, check_vma=False)
```

```python
import math

import jax
import jax.numpy as jnp
from jax import lax
from jax.experimental import pallas as pl
from jax.experimental.pallas import tpu as pltpu
from jax.sharding import PartitionSpec as P

SQRT_TWO_OVER_PI = 0.7978845608028654
CUBIC_TERM = 0.044715


def gelu_value(inputs):
    return (
        0.5
        * inputs
        * (1.0 + jnp.tanh(SQRT_TWO_OVER_PI * (inputs + CUBIC_TERM * inputs * inputs * inputs)))
    )


def gelu_slope(inputs):
    tangent = jnp.tanh(SQRT_TWO_OVER_PI * (inputs + CUBIC_TERM * inputs * inputs * inputs))
    return 0.5 * (1.0 + tangent) + 0.5 * inputs * (1.0 - tangent * tangent) * SQRT_TWO_OVER_PI * (
        1.0 + 3.0 * CUBIC_TERM * inputs * inputs
    )


def contract_rows(left_side, right_side):
    return lax.dot_general(
        left_side, right_side, (((0,), (0,)), ((), ())), preferred_element_type=jnp.float32
    )


def times_transposed(left_side, right_side):
    return lax.dot_general(
        left_side, right_side, (((1,), (1,)), ((), ())), preferred_element_type=jnp.float32
    )


def shift_rows(value, by):
    if abs(by) >= value.shape[0]:
        return jnp.zeros_like(value)
    pad = jnp.zeros((abs(by),) + value.shape[1:], value.dtype)
    if by > 0:
        return jnp.concatenate([pad, value[:-by]], 0)
    return jnp.concatenate([value[-by:], pad], 0)


MESH = pl.DeviceIdType.MESH
ANY = pl.BlockSpec(memory_space=pl.ANY)


def greet(peers):
    barrier = pltpu.get_barrier_semaphore()
    for peer in peers:
        pl.semaphore_signal(barrier, inc=1, device_id=peer, device_id_type=MESH)
    pl.semaphore_wait(barrier, len(peers))


def remote(src, dst, send, recv, peer):
    return pltpu.make_async_remote_copy(
        src_ref=src, dst_ref=dst, send_sem=send, recv_sem=recv, device_id=peer, device_id_type=MESH
    )


def both_gelu(inputs):
    square = inputs * inputs
    tangent = jnp.tanh(
        inputs * (SQRT_TWO_OVER_PI + (SQRT_TWO_OVER_PI * CUBIC_TERM) * square)
    )
    gate = 0.5 + 0.5 * tangent
    value = inputs * gate
    inside = 2.0 * SQRT_TWO_OVER_PI + (6.0 * SQRT_TWO_OVER_PI * CUBIC_TERM) * square
    return value, gate + value * (1.0 - gate) * inside


def tile_of(rows):
    for size in (512, 384, 256, 192, 128, 96, 64, 48, 32, 16):
        if rows % size == 0:
            return size
    return rows


def forward_tower(bases, stem, taps, proj, sections, unit):
    seqs, half, width = bases.shape
    length = seqs * half
    channels = stem.shape[1]
    inner = proj.shape[0]
    rows = taps.shape[0] + inner
    part = rows // 2
    tile = tile_of(half)
    steps = half // tile
    shifts = [unit * 2**k for k in range(sections)]

    def kernel(*refs):
        bases_ref, stem_ref, taps_ref, proj_ref = refs[:4]
        refs = refs[4:]
        top_ref, weights_ref = refs[:2]
        hidden_out, slope_out = refs[2 : 2 + sections], refs[2 + sections : 1 + 2 * sections]
        refs = refs[1 + 2 * sections :]
        active_out, bend_out = refs[:sections], refs[sections : 2 * sections]
        refs = refs[2 * sections :]
        full, held, turned, state = refs[:4]
        refs = refs[4:]
        hidden, slope = refs[:sections], refs[sections : 2 * sections - 1]
        refs = refs[2 * sections - 1 :]
        active, bend = refs[:sections], refs[sections : 2 * sections]
        refs = refs[2 * sections :]
        bsend, brecv, send, recv, send2, recv2, tsend, trecv, own_sem, out_sem = refs

        s, c = lax.axis_index("section"), lax.axis_index("seq")
        partner = {"section": s, "seq": 1 - c}
        peers = [{"section": lax.rem(s + k, sections), "seq": c} for k in range(1, sections)]
        loads = [
            pltpu.make_async_copy(bases_ref.at[c], full.at[c], own_sem.at[0]),
            pltpu.make_async_copy(
                taps_ref, held.at[s, pl.ds(0, taps.shape[0])], own_sem.at[1]
            ),
            pltpu.make_async_copy(
                proj_ref, held.at[s, pl.ds(taps.shape[0], inner)], own_sem.at[2]
            ),
        ]
        for copy in loads:
            copy.start()
        greet(peers + [partner])
        across = remote(bases_ref.at[1 - c], full.at[c], bsend, brecv, partner)
        across.start()
        loads[1].wait()
        loads[2].wait()
        mine = held.at[s, pl.ds(pl.multiple_of(c * part, 16), part)]
        first = []
        for k, peer in enumerate(peers):
            first.append(remote(mine, mine, send.at[k], recv.at[k], peer))
            first[-1].start()
        for k in range(sections):
            edge = jnp.zeros((shifts[k], channels), jnp.bfloat16)
            hidden[k][pl.ds(0, shifts[k]), :] = edge
            hidden[k][pl.ds(shifts[k] + length, shifts[k]), :] = edge

        def begin(number):
            def step(i, carry):
                at = i * tile
                codes = full[number, pl.ds(pl.multiple_of(at, 16), tile), :]
                onehot = jnp.concatenate(
                    [(codes == k).astype(jnp.bfloat16) for k in range(4)], 1
                )
                start = jnp.dot(onehot, stem_ref[...], preferred_element_type=jnp.float32)
                start = start.astype(jnp.bfloat16)
                place = pl.multiple_of(number * half + at, 16)
                state[pl.ds(place, tile), :] = start
                value = gelu_value(start.astype(jnp.float32)).astype(jnp.bfloat16)
                hidden[0][pl.ds(pl.multiple_of(shifts[0] + place, 16), tile), :] = value
                return carry

            lax.fori_loop(0, steps, step, 0)

        loads[0].wait()
        begin(c)
        across.wait_recv()
        begin(1 - c)

        second = []
        for k in range(sections - 1):
            first[k].wait_recv()
            source = lax.rem(s + sections - 1 - k, sections)
            piece = held.at[source, pl.ds(pl.multiple_of(c * part, 16), part)]
            second.append(remote(piece, piece, send2.at[k], recv2.at[k], partner))
            second[-1].start()
        for copy in second:
            copy.wait_recv()

        outs = []

        def keep(src, dst):
            outs.append(pltpu.make_async_copy(src, dst, out_sem.at[len(outs)]))
            outs[-1].start()

        keep(held, weights_ref)
        keep(hidden[0].at[pl.ds(shifts[0], length)], hidden_out[0])

        for k in range(sections):
            by = shifts[k]
            for j in range(3):
                tap = held[k, pl.ds(j * inner, inner), :]
                turned[pl.ds(j * channels, channels), :] = tap.T

            def step_at(place, k=k, by=by):
                wide = jnp.concatenate(
                    [
                        hidden[k][pl.ds(pl.multiple_of(place + j * by, 16), tile), :]
                        for j in range(3)
                    ],
                    1,
                )
                total = jnp.dot(wide, turned[...], preferred_element_type=jnp.float32)
                value, bent = both_gelu(total)
                value = value.astype(jnp.bfloat16)
                active[k][pl.ds(place, tile), :] = value
                bend[k][pl.ds(place, tile), :] = bent.astype(jnp.bfloat16)
                update = jnp.dot(
                    value,
                    held[k, pl.ds(3 * inner, inner), :],
                    preferred_element_type=jnp.float32,
                )
                return (state[pl.ds(place, tile), :].astype(jnp.float32) + update).astype(
                    jnp.bfloat16
                )

            if k < sections - 1:

                def step(i, carry, k=k):
                    place = pl.multiple_of(i * tile, 16)
                    new = step_at(place)
                    state[pl.ds(place, tile), :] = new
                    value, bent = both_gelu(new.astype(jnp.float32))
                    ahead = pl.multiple_of(shifts[k + 1] + place, 16)
                    hidden[k + 1][pl.ds(ahead, tile), :] = value.astype(jnp.bfloat16)
                    slope[k][pl.ds(place, tile), :] = bent.astype(jnp.bfloat16)
                    return carry

                lax.fori_loop(0, length // tile, step, 0)
                keep(hidden[k + 1].at[pl.ds(shifts[k + 1], length)], hidden_out[k + 1])
                keep(slope[k], slope_out[k])
            else:

                def away(i, carry):
                    place = pl.multiple_of((1 - c) * half + i * tile, 16)
                    state[pl.ds(place, tile), :] = step_at(place)
                    return carry

                lax.fori_loop(0, steps, away, 0)
                theirs = state.at[pl.ds(pl.multiple_of((1 - c) * half, 16), half)]
                last = remote(theirs, top_ref.at[c], tsend, trecv, partner)
                last.start()

                def here(i, carry):
                    at = pl.multiple_of(i * tile, 16)
                    place = pl.multiple_of(c * half + at, 16)
                    top_ref[c, pl.ds(at, tile), :] = step_at(place)
                    return carry

                lax.fori_loop(0, steps, here, 0)
            keep(active[k], active_out[k])
            keep(bend[k], bend_out[k])
        for copy in outs:
            copy.wait()
        last.wait()
        across.wait_send()
        for copy in first + second:
            copy.wait_send()

    bf16 = jnp.bfloat16
    long = jax.ShapeDtypeStruct((length, channels), bf16)
    thin = jax.ShapeDtypeStruct((length, inner), bf16)
    dma = pltpu.SemaphoreType.DMA
    copies = 4 * sections
    out = pl.pallas_call(
        kernel,
        out_shape=[
            jax.ShapeDtypeStruct((seqs, half, channels), bf16),
            jax.ShapeDtypeStruct((sections, rows, channels), bf16),
        ]
        + [long] * (2 * sections - 1)
        + [thin] * (2 * sections),
        in_specs=[ANY, pl.BlockSpec(memory_space=pltpu.VMEM), ANY, ANY],
        out_specs=[pl.BlockSpec(memory_space=pltpu.VMEM)] + [ANY] * (4 * sections),
        scratch_shapes=[
            pltpu.VMEM((seqs, half, width), jnp.int32),
            pltpu.VMEM((sections, rows, channels), bf16),
            pltpu.VMEM((3 * channels, inner), bf16),
            pltpu.VMEM((length, channels), bf16),
        ]
        + [pltpu.VMEM((length + 2 * by, channels), bf16) for by in shifts]
        + [pltpu.VMEM((length, channels), bf16)] * (sections - 1)
        + [pltpu.VMEM((length, inner), bf16)] * (2 * sections)
        + [dma, dma]
        + [dma((sections - 1,))] * 4
        + [dma, dma, dma((3,)), dma((copies,))],
        compiler_params=pltpu.CompilerParams(
            collective_id=0, has_side_effects=True, vmem_limit_bytes=54 * 2**20
        ),
        name="forward_tower",
    )(bases, stem, taps, proj)
    top, weights = out[:2]
    hidden, slope = out[2 : 2 + sections], out[2 + sections : 1 + 2 * sections]
    active = out[1 + 2 * sections : 1 + 3 * sections]
    bend = out[1 + 3 * sections :]
    return top, weights, hidden, slope, active, bend


def head(top, targets, head_weight, factor):
    seqs, half, channels = top.shape
    tracks = head_weight.shape[1]
    tile = tile_of(half)
    steps = half // tile

    def kernel(
        top_ref, targets_ref, weight_ref, grad_ref, cot_ref, counts, stage, load, send, recv
    ):
        s, c = lax.axis_index("section"), lax.axis_index("seq")
        partner = {"section": s, "seq": 1 - c}
        loads = []
        for n, b in enumerate((1 - c, c)):
            for i in range(steps):
                loads.append(
                    pltpu.make_async_copy(
                        targets_ref.at[b, pl.ds(i * tile, tile)],
                        counts.at[n * steps + i],
                        load.at[n * steps + i],
                    )
                )
                loads[-1].start()
        greet([partner])
        grad_ref[...] = jnp.zeros_like(grad_ref)

        def run(b, n, store):
            def step(i, carry):
                at = pl.multiple_of(i * tile, 16)
                pltpu.make_async_copy(
                    targets_ref.at[b, pl.ds(at, tile)], counts.at[n + i], load.at[n + i]
                ).wait()
                value, bent = both_gelu(top_ref[b, pl.ds(at, tile), :].astype(jnp.float32))
                lifted = value.astype(jnp.bfloat16)
                logits = jnp.dot(lifted, weight_ref[...], preferred_element_type=jnp.float32)
                drop = jnp.exp(logits) - counts[n + i].astype(jnp.float32)
                drop = (drop * factor).astype(jnp.bfloat16)
                grad_ref[...] += contract_rows(lifted, drop)
                lift = times_transposed(drop, weight_ref[...])
                store(at, (lift * bent).astype(jnp.bfloat16))
                return carry

            lax.fori_loop(0, steps, step, 0)

        def away(at, value):
            stage[pl.ds(at, tile), :] = value

        def here(at, value):
            cot_ref[c, pl.ds(at, tile), :] = value

        run(1 - c, 0, away)
        copy = remote(stage, cot_ref.at[c], send, recv, partner)
        copy.start()
        run(c, steps, here)
        copy.wait()

    vmem = pl.BlockSpec(memory_space=pltpu.VMEM)
    dma = pltpu.SemaphoreType.DMA
    return pl.pallas_call(
        kernel,
        out_shape=[
            jax.ShapeDtypeStruct((channels, tracks), jnp.float32),
            jax.ShapeDtypeStruct(top.shape, jnp.bfloat16),
        ],
        in_specs=[vmem, ANY, vmem],
        out_specs=[vmem, vmem],
        scratch_shapes=[
            pltpu.VMEM((seqs * steps, tile, tracks), jnp.int32),
            pltpu.VMEM((half, channels), jnp.bfloat16),
            dma((seqs * steps,)),
            dma,
            dma,
        ],
        compiler_params=pltpu.CompilerParams(
            collective_id=1, has_side_effects=True, vmem_limit_bytes=48 * 2**20
        ),
        name="head",
    )(top, targets, head_weight)


def backward_tower(head_part, cot, weights, hidden, slope, active, bend, sections, zones, unit):
    length, channels = hidden[0].shape
    inner = active[0].shape[1]
    rows = weights.shape[1]
    part = rows // 2
    quarter = part // sections
    levels = zones.bit_length() - 1
    tracks = head_part.shape[1]
    side = head_part.shape[0] // 2
    tile = length // 2
    most = unit * 2 ** (sections - 1)
    f32, bf16 = jnp.float32, jnp.bfloat16

    def kernel(*refs):
        head_ref, cot_ref, weights_ref = refs[:3]
        refs = refs[3:]
        hidden_in, slope_in = refs[:sections], refs[sections : 2 * sections - 1]
        refs = refs[2 * sections - 1 :]
        active_in, bend_in = refs[:sections], refs[sections : 2 * sections]
        refs = refs[2 * sections :]
        out, head_out = refs[:2]
        hidden, slope, active, bend = refs[2:4], refs[4:6], refs[6:8], refs[8:10]
        held, grad, pull, sums, load = refs[10:15]
        met, wire, came, total, zcame, final = refs[15:21]
        hmet, hsum, hcame = refs[21:24]
        sems = refs[24:]

        s, c, d = (lax.axis_index(name) for name in ("section", "seq", "dp"))
        partner = {"section": s, "seq": 1 - c, "dp": d}
        order = [lax.rem(s + k, sections) for k in range(1, sections)]
        across = [{"section": o, "seq": c, "dp": d} for o in order]
        bits = [lax.rem(d // 2**t, 2) for t in range(levels)]
        along = [
            {"section": s, "seq": c, "dp": d + 2**t * (1 - 2 * bits[t])} for t in range(levels)
        ]
        count = [0]

        def fetch(src, dst):
            copy = pltpu.make_async_copy(src, dst, load.at[count[0]])
            count[0] += 1
            copy.start()
            return copy

        bring = {}

        def prefetch(k):
            slot = k % 2
            early = [
                fetch(weights_ref.at[k], held.at[k]),
                fetch(bend_in[k], bend[slot]),
                fetch(active_in[k], active[slot]),
            ]
            late = [fetch(hidden_in[k], hidden[slot])]
            if k:
                late.append(fetch(slope_in[k - 1], slope[slot]))
            bring[k] = (early, late)

        prefetch(sections - 1)
        greet([partner] + across + along)

        sends = []

        def launch(src, dst, pair, index, peer):
            copy = remote(src, dst, sems[2 * pair].at[index], sems[2 * pair + 1].at[index], peer)
            copy.start()
            sends.append(copy)
            return copy

        def block(base, size, number):
            return pl.ds(pl.multiple_of(base + number * size, 8), size)

        flight = {}

        def swap(k):
            far = sums.at[k, block(0, part, 1 - c)]
            flight[k] = [launch(far, met.at[k], 0, k, partner)]

        def spread(k):
            flight[k][0].wait_recv()
            flight[k] = []

            def both(o):
                return met[k, block(0, quarter, o), :] + sums[k, block(c * part, quarter, o), :]

            for n, o in enumerate(order):
                wire[k, n] = both(o).astype(bf16)
                flight[k].append(
                    launch(wire.at[k, n], came.at[k, n], 1, k * (sections - 1) + n, across[n])
                )
            total[k] = both(s)

        def kept(span, t):
            base = 0
            for step in range(t):
                base = base + bits[step] * (span >> (step + 1))
            return base

        def landing(span, t):
            return pl.ds(span - (span >> t), span >> (t + 1))

        def climb(k, t):
            for copy in flight[k]:
                copy.wait_recv()
            if t == 0:
                value = total[k]
                for n in range(sections - 1):
                    value = value + came[k, n].astype(f32)
                total[k] = value
            else:
                mine = block(kept(quarter, t), quarter >> t, 0)
                total[k, mine, :] = total[k, mine, :] + zcame[k, landing(quarter, t - 1), :]
            size = quarter >> (t + 1)
            away = block(kept(quarter, t), size, 1 - bits[t])
            flight[k] = [
                launch(
                    total.at[k, away],
                    zcame.at[k, landing(quarter, t)],
                    2,
                    k * levels + t,
                    along[t],
                )
            ]

        def level(k, t):
            for copy in flight[k]:
                copy.wait_recv()
            mine = block(kept(quarter, t + 1), quarter >> (t + 1), 0)
            if t == levels - 1:
                final[k, mine, :] = total[k, mine, :] + zcame[k, landing(quarter, t), :]
            piece = final.at[k, mine]
            flight[k] = [launch(piece, piece, 3, k * levels + t, along[t])]

        def home(k):
            owner = {"section": k, "seq": c, "dp": d}
            index = lax.rem(s + 2 * sections - k - 1, sections)
            place = out.at[block(c * part, quarter, s)]
            return remote(final.at[k], place, sems[8].at[k], sems[9].at[index], owner)

        def deliver(k):
            for copy in flight[k]:
                copy.wait_recv()

            @pl.when(s != k)
            def _():
                home(k).start()

            @pl.when(s == k)
            def _():
                out[block(c * part, quarter, s), :] = final[k]
                relay(0, s).start()

        def relay(n, source):
            piece = out.at[block(c * part, quarter, source)]
            return remote(piece, piece, sems[10].at[n], sems[11].at[n], partner)

        def hand(k):
            @pl.when(s == k)
            def _():
                for n, o in enumerate(order):
                    piece = out.at[block(c * part, quarter, o)]
                    remote(final.at[k], piece, sems[8].at[k], sems[9].at[n], across[n]).wait_recv()
                    relay(n + 1, o).start()

        def settle(k):
            @pl.when(s != k)
            def _():
                home(k).wait_send()

            @pl.when(s == k)
            def _():
                for n, o in enumerate([s] + order):
                    relay(n, o).wait()

        def head_swap():
            far = head_ref.at[block(0, side, 1 - c)]
            flight["h"] = [launch(far, hmet, 6, 0, partner)]

        def head_climb(t):
            flight["h"][0].wait_recv()
            if t == 0:
                hsum[...] = hmet[...] + head_ref[block(0, side, c), :]
            else:
                mine = block(kept(side, t), side >> t, 0)
                hsum[mine, :] = hsum[mine, :] + hcame[landing(side, t - 1), :]
            away = block(kept(side, t), side >> (t + 1), 1 - bits[t])
            flight["h"] = [
                launch(hsum.at[away], hcame.at[landing(side, t)], 7, t, along[t])
            ]

        flight["r"] = []

        def pass_on(start, size):
            piece = head_out.at[block(c * side + start, size, 0)]
            flight["r"].append(launch(piece, piece, 9, len(flight["r"]), partner))

        def other(span, t):
            return kept(span, t) + (1 - bits[t]) * (span >> (t + 1))

        def head_level(t):
            flight["h"][0].wait_recv()
            start, size = kept(side, t + 1), side >> (t + 1)
            place = block(c * side + start, size, 0)
            if t == levels - 1:
                mine = block(start, size, 0)
                head_out[place, :] = hsum[mine, :] + hcame[landing(side, t), :]
                pass_on(start, size)
            else:
                pass_on(other(side, t + 1), side >> (t + 2))
            piece = head_out.at[place]
            flight["h"] = [launch(piece, piece, 8, t, along[t])]

        def head_hand():
            flight["h"][0].wait_recv()
            pass_on(other(side, 0), side // 2)

        head_swap()
        pull[pl.ds(0, most), :] = jnp.zeros((most, inner), bf16)
        pull[pl.ds(most + length, most), :] = jnp.zeros((most, inner), bf16)
        sums[...] = jnp.zeros_like(sums)

        top = sections - 1
        stages = {}
        for k in range(sections):
            line = [lambda k=k: swap(k), lambda k=k: spread(k)]
            line += [lambda k=k, t=t: climb(k, t) for t in range(levels)]
            line += [lambda k=k, t=t: level(k, t) for t in reversed(range(levels))]
            stages[k] = line + [lambda k=k: deliver(k), lambda k=k: hand(k)]
        line = [lambda t=t: head_climb(t) for t in range(levels)]
        line += [lambda t=t: head_level(t) for t in reversed(range(levels))]
        stages["h"] = line + [head_hand]
        marks = {}

        def plan(name, at, gap, until):
            while at <= until and stages[name]:
                marks.setdefault(at, []).append(stages[name].pop(0))
                at += gap

        ends = 4 * sections - 1
        for k in reversed(range(sections)):
            plan(k, 4 * (top - k) + 3, 2, ends)
        plan("h", 1, 4, ends)
        clock = [0]

        def tick():
            for stage in marks.get(clock[0], []):
                stage()
            clock[0] += 1

        for k in reversed(range(sections)):
            by = unit * 2**k
            slot = k % 2
            above = cot_ref if k == top else grad
            if k:
                prefetch(k - 1)
            for copy in bring[k][0]:
                copy.wait()

            def inward(i, k=k, slot=slot, above=above):
                place = i * tile
                here = above[pl.ds(place, tile), :]
                back = times_transposed(here, held[k, pl.ds(3 * inner, inner), :])
                back = back * bend[slot][pl.ds(place, tile), :].astype(f32)
                pull[pl.ds(most + place, tile), :] = back.astype(bf16)
                sums[k, pl.ds(3 * inner, inner), :] += contract_rows(
                    active[slot][pl.ds(place, tile), :], here
                )

            for i in range(length // tile):
                inward(i)
                tick()
            for copy in bring[k][1]:
                copy.wait()

            def outward(i, k=k, by=by, slot=slot, above=above):
                place = i * tile
                there = hidden[slot][pl.ds(place, tile), :]
                value = None
                for j in range(3):
                    piece = pull[pl.ds(most + place + (1 - j) * by, tile), :]
                    span = pl.ds(j * inner, inner)
                    sums[k, span, :] += contract_rows(piece, there)
                    if k:
                        term = jnp.dot(piece, held[k, span, :], preferred_element_type=f32)
                        value = term if value is None else value + term
                if k:
                    value = value * slope[slot][pl.ds(place, tile), :].astype(f32)
                    value = value + above[pl.ds(place, tile), :].astype(f32)
                    grad[pl.ds(place, tile), :] = value.astype(bf16)

            for i in range(length // tile):
                outward(i)
                tick()

        while any(stages.values()):
            for name in [*reversed(range(1, sections)), "h", 0]:
                if stages[name]:
                    stages[name].pop(0)()
        for copy in flight["r"]:
            copy.wait_recv()
        for k in range(sections):
            settle(k)
        for copy in sends:
            copy.wait_send()

    dma = pltpu.SemaphoreType.DMA

    def pair(count):
        return [dma((count,))] * 2

    long, thin = pltpu.VMEM((length, channels), bf16), pltpu.VMEM((length, inner), bf16)
    vmem = pl.BlockSpec(memory_space=pltpu.VMEM)
    return pl.pallas_call(
        kernel,
        out_shape=[
            jax.ShapeDtypeStruct((rows, channels), f32),
            jax.ShapeDtypeStruct(head_part.shape, f32),
        ],
        in_specs=[vmem, vmem] + [ANY] * (4 * sections),
        out_specs=[vmem, vmem],
        scratch_shapes=[long] * 4
        + [thin] * 4
        + [
            pltpu.VMEM(weights.shape, bf16),
            long,
            pltpu.VMEM((length + 2 * most, inner), bf16),
            pltpu.VMEM((sections, rows, channels), f32),
            dma((5 * sections,)),
            pltpu.VMEM((sections, part, channels), f32),
            pltpu.VMEM((sections, sections - 1, quarter, channels), bf16),
            pltpu.VMEM((sections, sections - 1, quarter, channels), bf16),
            pltpu.VMEM((sections, quarter, channels), f32),
            pltpu.VMEM((sections, quarter, channels), f32),
            pltpu.VMEM((sections, quarter, channels), f32),
            pltpu.VMEM((side, tracks), f32),
            pltpu.VMEM((side, tracks), f32),
            pltpu.VMEM((side, tracks), f32),
        ]
        + pair(sections)
        + pair(sections * (sections - 1))
        + pair(sections * levels)
        + pair(sections * levels)
        + [dma((sections,)), dma((sections,))]
        + pair(sections)
        + pair(1)
        + pair(levels)
        + pair(levels)
        + pair(levels + 1),
        compiler_params=pltpu.CompilerParams(
            collective_id=2, has_side_effects=True, vmem_limit_bytes=56 * 2**20
        ),
        name="backward_tower",
    )(head_part, cot, weights, *hidden, *slope, *active, *bend)


def finish(total, head_sum, split):
    def kernel(total_ref, head_ref, conv_out, proj_out, head_out, sems):
        copies = [
            pltpu.make_async_copy(total_ref.at[pl.ds(0, split)], conv_out, sems.at[0]),
            pltpu.make_async_copy(
                total_ref.at[pl.ds(split, total.shape[0] - split)], proj_out, sems.at[1]
            ),
            pltpu.make_async_copy(head_ref, head_out, sems.at[2]),
        ]
        for copy in copies:
            copy.start()
        for copy in copies:
            copy.wait()

    width = total.shape[1]
    return pl.pallas_call(
        kernel,
        out_shape=[
            jax.ShapeDtypeStruct((split, width), total.dtype),
            jax.ShapeDtypeStruct((total.shape[0] - split, width), total.dtype),
            jax.ShapeDtypeStruct(head_sum.shape, head_sum.dtype),
        ],
        in_specs=[ANY] * 2,
        out_specs=[ANY] * 3,
        scratch_shapes=[pltpu.SemaphoreType.DMA((3,))],
        name="finish",
    )(total, head_sum)


def plain_body(bases, targets, stem_weight, conv_weight, proj_weight, head_weight):
    sections = lax.axis_size("section")
    seqs = lax.axis_size("seq")
    section_number = lax.axis_index("section")
    batches, row_count, bin_width = bases.shape
    channels = stem_weight.shape[1]
    length = row_count * seqs
    factor = 1.0 / math.sqrt(batches * lax.axis_size("dp") * length)
    unit = length // 2**sections
    local_q = row_count // unit
    blocks = length // unit
    columns = batches * unit // (seqs * sections)

    conv_all = lax.all_gather(conv_weight, "section", axis=0, tiled=True)
    proj_all = lax.all_gather(proj_weight, "section", axis=0, tiled=True)

    def to_chains(value):
        value = lax.all_to_all(value, "seq", split_axis=1, concat_axis=0, tiled=True)
        return value.reshape(blocks * columns, value.shape[-1])

    own = bases.reshape(batches, local_q, unit, bin_width).transpose(1, 0, 2, 3)
    own = own.reshape(local_q, seqs, sections, columns, bin_width)
    own = lax.dynamic_index_in_dim(own, section_number, 2, keepdims=False)
    picked = to_chains(own.astype(jnp.bfloat16))
    onehot = jnp.concatenate([(picked == c).astype(jnp.bfloat16) for c in range(4)], 1)
    stem = stem_weight.reshape(bin_width, 4, channels).transpose(1, 0, 2).reshape(-1, channels)
    state = jnp.dot(onehot, stem, preferred_element_type=jnp.float32).astype(jnp.bfloat16)

    saved = []
    for layer in range(sections):
        by = columns * 2**layer
        taps = conv_all[layer].reshape(-1, conv_all.shape[-1])
        hidden = gelu_value(state.astype(jnp.float32)).astype(jnp.bfloat16)
        wide = jnp.concatenate([shift_rows(hidden, by), hidden, shift_rows(hidden, -by)], 1)
        inner_sum = jnp.dot(wide, taps, preferred_element_type=jnp.float32)
        active = gelu_value(inner_sum).astype(jnp.bfloat16)
        update = jnp.dot(active, proj_all[layer], preferred_element_type=jnp.float32)
        saved.append((state, wide, inner_sum, active))
        state = (state.astype(jnp.float32) + update).astype(jnp.bfloat16)

    lifted = gelu_value(state.astype(jnp.float32)).astype(jnp.bfloat16)
    lifted = lifted.reshape(seqs, local_q, 1, columns, channels)
    lifted = lax.all_to_all(lifted, "seq", split_axis=0, concat_axis=2, tiled=True)
    lifted = lifted.reshape(local_q, seqs, 1, columns, channels)
    lifted = lax.all_gather(lifted, "section", axis=2, tiled=True)
    lifted = lifted.reshape(local_q, batches, unit, channels).transpose(1, 0, 2, 3)
    lifted = lifted.reshape(batches * row_count, channels)

    logits = jnp.dot(lifted, head_weight, preferred_element_type=jnp.float32)
    counts = targets.reshape(batches * row_count, targets.shape[2]).astype(jnp.float32)
    slope = ((jnp.exp(logits) - counts) * factor).astype(jnp.bfloat16)
    head_sum = lax.psum(contract_rows(lifted, slope), ("seq", "dp"))
    lift_part = times_transposed(slope, head_weight)

    lift_part = lift_part.reshape(batches, local_q, unit, channels).transpose(1, 0, 2, 3)
    lift_part = lift_part.reshape(local_q, seqs, sections, columns, channels)
    lift_part = lax.psum_scatter(lift_part, "section", scatter_dimension=2, tiled=True)
    lift_grad = to_chains(lift_part.reshape(local_q, seqs, columns, channels))


    grad = (lift_grad * gelu_slope(state.astype(jnp.float32))).astype(jnp.bfloat16)
    parts = []
    for layer in reversed(range(sections)):
        by = columns * 2**layer
        start_state, wide, inner_sum, active = saved[layer]
        kernel = conv_all[layer]
        proj_part = contract_rows(active, grad)
        active_grad = times_transposed(grad, proj_all[layer])
        inner_grad = (active_grad * gelu_slope(inner_sum)).astype(jnp.bfloat16)
        parts.append(jnp.concatenate([contract_rows(inner_grad, wide), proj_part], 1))
        wide_grad = jnp.concatenate(
            [shift_rows(inner_grad, -by), inner_grad, shift_rows(inner_grad, by)], 1
        )
        turned = kernel.transpose(0, 2, 1).reshape(-1, channels)
        hidden_grad = jnp.dot(wide_grad, turned, preferred_element_type=jnp.float32)
        grad = (
            grad.astype(jnp.float32) + hidden_grad * gelu_slope(start_state.astype(jnp.float32))
        ).astype(jnp.bfloat16)
    parts = jnp.stack(parts[::-1])
    total = lax.psum_scatter(parts, "section", scatter_dimension=0, tiled=True)
    total = lax.psum(total[0], ("seq", "dp"))
    taps_width = total.shape[1] - channels
    conv_sum = total[:, :taps_width].T.reshape(conv_weight.shape)
    return conv_sum, total[:, taps_width:][None], head_sum


def paired_body(bases, targets, stem_weight, conv_weight, proj_weight, head_weight):
    sections = lax.axis_size("section")
    zones = lax.axis_size("dp")
    batches, half, bin_width = bases.shape
    channels = stem_weight.shape[1]
    inner = proj_weight.shape[1]
    length = batches * half
    unit = length // 2**sections
    factor = 1.0 / math.sqrt(batches * zones * length)
    stem = stem_weight.reshape(bin_width, 4, channels).transpose(1, 0, 2).reshape(-1, channels)
    taps = conv_weight[0].transpose(0, 2, 1).reshape(3 * inner, channels)
    top, weights, hidden, slope, active, bend = forward_tower(
        bases, stem, taps, proj_weight[0], sections, unit
    )
    head_part, cot = head(top, targets, head_weight, factor)
    cot = cot.reshape(length, channels)
    total, head_sum = backward_tower(
        head_part, cot, weights, hidden, slope, active, bend, sections, zones, unit
    )
    conv_sum, proj_sum, head_sum = finish(total, head_sum, 3 * inner)
    conv_sum = conv_sum.reshape(3, inner, channels).transpose(0, 2, 1)
    return conv_sum[None], proj_sum[None], head_sum


def body(bases, targets, stem_weight, conv_weight, proj_weight, head_weight):
    sections, zones = lax.axis_size("section"), lax.axis_size("dp")
    batches, half = bases.shape[:2]
    inner = proj_weight.shape[1]
    unit = batches * half // 2**sections
    paired = lax.axis_size("seq") == 2 and batches == 2 and zones > 1 and sections > 1
    paired = paired and unit % 16 == 0 and half % 16 == 0 and inner % 16 == 0
    paired = paired and (2 * inner) % (16 * sections) == 0
    paired = paired and (2 * inner) % (8 * sections * zones) == 0
    paired = paired and zones & (zones - 1) == 0
    paired = paired and stem_weight.shape[1] % (16 * zones) == 0
    run = paired_body if paired else plain_body
    return run(bases, targets, stem_weight, conv_weight, proj_weight, head_weight)


def solution(mesh):
    in_specs = (
        P("dp", "seq", None),
        P("dp", "seq", "section"),
        P(),
        P("section", None, None, None),
        P("section", None, None),
        P(None, "section"),
    )
    out_specs = (P("section", None, None, None), P("section", None, None), P(None, "section"))
    return jax.shard_map(body, mesh=mesh, in_specs=in_specs, out_specs=out_specs, check_vma=False)
```

```python
import math

import jax
import jax.numpy as jnp
from jax import lax
from jax.experimental import pallas as pl
from jax.experimental.pallas import tpu as pltpu
from jax.sharding import PartitionSpec as P

SQRT_TWO_OVER_PI = 0.7978845608028654
CUBIC_TERM = 0.044715


def gelu_value(inputs):
    return (
        0.5
        * inputs
        * (1.0 + jnp.tanh(SQRT_TWO_OVER_PI * (inputs + CUBIC_TERM * inputs * inputs * inputs)))
    )


def gelu_slope(inputs):
    tangent = jnp.tanh(SQRT_TWO_OVER_PI * (inputs + CUBIC_TERM * inputs * inputs * inputs))
    return 0.5 * (1.0 + tangent) + 0.5 * inputs * (1.0 - tangent * tangent) * SQRT_TWO_OVER_PI * (
        1.0 + 3.0 * CUBIC_TERM * inputs * inputs
    )


def contract_rows(left_side, right_side):
    return lax.dot_general(
        left_side, right_side, (((0,), (0,)), ((), ())), preferred_element_type=jnp.float32
    )


def times_transposed(left_side, right_side):
    return lax.dot_general(
        left_side, right_side, (((1,), (1,)), ((), ())), preferred_element_type=jnp.float32
    )


def shift_rows(value, by):
    if abs(by) >= value.shape[0]:
        return jnp.zeros_like(value)
    pad = jnp.zeros((abs(by),) + value.shape[1:], value.dtype)
    if by > 0:
        return jnp.concatenate([pad, value[:-by]], 0)
    return jnp.concatenate([value[-by:], pad], 0)


MESH = pl.DeviceIdType.MESH
ANY = pl.BlockSpec(memory_space=pl.ANY)


def greet(peers):
    barrier = pltpu.get_barrier_semaphore()
    for peer in peers:
        pl.semaphore_signal(barrier, inc=1, device_id=peer, device_id_type=MESH)
    pl.semaphore_wait(barrier, len(peers))


def remote(src, dst, send, recv, peer):
    return pltpu.make_async_remote_copy(
        src_ref=src, dst_ref=dst, send_sem=send, recv_sem=recv, device_id=peer, device_id_type=MESH
    )


def both_gelu(inputs):
    square = inputs * inputs
    tangent = jnp.tanh(
        inputs * (SQRT_TWO_OVER_PI + (SQRT_TWO_OVER_PI * CUBIC_TERM) * square)
    )
    gate = 0.5 + 0.5 * tangent
    value = inputs * gate
    inside = 2.0 * SQRT_TWO_OVER_PI + (6.0 * SQRT_TWO_OVER_PI * CUBIC_TERM) * square
    return value, gate + value * (1.0 - gate) * inside


def tile_of(rows):
    for size in (768, 512, 384, 256, 192, 128, 96, 64, 48, 32, 16):
        if rows % size == 0:
            return size
    return rows


def forward_tower(bases, stem, taps, proj, sections, unit):
    seqs, half, width = bases.shape
    length = seqs * half
    channels = stem.shape[1]
    inner = proj.shape[0]
    rows = taps.shape[0] + inner
    part = rows // 2
    tile = tile_of(half)
    steps = half // tile
    shifts = [unit * 2**k for k in range(sections)]

    def kernel(*refs):
        bases_ref, stem_ref, taps_ref, proj_ref = refs[:4]
        refs = refs[4:]
        top_ref, weights_ref = refs[:2]
        hidden_out, slope_out = refs[2 : 2 + sections], refs[2 + sections : 1 + 2 * sections]
        refs = refs[1 + 2 * sections :]
        active_out, bend_out = refs[:sections], refs[sections : 2 * sections]
        refs = refs[2 * sections :]
        full, held, turned, state = refs[:4]
        refs = refs[4:]
        hidden, slope = refs[:sections], refs[sections : 2 * sections - 1]
        refs = refs[2 * sections - 1 :]
        active, bend = refs[:sections], refs[sections : 2 * sections]
        refs = refs[2 * sections :]
        bsend, brecv, send, recv, send2, recv2, tsend, trecv, own_sem, out_sem = refs

        s, c = lax.axis_index("section"), lax.axis_index("seq")
        partner = {"section": s, "seq": 1 - c}
        peers = [{"section": lax.rem(s + k, sections), "seq": c} for k in range(1, sections)]
        loads = [
            pltpu.make_async_copy(bases_ref.at[c], full.at[c], own_sem.at[0]),
            pltpu.make_async_copy(
                taps_ref, held.at[s, pl.ds(0, taps.shape[0])], own_sem.at[1]
            ),
            pltpu.make_async_copy(
                proj_ref, held.at[s, pl.ds(taps.shape[0], inner)], own_sem.at[2]
            ),
        ]
        for copy in loads:
            copy.start()
        greet(peers + [partner])
        across = remote(bases_ref.at[1 - c], full.at[c], bsend, brecv, partner)
        across.start()
        loads[1].wait()
        loads[2].wait()
        mine = held.at[s, pl.ds(pl.multiple_of(c * part, 16), part)]
        first = []
        for k, peer in enumerate(peers):
            first.append(remote(mine, mine, send.at[k], recv.at[k], peer))
            first[-1].start()
        for k in range(sections):
            edge = jnp.zeros((shifts[k], channels), jnp.bfloat16)
            hidden[k][pl.ds(0, shifts[k]), :] = edge
            hidden[k][pl.ds(shifts[k] + length, shifts[k]), :] = edge

        def begin(number):
            def step(i, carry):
                at = i * tile
                codes = full[number, pl.ds(pl.multiple_of(at, 16), tile), :]
                onehot = jnp.concatenate(
                    [(codes == k).astype(jnp.bfloat16) for k in range(4)], 1
                )
                start = jnp.dot(onehot, stem_ref[...], preferred_element_type=jnp.float32)
                start = start.astype(jnp.bfloat16)
                place = pl.multiple_of(number * half + at, 16)
                state[pl.ds(place, tile), :] = start
                value = gelu_value(start.astype(jnp.float32)).astype(jnp.bfloat16)
                hidden[0][pl.ds(pl.multiple_of(shifts[0] + place, 16), tile), :] = value
                return carry

            lax.fori_loop(0, steps, step, 0)

        loads[0].wait()
        begin(c)
        across.wait_recv()
        begin(1 - c)

        second = []
        for k in range(sections - 1):
            first[k].wait_recv()
            source = lax.rem(s + sections - 1 - k, sections)
            piece = held.at[source, pl.ds(pl.multiple_of(c * part, 16), part)]
            second.append(remote(piece, piece, send2.at[k], recv2.at[k], partner))
            second[-1].start()
        for copy in second:
            copy.wait_recv()

        outs = []

        def keep(src, dst):
            outs.append(pltpu.make_async_copy(src, dst, out_sem.at[len(outs)]))
            outs[-1].start()

        keep(held, weights_ref)
        keep(hidden[0].at[pl.ds(shifts[0], length)], hidden_out[0])

        for k in range(sections):
            by = shifts[k]
            for j in range(3):
                tap = held[k, pl.ds(j * inner, inner), :]
                turned[pl.ds(j * channels, channels), :] = tap.T

            def step_at(place, k=k, by=by):
                wide = jnp.concatenate(
                    [
                        hidden[k][pl.ds(pl.multiple_of(place + j * by, 16), tile), :]
                        for j in range(3)
                    ],
                    1,
                )
                total = jnp.dot(wide, turned[...], preferred_element_type=jnp.float32)
                value, bent = both_gelu(total)
                value = value.astype(jnp.bfloat16)
                active[k][pl.ds(place, tile), :] = value
                bend[k][pl.ds(place, tile), :] = bent.astype(jnp.bfloat16)
                update = jnp.dot(
                    value,
                    held[k, pl.ds(3 * inner, inner), :],
                    preferred_element_type=jnp.float32,
                )
                return (state[pl.ds(place, tile), :].astype(jnp.float32) + update).astype(
                    jnp.bfloat16
                )

            if k < sections - 1:

                def step(i, carry, k=k):
                    place = pl.multiple_of(i * tile, 16)
                    new = step_at(place)
                    state[pl.ds(place, tile), :] = new
                    value, bent = both_gelu(new.astype(jnp.float32))
                    ahead = pl.multiple_of(shifts[k + 1] + place, 16)
                    hidden[k + 1][pl.ds(ahead, tile), :] = value.astype(jnp.bfloat16)
                    slope[k][pl.ds(place, tile), :] = bent.astype(jnp.bfloat16)
                    return carry

                lax.fori_loop(0, length // tile, step, 0)
                keep(hidden[k + 1].at[pl.ds(shifts[k + 1], length)], hidden_out[k + 1])
                keep(slope[k], slope_out[k])
            else:

                def away(i, carry):
                    place = pl.multiple_of((1 - c) * half + i * tile, 16)
                    state[pl.ds(place, tile), :] = step_at(place)
                    return carry

                lax.fori_loop(0, steps, away, 0)
                theirs = state.at[pl.ds(pl.multiple_of((1 - c) * half, 16), half)]
                last = remote(theirs, top_ref.at[c], tsend, trecv, partner)
                last.start()

                def here(i, carry):
                    at = pl.multiple_of(i * tile, 16)
                    place = pl.multiple_of(c * half + at, 16)
                    top_ref[c, pl.ds(at, tile), :] = step_at(place)
                    return carry

                lax.fori_loop(0, steps, here, 0)
            keep(active[k], active_out[k])
            keep(bend[k], bend_out[k])
        for copy in outs:
            copy.wait()
        last.wait()
        across.wait_send()
        for copy in first + second:
            copy.wait_send()

    bf16 = jnp.bfloat16
    long = jax.ShapeDtypeStruct((length, channels), bf16)
    thin = jax.ShapeDtypeStruct((length, inner), bf16)
    dma = pltpu.SemaphoreType.DMA
    copies = 4 * sections
    out = pl.pallas_call(
        kernel,
        out_shape=[
            jax.ShapeDtypeStruct((seqs, half, channels), bf16),
            jax.ShapeDtypeStruct((sections, rows, channels), bf16),
        ]
        + [long] * (2 * sections - 1)
        + [thin] * (2 * sections),
        in_specs=[ANY, pl.BlockSpec(memory_space=pltpu.VMEM), ANY, ANY],
        out_specs=[pl.BlockSpec(memory_space=pltpu.VMEM)] + [ANY] * (4 * sections),
        scratch_shapes=[
            pltpu.VMEM((seqs, half, width), jnp.int32),
            pltpu.VMEM((sections, rows, channels), bf16),
            pltpu.VMEM((3 * channels, inner), bf16),
            pltpu.VMEM((length, channels), bf16),
        ]
        + [pltpu.VMEM((length + 2 * by, channels), bf16) for by in shifts]
        + [pltpu.VMEM((length, channels), bf16)] * (sections - 1)
        + [pltpu.VMEM((length, inner), bf16)] * (2 * sections)
        + [dma, dma]
        + [dma((sections - 1,))] * 4
        + [dma, dma, dma((3,)), dma((copies,))],
        compiler_params=pltpu.CompilerParams(
            collective_id=0, has_side_effects=True, vmem_limit_bytes=54 * 2**20
        ),
        name="forward_tower",
    )(bases, stem, taps, proj)
    top, weights = out[:2]
    hidden, slope = out[2 : 2 + sections], out[2 + sections : 1 + 2 * sections]
    active = out[1 + 2 * sections : 1 + 3 * sections]
    bend = out[1 + 3 * sections :]
    return top, weights, hidden, slope, active, bend


def head(top, targets, head_weight, factor):
    seqs, half, channels = top.shape
    tracks = head_weight.shape[1]
    tile = tile_of(half)
    if half % 512 == 0:
        tile = 512
    steps = half // tile

    def kernel(
        top_ref, targets_ref, weight_ref, grad_ref, cot_ref, counts, stage, load, send, recv
    ):
        s, c = lax.axis_index("section"), lax.axis_index("seq")
        partner = {"section": s, "seq": 1 - c}
        loads = []
        for n, b in enumerate((1 - c, c)):
            for i in range(steps):
                loads.append(
                    pltpu.make_async_copy(
                        targets_ref.at[b, pl.ds(i * tile, tile)],
                        counts.at[n * steps + i],
                        load.at[n * steps + i],
                    )
                )
                loads[-1].start()
        greet([partner])
        grad_ref[...] = jnp.zeros_like(grad_ref)

        def run(b, n, store):
            def step(i, carry):
                at = pl.multiple_of(i * tile, 16)
                pltpu.make_async_copy(
                    targets_ref.at[b, pl.ds(at, tile)], counts.at[n + i], load.at[n + i]
                ).wait()
                value, bent = both_gelu(top_ref[b, pl.ds(at, tile), :].astype(jnp.float32))
                lifted = value.astype(jnp.bfloat16)
                logits = jnp.dot(lifted, weight_ref[...], preferred_element_type=jnp.float32)
                drop = jnp.exp(logits) - counts[n + i].astype(jnp.float32)
                drop = (drop * factor).astype(jnp.bfloat16)
                grad_ref[...] += contract_rows(lifted, drop)
                lift = times_transposed(drop, weight_ref[...])
                store(at, (lift * bent).astype(jnp.bfloat16))
                return carry

            lax.fori_loop(0, steps, step, 0)

        def away(at, value):
            stage[pl.ds(at, tile), :] = value

        def here(at, value):
            cot_ref[c, pl.ds(at, tile), :] = value

        run(1 - c, 0, away)
        copy = remote(stage, cot_ref.at[c], send, recv, partner)
        copy.start()
        run(c, steps, here)
        copy.wait()

    vmem = pl.BlockSpec(memory_space=pltpu.VMEM)
    dma = pltpu.SemaphoreType.DMA
    return pl.pallas_call(
        kernel,
        out_shape=[
            jax.ShapeDtypeStruct((channels, tracks), jnp.float32),
            jax.ShapeDtypeStruct(top.shape, jnp.bfloat16),
        ],
        in_specs=[vmem, ANY, vmem],
        out_specs=[vmem, vmem],
        scratch_shapes=[
            pltpu.VMEM((seqs * steps, tile, tracks), jnp.int32),
            pltpu.VMEM((half, channels), jnp.bfloat16),
            dma((seqs * steps,)),
            dma,
            dma,
        ],
        compiler_params=pltpu.CompilerParams(
            collective_id=1, has_side_effects=True, vmem_limit_bytes=48 * 2**20
        ),
        name="head",
    )(top, targets, head_weight)


def backward_tower(head_part, cot, weights, hidden, slope, active, bend, sections, zones, unit):
    length, channels = hidden[0].shape
    inner = active[0].shape[1]
    rows = weights.shape[1]
    part = rows // 2
    quarter = part // sections
    levels = zones.bit_length() - 1
    tracks = head_part.shape[1]
    side = head_part.shape[0] // 2
    tile = length // 2
    most = unit * 2 ** (sections - 1)
    f32, bf16 = jnp.float32, jnp.bfloat16

    def kernel(*refs):
        head_ref, cot_ref, weights_ref = refs[:3]
        refs = refs[3:]
        hidden_in, slope_in = refs[:sections], refs[sections : 2 * sections - 1]
        refs = refs[2 * sections - 1 :]
        active_in, bend_in = refs[:sections], refs[sections : 2 * sections]
        refs = refs[2 * sections :]
        out, head_out = refs[:2]
        hidden, slope, active, bend = refs[2:4], refs[4:6], refs[6:8], refs[8:10]
        held, grad, pull, sums, load = refs[10:15]
        met, wire, came, total, zcame, final = refs[15:21]
        hmet, hsum, hcame = refs[21:24]
        sems = refs[24:]

        s, c, d = (lax.axis_index(name) for name in ("section", "seq", "dp"))
        partner = {"section": s, "seq": 1 - c, "dp": d}
        order = [lax.rem(s + k, sections) for k in range(1, sections)]
        across = [{"section": o, "seq": c, "dp": d} for o in order]
        bits = [lax.rem(d // 2**t, 2) for t in range(levels)]
        along = [
            {"section": s, "seq": c, "dp": d + 2**t * (1 - 2 * bits[t])} for t in range(levels)
        ]
        count = [0]

        def fetch(src, dst):
            copy = pltpu.make_async_copy(src, dst, load.at[count[0]])
            count[0] += 1
            copy.start()
            return copy

        bring = {}

        def prefetch(k):
            slot = k % 2
            early = [
                fetch(weights_ref.at[k], held.at[k]),
                fetch(bend_in[k], bend[slot]),
                fetch(active_in[k], active[slot]),
            ]
            late = [fetch(hidden_in[k], hidden[slot])]
            if k:
                late.append(fetch(slope_in[k - 1], slope[slot]))
            bring[k] = (early, late)

        prefetch(sections - 1)
        greet([partner] + across + along)

        sends = []

        def launch(src, dst, pair, index, peer):
            copy = remote(src, dst, sems[2 * pair].at[index], sems[2 * pair + 1].at[index], peer)
            copy.start()
            sends.append(copy)
            return copy

        def block(base, size, number):
            return pl.ds(pl.multiple_of(base + number * size, 8), size)

        flight = {}

        def swap(k):
            far = sums.at[k, block(0, part, 1 - c)]
            flight[k] = [launch(far, met.at[k], 0, k, partner)]

        def spread(k):
            flight[k][0].wait_recv()
            flight[k] = []

            def both(o):
                return met[k, block(0, quarter, o), :] + sums[k, block(c * part, quarter, o), :]

            for n, o in enumerate(order):
                wire[k, n] = both(o).astype(bf16)
                flight[k].append(
                    launch(wire.at[k, n], came.at[k, n], 1, k * (sections - 1) + n, across[n])
                )
            total[k] = both(s)

        def kept(span, t):
            base = 0
            for step in range(t):
                base = base + bits[step] * (span >> (step + 1))
            return base

        def landing(span, t):
            return pl.ds(span - (span >> t), span >> (t + 1))

        def climb(k, t):
            for copy in flight[k]:
                copy.wait_recv()
            if t == 0:
                value = total[k]
                for n in range(sections - 1):
                    value = value + came[k, n].astype(f32)
                total[k] = value
            else:
                mine = block(kept(quarter, t), quarter >> t, 0)
                total[k, mine, :] = total[k, mine, :] + zcame[k, landing(quarter, t - 1), :]
            size = quarter >> (t + 1)
            away = block(kept(quarter, t), size, 1 - bits[t])
            flight[k] = [
                launch(
                    total.at[k, away],
                    zcame.at[k, landing(quarter, t)],
                    2,
                    k * levels + t,
                    along[t],
                )
            ]

        def level(k, t):
            for copy in flight[k]:
                copy.wait_recv()
            mine = block(kept(quarter, t + 1), quarter >> (t + 1), 0)
            if t == levels - 1:
                final[k, mine, :] = total[k, mine, :] + zcame[k, landing(quarter, t), :]
            piece = final.at[k, mine]
            flight[k] = [launch(piece, piece, 3, k * levels + t, along[t])]

        def home(k):
            owner = {"section": k, "seq": c, "dp": d}
            index = lax.rem(s + 2 * sections - k - 1, sections)
            place = out.at[block(c * part, quarter, s)]
            return remote(final.at[k], place, sems[8].at[k], sems[9].at[index], owner)

        def deliver(k):
            for copy in flight[k]:
                copy.wait_recv()

            @pl.when(s != k)
            def _():
                home(k).start()

            @pl.when(s == k)
            def _():
                out[block(c * part, quarter, s), :] = final[k]
                relay(0, s).start()

        def relay(n, source):
            piece = out.at[block(c * part, quarter, source)]
            return remote(piece, piece, sems[10].at[n], sems[11].at[n], partner)

        def hand(k):
            @pl.when(s == k)
            def _():
                for n, o in enumerate(order):
                    piece = out.at[block(c * part, quarter, o)]
                    remote(final.at[k], piece, sems[8].at[k], sems[9].at[n], across[n]).wait_recv()
                    relay(n + 1, o).start()

        def settle(k):
            @pl.when(s != k)
            def _():
                home(k).wait_send()

            @pl.when(s == k)
            def _():
                for n, o in enumerate([s] + order):
                    relay(n, o).wait()

        def head_swap():
            far = head_ref.at[block(0, side, 1 - c)]
            flight["h"] = [launch(far, hmet, 6, 0, partner)]

        def head_climb(t):
            flight["h"][0].wait_recv()
            if t == 0:
                hsum[...] = hmet[...] + head_ref[block(0, side, c), :]
            else:
                mine = block(kept(side, t), side >> t, 0)
                hsum[mine, :] = hsum[mine, :] + hcame[landing(side, t - 1), :]
            away = block(kept(side, t), side >> (t + 1), 1 - bits[t])
            flight["h"] = [
                launch(hsum.at[away], hcame.at[landing(side, t)], 7, t, along[t])
            ]

        flight["r"] = []

        def pass_on(start, size):
            piece = head_out.at[block(c * side + start, size, 0)]
            flight["r"].append(launch(piece, piece, 9, len(flight["r"]), partner))

        def other(span, t):
            return kept(span, t) + (1 - bits[t]) * (span >> (t + 1))

        def head_level(t):
            flight["h"][0].wait_recv()
            start, size = kept(side, t + 1), side >> (t + 1)
            place = block(c * side + start, size, 0)
            if t == levels - 1:
                mine = block(start, size, 0)
                head_out[place, :] = hsum[mine, :] + hcame[landing(side, t), :]
                pass_on(start, size)
            else:
                pass_on(other(side, t + 1), side >> (t + 2))
            piece = head_out.at[place]
            flight["h"] = [launch(piece, piece, 8, t, along[t])]

        def head_hand():
            flight["h"][0].wait_recv()
            pass_on(other(side, 0), side // 2)

        head_swap()
        pull[pl.ds(0, most), :] = jnp.zeros((most, inner), bf16)
        pull[pl.ds(most + length, most), :] = jnp.zeros((most, inner), bf16)
        sums[...] = jnp.zeros_like(sums)

        top = sections - 1
        stages = {}
        for k in range(sections):
            line = [lambda k=k: swap(k), lambda k=k: spread(k)]
            line += [lambda k=k, t=t: climb(k, t) for t in range(levels)]
            line += [lambda k=k, t=t: level(k, t) for t in reversed(range(levels))]
            stages[k] = line + [lambda k=k: deliver(k), lambda k=k: hand(k)]
        line = [lambda t=t: head_climb(t) for t in range(levels)]
        line += [lambda t=t: head_level(t) for t in reversed(range(levels))]
        stages["h"] = line + [head_hand]
        marks = {}

        def plan(name, ticks):
            for at in ticks:
                if at <= 4 * sections - 1 and stages[name]:
                    marks.setdefault(at, []).append(stages[name].pop(0))

        for k in reversed(range(sections)):
            plan(k, [4 * (top - k) + 3 + gap for gap in (0, 2, 4, 7, 9, 11)])
        plan("h", (2, 7, 14))
        clock = [0]

        def tick():
            for stage in marks.get(clock[0], []):
                stage()
            clock[0] += 1

        for k in reversed(range(sections)):
            by = unit * 2**k
            slot = k % 2
            above = cot_ref if k == top else grad
            if k:
                prefetch(k - 1)
            for copy in bring[k][0]:
                copy.wait()

            def inward(i, k=k, slot=slot, above=above):
                place = i * tile
                here = above[pl.ds(place, tile), :]
                back = times_transposed(here, held[k, pl.ds(3 * inner, inner), :])
                back = back * bend[slot][pl.ds(place, tile), :].astype(f32)
                pull[pl.ds(most + place, tile), :] = back.astype(bf16)
                sums[k, pl.ds(3 * inner, inner), :] += contract_rows(
                    active[slot][pl.ds(place, tile), :], here
                )

            for i in range(length // tile):
                inward(i)
                tick()
            for copy in bring[k][1]:
                copy.wait()

            def outward(i, k=k, by=by, slot=slot, above=above):
                place = i * tile
                there = hidden[slot][pl.ds(place, tile), :]
                value = None
                for j in range(3):
                    piece = pull[pl.ds(most + place + (1 - j) * by, tile), :]
                    span = pl.ds(j * inner, inner)
                    sums[k, span, :] += contract_rows(piece, there)
                    if k:
                        term = jnp.dot(piece, held[k, span, :], preferred_element_type=f32)
                        value = term if value is None else value + term
                if k:
                    value = value * slope[slot][pl.ds(place, tile), :].astype(f32)
                    value = value + above[pl.ds(place, tile), :].astype(f32)
                    grad[pl.ds(place, tile), :] = value.astype(bf16)

            for i in range(length // tile):
                outward(i)
                tick()

        rounds = 0
        while any(stages.values()):
            for name in [*reversed(range(2, sections)), 0, 1, "h"]:
                if stages[name] and (name != "h" or rounds > 1):
                    stages[name].pop(0)()
            rounds += 1
        for copy in flight["r"]:
            copy.wait_recv()
        for k in range(sections):
            settle(k)
        for copy in sends:
            copy.wait_send()

    dma = pltpu.SemaphoreType.DMA

    def pair(count):
        return [dma((count,))] * 2

    long, thin = pltpu.VMEM((length, channels), bf16), pltpu.VMEM((length, inner), bf16)
    vmem = pl.BlockSpec(memory_space=pltpu.VMEM)
    return pl.pallas_call(
        kernel,
        out_shape=[
            jax.ShapeDtypeStruct((rows, channels), f32),
            jax.ShapeDtypeStruct(head_part.shape, f32),
        ],
        in_specs=[vmem, vmem] + [ANY] * (4 * sections),
        out_specs=[vmem, vmem],
        scratch_shapes=[long] * 4
        + [thin] * 4
        + [
            pltpu.VMEM(weights.shape, bf16),
            long,
            pltpu.VMEM((length + 2 * most, inner), bf16),
            pltpu.VMEM((sections, rows, channels), f32),
            dma((5 * sections,)),
            pltpu.VMEM((sections, part, channels), f32),
            pltpu.VMEM((sections, sections - 1, quarter, channels), bf16),
            pltpu.VMEM((sections, sections - 1, quarter, channels), bf16),
            pltpu.VMEM((sections, quarter, channels), f32),
            pltpu.VMEM((sections, quarter, channels), f32),
            pltpu.VMEM((sections, quarter, channels), f32),
            pltpu.VMEM((side, tracks), f32),
            pltpu.VMEM((side, tracks), f32),
            pltpu.VMEM((side, tracks), f32),
        ]
        + pair(sections)
        + pair(sections * (sections - 1))
        + pair(sections * levels)
        + pair(sections * levels)
        + [dma((sections,)), dma((sections,))]
        + pair(sections)
        + pair(1)
        + pair(levels)
        + pair(levels)
        + pair(levels + 1),
        compiler_params=pltpu.CompilerParams(
            collective_id=2, has_side_effects=True, vmem_limit_bytes=48 * 2**20
        ),
        name="backward_tower",
    )(head_part, cot, weights, *hidden, *slope, *active, *bend)


def finish(total, head_sum, split):
    def kernel(total_ref, head_ref, conv_out, proj_out, head_out, sems):
        copies = [
            pltpu.make_async_copy(total_ref.at[pl.ds(0, split)], conv_out, sems.at[0]),
            pltpu.make_async_copy(
                total_ref.at[pl.ds(split, total.shape[0] - split)], proj_out, sems.at[1]
            ),
            pltpu.make_async_copy(head_ref, head_out, sems.at[2]),
        ]
        for copy in copies:
            copy.start()
        for copy in copies:
            copy.wait()

    width = total.shape[1]
    return pl.pallas_call(
        kernel,
        out_shape=[
            jax.ShapeDtypeStruct((split, width), total.dtype),
            jax.ShapeDtypeStruct((total.shape[0] - split, width), total.dtype),
            jax.ShapeDtypeStruct(head_sum.shape, head_sum.dtype),
        ],
        in_specs=[pl.BlockSpec(memory_space=pltpu.VMEM)] * 2,
        out_specs=[ANY] * 3,
        scratch_shapes=[pltpu.SemaphoreType.DMA((3,))],
        compiler_params=pltpu.CompilerParams(vmem_limit_bytes=8 * 2**20),
        name="finish",
    )(total, head_sum)


def plain_body(bases, targets, stem_weight, conv_weight, proj_weight, head_weight):
    sections = lax.axis_size("section")
    seqs = lax.axis_size("seq")
    section_number = lax.axis_index("section")
    batches, row_count, bin_width = bases.shape
    channels = stem_weight.shape[1]
    length = row_count * seqs
    factor = 1.0 / math.sqrt(batches * lax.axis_size("dp") * length)
    unit = length // 2**sections
    local_q = row_count // unit
    blocks = length // unit
    columns = batches * unit // (seqs * sections)

    conv_all = lax.all_gather(conv_weight, "section", axis=0, tiled=True)
    proj_all = lax.all_gather(proj_weight, "section", axis=0, tiled=True)

    def to_chains(value):
        value = lax.all_to_all(value, "seq", split_axis=1, concat_axis=0, tiled=True)
        return value.reshape(blocks * columns, value.shape[-1])

    own = bases.reshape(batches, local_q, unit, bin_width).transpose(1, 0, 2, 3)
    own = own.reshape(local_q, seqs, sections, columns, bin_width)
    own = lax.dynamic_index_in_dim(own, section_number, 2, keepdims=False)
    picked = to_chains(own.astype(jnp.bfloat16))
    onehot = jnp.concatenate([(picked == c).astype(jnp.bfloat16) for c in range(4)], 1)
    stem = stem_weight.reshape(bin_width, 4, channels).transpose(1, 0, 2).reshape(-1, channels)
    state = jnp.dot(onehot, stem, preferred_element_type=jnp.float32).astype(jnp.bfloat16)

    saved = []
    for layer in range(sections):
        by = columns * 2**layer
        taps = conv_all[layer].reshape(-1, conv_all.shape[-1])
        hidden = gelu_value(state.astype(jnp.float32)).astype(jnp.bfloat16)
        wide = jnp.concatenate([shift_rows(hidden, by), hidden, shift_rows(hidden, -by)], 1)
        inner_sum = jnp.dot(wide, taps, preferred_element_type=jnp.float32)
        active = gelu_value(inner_sum).astype(jnp.bfloat16)
        update = jnp.dot(active, proj_all[layer], preferred_element_type=jnp.float32)
        saved.append((state, wide, inner_sum, active))
        state = (state.astype(jnp.float32) + update).astype(jnp.bfloat16)

    lifted = gelu_value(state.astype(jnp.float32)).astype(jnp.bfloat16)
    lifted = lifted.reshape(seqs, local_q, 1, columns, channels)
    lifted = lax.all_to_all(lifted, "seq", split_axis=0, concat_axis=2, tiled=True)
    lifted = lifted.reshape(local_q, seqs, 1, columns, channels)
    lifted = lax.all_gather(lifted, "section", axis=2, tiled=True)
    lifted = lifted.reshape(local_q, batches, unit, channels).transpose(1, 0, 2, 3)
    lifted = lifted.reshape(batches * row_count, channels)

    logits = jnp.dot(lifted, head_weight, preferred_element_type=jnp.float32)
    counts = targets.reshape(batches * row_count, targets.shape[2]).astype(jnp.float32)
    slope = ((jnp.exp(logits) - counts) * factor).astype(jnp.bfloat16)
    head_sum = lax.psum(contract_rows(lifted, slope), ("seq", "dp"))
    lift_part = times_transposed(slope, head_weight)

    lift_part = lift_part.reshape(batches, local_q, unit, channels).transpose(1, 0, 2, 3)
    lift_part = lift_part.reshape(local_q, seqs, sections, columns, channels)
    lift_part = lax.psum_scatter(lift_part, "section", scatter_dimension=2, tiled=True)
    lift_grad = to_chains(lift_part.reshape(local_q, seqs, columns, channels))


    grad = (lift_grad * gelu_slope(state.astype(jnp.float32))).astype(jnp.bfloat16)
    parts = []
    for layer in reversed(range(sections)):
        by = columns * 2**layer
        start_state, wide, inner_sum, active = saved[layer]
        kernel = conv_all[layer]
        proj_part = contract_rows(active, grad)
        active_grad = times_transposed(grad, proj_all[layer])
        inner_grad = (active_grad * gelu_slope(inner_sum)).astype(jnp.bfloat16)
        parts.append(jnp.concatenate([contract_rows(inner_grad, wide), proj_part], 1))
        wide_grad = jnp.concatenate(
            [shift_rows(inner_grad, -by), inner_grad, shift_rows(inner_grad, by)], 1
        )
        turned = kernel.transpose(0, 2, 1).reshape(-1, channels)
        hidden_grad = jnp.dot(wide_grad, turned, preferred_element_type=jnp.float32)
        grad = (
            grad.astype(jnp.float32) + hidden_grad * gelu_slope(start_state.astype(jnp.float32))
        ).astype(jnp.bfloat16)
    parts = jnp.stack(parts[::-1])
    total = lax.psum_scatter(parts, "section", scatter_dimension=0, tiled=True)
    total = lax.psum(total[0], ("seq", "dp"))
    taps_width = total.shape[1] - channels
    conv_sum = total[:, :taps_width].T.reshape(conv_weight.shape)
    return conv_sum, total[:, taps_width:][None], head_sum


def paired_body(bases, targets, stem_weight, conv_weight, proj_weight, head_weight):
    sections = lax.axis_size("section")
    zones = lax.axis_size("dp")
    batches, half, bin_width = bases.shape
    channels = stem_weight.shape[1]
    inner = proj_weight.shape[1]
    length = batches * half
    unit = length // 2**sections
    factor = 1.0 / math.sqrt(batches * zones * length)
    stem = stem_weight.reshape(bin_width, 4, channels).transpose(1, 0, 2).reshape(-1, channels)
    taps = conv_weight[0].transpose(0, 2, 1).reshape(3 * inner, channels)
    top, weights, hidden, slope, active, bend = forward_tower(
        bases, stem, taps, proj_weight[0], sections, unit
    )
    head_part, cot = head(top, targets, head_weight, factor)
    cot = cot.reshape(length, channels)
    total, head_sum = backward_tower(
        head_part, cot, weights, hidden, slope, active, bend, sections, zones, unit
    )
    conv_sum, proj_sum, head_sum = finish(total, head_sum, 3 * inner)
    conv_sum = conv_sum.reshape(3, inner, channels).transpose(0, 2, 1)
    return conv_sum[None], proj_sum[None], head_sum


def body(bases, targets, stem_weight, conv_weight, proj_weight, head_weight):
    sections, zones = lax.axis_size("section"), lax.axis_size("dp")
    batches, half = bases.shape[:2]
    inner = proj_weight.shape[1]
    unit = batches * half // 2**sections
    paired = lax.axis_size("seq") == 2 and batches == 2 and zones > 1 and sections > 1
    paired = paired and unit % 16 == 0 and half % 16 == 0 and inner % 16 == 0
    paired = paired and (2 * inner) % (16 * sections) == 0
    paired = paired and (2 * inner) % (8 * sections * zones) == 0
    paired = paired and zones & (zones - 1) == 0
    paired = paired and stem_weight.shape[1] % (16 * zones) == 0
    run = paired_body if paired else plain_body
    return run(bases, targets, stem_weight, conv_weight, proj_weight, head_weight)


def solution(mesh):
    in_specs = (
        P("dp", "seq", None),
        P("dp", "seq", "section"),
        P(),
        P("section", None, None, None),
        P("section", None, None),
        P(None, "section"),
    )
    out_specs = (P("section", None, None, None), P("section", None, None), P(None, "section"))
    return jax.shard_map(body, mesh=mesh, in_specs=in_specs, out_specs=out_specs, check_vma=False)
```

```python
import math

import jax
import jax.numpy as jnp
from jax import lax
from jax.experimental import pallas as pl
from jax.experimental.pallas import tpu as pltpu
from jax.sharding import PartitionSpec as P

SQRT_TWO_OVER_PI = 0.7978845608028654
CUBIC_TERM = 0.044715


def gelu_value(inputs):
    return (
        0.5
        * inputs
        * (1.0 + jnp.tanh(SQRT_TWO_OVER_PI * (inputs + CUBIC_TERM * inputs * inputs * inputs)))
    )


def gelu_slope(inputs):
    tangent = jnp.tanh(SQRT_TWO_OVER_PI * (inputs + CUBIC_TERM * inputs * inputs * inputs))
    return 0.5 * (1.0 + tangent) + 0.5 * inputs * (1.0 - tangent * tangent) * SQRT_TWO_OVER_PI * (
        1.0 + 3.0 * CUBIC_TERM * inputs * inputs
    )


def contract_rows(left_side, right_side):
    return lax.dot_general(
        left_side, right_side, (((0,), (0,)), ((), ())), preferred_element_type=jnp.float32
    )


def times_transposed(left_side, right_side):
    return lax.dot_general(
        left_side, right_side, (((1,), (1,)), ((), ())), preferred_element_type=jnp.float32
    )


def shift_rows(value, by):
    if abs(by) >= value.shape[0]:
        return jnp.zeros_like(value)
    pad = jnp.zeros((abs(by),) + value.shape[1:], value.dtype)
    if by > 0:
        return jnp.concatenate([pad, value[:-by]], 0)
    return jnp.concatenate([value[-by:], pad], 0)


MESH = pl.DeviceIdType.MESH
ANY = pl.BlockSpec(memory_space=pl.ANY)


def greet(peers):
    barrier = pltpu.get_barrier_semaphore()
    for peer in peers:
        pl.semaphore_signal(barrier, inc=1, device_id=peer, device_id_type=MESH)
    pl.semaphore_wait(barrier, len(peers))


def remote(src, dst, send, recv, peer):
    return pltpu.make_async_remote_copy(
        src_ref=src, dst_ref=dst, send_sem=send, recv_sem=recv, device_id=peer, device_id_type=MESH
    )


def both_gelu(inputs):
    square = inputs * inputs
    tangent = jnp.tanh(
        inputs * (SQRT_TWO_OVER_PI + (SQRT_TWO_OVER_PI * CUBIC_TERM) * square)
    )
    gate = 0.5 + 0.5 * tangent
    value = inputs * gate
    inside = 2.0 * SQRT_TWO_OVER_PI + (6.0 * SQRT_TWO_OVER_PI * CUBIC_TERM) * square
    return value, gate + value * (1.0 - gate) * inside


def tile_of(rows):
    for size in (512, 384, 256, 192, 128, 96, 64, 48, 32, 16):
        if rows % size == 0:
            return size
    return rows


def forward_tower(bases, stem, taps, proj, sections, unit):
    seqs, half, width = bases.shape
    length = seqs * half
    channels = stem.shape[1]
    inner = proj.shape[0]
    rows = taps.shape[0] + inner
    part = rows // 2
    tile = tile_of(half)
    steps = half // tile
    team = 3 if steps % 3 == 0 else 1
    shifts = [unit * 2**k for k in range(sections)]

    def kernel(*refs):
        bases_ref, stem_ref, taps_ref, proj_ref = refs[:4]
        refs = refs[4:]
        top_ref, weights_ref = refs[:2]
        hidden_out, slope_out = refs[2 : 2 + sections], refs[2 + sections : 1 + 2 * sections]
        refs = refs[1 + 2 * sections :]
        active_out, bend_out = refs[:sections], refs[sections : 2 * sections]
        refs = refs[2 * sections :]
        full, held, turned, state = refs[:4]
        refs = refs[4:]
        hidden, slope = refs[:sections], refs[sections : 2 * sections - 1]
        refs = refs[2 * sections - 1 :]
        active, bend = refs[:sections], refs[sections : 2 * sections]
        refs = refs[2 * sections :]
        bsend, brecv, send, recv, send2, recv2, tsend, trecv, own_sem, out_sem = refs

        s, c = lax.axis_index("section"), lax.axis_index("seq")
        partner = {"section": s, "seq": 1 - c}
        peers = [{"section": lax.rem(s + k, sections), "seq": c} for k in range(1, sections)]
        loads = [
            pltpu.make_async_copy(bases_ref.at[c], full.at[c], own_sem.at[0]),
            pltpu.make_async_copy(
                taps_ref, held.at[s, pl.ds(0, taps.shape[0])], own_sem.at[1]
            ),
            pltpu.make_async_copy(
                proj_ref, held.at[s, pl.ds(taps.shape[0], inner)], own_sem.at[2]
            ),
        ]
        for copy in loads:
            copy.start()
        greet(peers + [partner])
        across = remote(bases_ref.at[1 - c], full.at[c], bsend, brecv, partner)
        across.start()
        loads[1].wait()
        loads[2].wait()
        mine = held.at[s, pl.ds(pl.multiple_of(c * part, 16), part)]
        first = []
        for k, peer in enumerate(peers):
            first.append(remote(mine, mine, send.at[k], recv.at[k], peer))
            first[-1].start()
        for k in range(sections):
            edge = jnp.zeros((shifts[k], channels), jnp.bfloat16)
            hidden[k][pl.ds(0, shifts[k]), :] = edge
            hidden[k][pl.ds(shifts[k] + length, shifts[k]), :] = edge

        def begin(number):
            def step(i, carry):
                at = i * tile
                codes = full[number, pl.ds(pl.multiple_of(at, 16), tile), :]
                onehot = jnp.concatenate(
                    [(codes == k).astype(jnp.bfloat16) for k in range(4)], 1
                )
                start = jnp.dot(onehot, stem_ref[...], preferred_element_type=jnp.float32)
                start = start.astype(jnp.bfloat16)
                place = pl.multiple_of(number * half + at, 16)
                state[pl.ds(place, tile), :] = start
                value = gelu_value(start.astype(jnp.float32)).astype(jnp.bfloat16)
                hidden[0][pl.ds(pl.multiple_of(shifts[0] + place, 16), tile), :] = value
                return carry

            lax.fori_loop(0, steps, step, 0)

        loads[0].wait()
        begin(c)
        across.wait_recv()
        begin(1 - c)

        second = []
        for k in range(sections - 1):
            first[k].wait_recv()
            source = lax.rem(s + sections - 1 - k, sections)
            piece = held.at[source, pl.ds(pl.multiple_of(c * part, 16), part)]
            second.append(remote(piece, piece, send2.at[k], recv2.at[k], partner))
            second[-1].start()
        for copy in second:
            copy.wait_recv()

        outs = []

        def keep(src, dst):
            outs.append(pltpu.make_async_copy(src, dst, out_sem.at[len(outs)]))
            outs[-1].start()

        keep(held, weights_ref)
        keep(hidden[0].at[pl.ds(shifts[0], length)], hidden_out[0])

        for k in range(sections):
            by = shifts[k]
            for j in range(3):
                tap = held[k, pl.ds(j * inner, inner), :]
                turned[pl.ds(j * channels, channels), :] = tap.T

            def group(places, k=k, by=by):
                inners = []
                for place in places:
                    wide = jnp.concatenate(
                        [
                            hidden[k][pl.ds(pl.multiple_of(place + j * by, 16), tile), :]
                            for j in range(3)
                        ],
                        1,
                    )
                    inners.append(
                        jnp.dot(wide, turned[...], preferred_element_type=jnp.float32)
                    )
                olds = [state[pl.ds(place, tile), :].astype(jnp.float32) for place in places]
                results = []
                for inner_sum, old in zip(inners, olds):
                    value, bent = both_gelu(inner_sum)
                    value, bent = value.astype(jnp.bfloat16), bent.astype(jnp.bfloat16)
                    update = jnp.dot(
                        value,
                        held[k, pl.ds(3 * inner, inner), :],
                        preferred_element_type=jnp.float32,
                    )
                    results.append((value, bent, (old + update).astype(jnp.bfloat16)))
                for place, (value, bent, _) in zip(places, results):
                    active[k][pl.ds(place, tile), :] = value
                    bend[k][pl.ds(place, tile), :] = bent
                return [new for _, _, new in results]

            def spots(i, base):
                return [
                    pl.multiple_of(base + (i * team + g) * tile, 16) for g in range(team)
                ]

            if k < sections - 1:

                def step(i, carry, k=k):
                    places = spots(i, 0)
                    news = group(places)
                    pairs = [both_gelu(new.astype(jnp.float32)) for new in news]
                    for place, new, (value, bent) in zip(places, news, pairs):
                        state[pl.ds(place, tile), :] = new
                        ahead = pl.multiple_of(shifts[k + 1] + place, 16)
                        hidden[k + 1][pl.ds(ahead, tile), :] = value.astype(jnp.bfloat16)
                        slope[k][pl.ds(place, tile), :] = bent.astype(jnp.bfloat16)
                    return carry

                lax.fori_loop(0, length // (tile * team), step, 0)
                keep(hidden[k + 1].at[pl.ds(shifts[k + 1], length)], hidden_out[k + 1])
                keep(slope[k], slope_out[k])
            else:

                def finish_half(number):
                    def step(i, carry):
                        places = spots(i, number * half)
                        for place, new in zip(places, group(places)):
                            state[pl.ds(place, tile), :] = new
                        return carry

                    lax.fori_loop(0, steps // team, step, 0)

                finish_half(1 - c)
                theirs = state.at[pl.ds(pl.multiple_of((1 - c) * half, 16), half)]
                last = remote(theirs, top_ref.at[c], tsend, trecv, partner)
                last.start()
                finish_half(c)
                top_ref[c] = state[pl.ds(pl.multiple_of(c * half, 16), half), :]
            keep(active[k], active_out[k])
            keep(bend[k], bend_out[k])
        for copy in outs:
            copy.wait()
        last.wait()
        across.wait_send()
        for copy in first + second:
            copy.wait_send()

    bf16 = jnp.bfloat16
    long = jax.ShapeDtypeStruct((length, channels), bf16)
    thin = jax.ShapeDtypeStruct((length, inner), bf16)
    dma = pltpu.SemaphoreType.DMA
    copies = 4 * sections
    out = pl.pallas_call(
        kernel,
        out_shape=[
            jax.ShapeDtypeStruct((seqs, half, channels), bf16),
            jax.ShapeDtypeStruct((sections, rows, channels), bf16),
        ]
        + [long] * (2 * sections - 1)
        + [thin] * (2 * sections),
        in_specs=[ANY, pl.BlockSpec(memory_space=pltpu.VMEM), ANY, ANY],
        out_specs=[pl.BlockSpec(memory_space=pltpu.VMEM)] + [ANY] * (4 * sections),
        scratch_shapes=[
            pltpu.VMEM((seqs, half, width), jnp.int32),
            pltpu.VMEM((sections, rows, channels), bf16),
            pltpu.VMEM((3 * channels, inner), bf16),
            pltpu.VMEM((length, channels), bf16),
        ]
        + [pltpu.VMEM((length + 2 * by, channels), bf16) for by in shifts]
        + [pltpu.VMEM((length, channels), bf16)] * (sections - 1)
        + [pltpu.VMEM((length, inner), bf16)] * (2 * sections)
        + [dma, dma]
        + [dma((sections - 1,))] * 4
        + [dma, dma, dma((3,)), dma((copies,))],
        compiler_params=pltpu.CompilerParams(
            collective_id=0, has_side_effects=True, vmem_limit_bytes=54 * 2**20
        ),
        name="forward_tower",
    )(bases, stem, taps, proj)
    top, weights = out[:2]
    hidden, slope = out[2 : 2 + sections], out[2 + sections : 1 + 2 * sections]
    active = out[1 + 2 * sections : 1 + 3 * sections]
    bend = out[1 + 3 * sections :]
    return top, weights, hidden, slope, active, bend


def head(top, targets, head_weight, factor):
    seqs, half, channels = top.shape
    tracks = head_weight.shape[1]
    tile = tile_of(half)
    if half % 512 == 0:
        tile = 512
    steps = half // tile

    def kernel(
        top_ref, targets_ref, weight_ref, grad_ref, cot_ref, counts, stage, load, send, recv
    ):
        s, c = lax.axis_index("section"), lax.axis_index("seq")
        partner = {"section": s, "seq": 1 - c}
        loads = []
        for n, b in enumerate((1 - c, c)):
            for i in range(steps):
                loads.append(
                    pltpu.make_async_copy(
                        targets_ref.at[b, pl.ds(i * tile, tile)],
                        counts.at[n * steps + i],
                        load.at[n * steps + i],
                    )
                )
                loads[-1].start()
        greet([partner])
        grad_ref[...] = jnp.zeros_like(grad_ref)

        def run(b, n, store):
            def step(i, carry):
                at = pl.multiple_of(i * tile, 16)
                pltpu.make_async_copy(
                    targets_ref.at[b, pl.ds(at, tile)], counts.at[n + i], load.at[n + i]
                ).wait()
                value, bent = both_gelu(top_ref[b, pl.ds(at, tile), :].astype(jnp.float32))
                lifted = value.astype(jnp.bfloat16)
                logits = jnp.dot(lifted, weight_ref[...], preferred_element_type=jnp.float32)
                drop = jnp.exp(logits) - counts[n + i].astype(jnp.float32)
                drop = (drop * factor).astype(jnp.bfloat16)
                grad_ref[...] += contract_rows(lifted, drop)
                lift = times_transposed(drop, weight_ref[...])
                store(at, (lift * bent).astype(jnp.bfloat16))
                return carry

            lax.fori_loop(0, steps, step, 0)

        def away(at, value):
            stage[pl.ds(at, tile), :] = value

        def here(at, value):
            cot_ref[c, pl.ds(at, tile), :] = value

        run(1 - c, 0, away)
        copy = remote(stage, cot_ref.at[c], send, recv, partner)
        copy.start()
        run(c, steps, here)
        copy.wait()

    vmem = pl.BlockSpec(memory_space=pltpu.VMEM)
    dma = pltpu.SemaphoreType.DMA
    return pl.pallas_call(
        kernel,
        out_shape=[
            jax.ShapeDtypeStruct((channels, tracks), jnp.float32),
            jax.ShapeDtypeStruct(top.shape, jnp.bfloat16),
        ],
        in_specs=[vmem, ANY, vmem],
        out_specs=[vmem, vmem],
        scratch_shapes=[
            pltpu.VMEM((seqs * steps, tile, tracks), jnp.int32),
            pltpu.VMEM((half, channels), jnp.bfloat16),
            dma((seqs * steps,)),
            dma,
            dma,
        ],
        compiler_params=pltpu.CompilerParams(
            collective_id=1, has_side_effects=True, vmem_limit_bytes=48 * 2**20
        ),
        name="head",
    )(top, targets, head_weight)


def backward_tower(head_part, cot, weights, hidden, slope, active, bend, sections, zones, unit):
    length, channels = hidden[0].shape
    inner = active[0].shape[1]
    rows = weights.shape[1]
    part = rows // 2
    quarter = part // sections
    levels = zones.bit_length() - 1
    tracks = head_part.shape[1]
    side = head_part.shape[0] // 2
    tile = length // 2
    most = unit * 2 ** (sections - 1)
    f32, bf16 = jnp.float32, jnp.bfloat16

    def kernel(*refs):
        head_ref, cot_ref, weights_ref = refs[:3]
        refs = refs[3:]
        hidden_in, slope_in = refs[:sections], refs[sections : 2 * sections - 1]
        refs = refs[2 * sections - 1 :]
        active_in, bend_in = refs[:sections], refs[sections : 2 * sections]
        refs = refs[2 * sections :]
        out, head_out = refs[:2]
        hidden, slope, active, bend = refs[2:4], refs[4:6], refs[6:8], refs[8:10]
        held, grad, pull, sums, load = refs[10:15]
        met, wire, came, total, zcame, final = refs[15:21]
        hmet, hsum, hcame = refs[21:24]
        sems = refs[24:]

        s, c, d = (lax.axis_index(name) for name in ("section", "seq", "dp"))
        partner = {"section": s, "seq": 1 - c, "dp": d}
        order = [lax.rem(s + k, sections) for k in range(1, sections)]
        across = [{"section": o, "seq": c, "dp": d} for o in order]
        bits = [lax.rem(d // 2**t, 2) for t in range(levels)]
        along = [
            {"section": s, "seq": c, "dp": d + 2**t * (1 - 2 * bits[t])} for t in range(levels)
        ]
        count = [0]

        def fetch(src, dst):
            copy = pltpu.make_async_copy(src, dst, load.at[count[0]])
            count[0] += 1
            copy.start()
            return copy

        bring = {}

        def prefetch(k):
            slot = k % 2
            early = [
                fetch(weights_ref.at[k], held.at[k]),
                fetch(bend_in[k], bend[slot]),
                fetch(active_in[k], active[slot]),
            ]
            late = [fetch(hidden_in[k], hidden[slot])]
            if k:
                late.append(fetch(slope_in[k - 1], slope[slot]))
            bring[k] = (early, late)

        prefetch(sections - 1)
        greet([partner] + across + along)

        sends = []

        def launch(src, dst, pair, index, peer):
            copy = remote(src, dst, sems[2 * pair].at[index], sems[2 * pair + 1].at[index], peer)
            copy.start()
            sends.append(copy)
            return copy

        def block(base, size, number):
            return pl.ds(pl.multiple_of(base + number * size, 8), size)

        flight = {}

        def swap(k):
            far = sums.at[k, block(0, part, 1 - c)]
            flight[k] = [launch(far, met.at[k], 0, k, partner)]

        def spread(k):
            flight[k][0].wait_recv()
            flight[k] = []

            def both(o):
                return met[k, block(0, quarter, o), :] + sums[k, block(c * part, quarter, o), :]

            for n, o in enumerate(order):
                wire[k, n] = both(o).astype(bf16)
                flight[k].append(
                    launch(wire.at[k, n], came.at[k, n], 1, k * (sections - 1) + n, across[n])
                )
            total[k] = both(s)

        def kept(span, t):
            base = 0
            for step in range(t):
                base = base + bits[step] * (span >> (step + 1))
            return base

        def landing(span, t):
            return pl.ds(span - (span >> t), span >> (t + 1))

        def climb(k, t):
            for copy in flight[k]:
                copy.wait_recv()
            if t == 0:
                value = total[k]
                for n in range(sections - 1):
                    value = value + came[k, n].astype(f32)
                total[k] = value
            else:
                mine = block(kept(quarter, t), quarter >> t, 0)
                total[k, mine, :] = total[k, mine, :] + zcame[k, landing(quarter, t - 1), :]
            size = quarter >> (t + 1)
            away = block(kept(quarter, t), size, 1 - bits[t])
            flight[k] = [
                launch(
                    total.at[k, away],
                    zcame.at[k, landing(quarter, t)],
                    2,
                    k * levels + t,
                    along[t],
                )
            ]

        def level(k, t):
            for copy in flight[k]:
                copy.wait_recv()
            mine = block(kept(quarter, t + 1), quarter >> (t + 1), 0)
            if t == levels - 1:
                final[k, mine, :] = total[k, mine, :] + zcame[k, landing(quarter, t), :]
            piece = final.at[k, mine]
            flight[k] = [launch(piece, piece, 3, k * levels + t, along[t])]

        strip = quarter // zones
        floors = [lax.rem(d + n, zones) for n in range(1, zones)]
        lifts = [{"section": s, "seq": c, "dp": z} for z in floors]

        def climb_at_once():
            for copy in flight[0]:
                copy.wait_recv()
            value = total[0]
            for n in range(sections - 1):
                value = value + came[0, n].astype(f32)
            total[0] = value
            flight[0] = [
                launch(
                    total.at[0, block(0, strip, z)],
                    zcame.at[0, pl.ds(n * strip, strip)],
                    10,
                    n,
                    lifts[n],
                )
                for n, z in enumerate(floors)
            ]

        def level_at_once():
            for copy in flight[0]:
                copy.wait_recv()
            value = total[0, block(0, strip, d), :]
            for n in range(zones - 1):
                value = value + zcame[0, pl.ds(n * strip, strip), :]
            final[0, block(0, strip, d), :] = value
            piece = final.at[0, block(0, strip, d)]
            flight[0] = [launch(piece, piece, 11, n, peer) for n, peer in enumerate(lifts)]
            strip_home(d)

        def home_strip(z):
            owner = {"section": 0, "seq": c, "dp": d}
            index = lax.rem(s + sections - 1, sections) * zones + z
            place = out.at[block(c * part + s * quarter, strip, z)]
            return remote(
                final.at[0, block(0, strip, z)],
                place,
                sems[24].at[z],
                sems[25].at[index],
                owner,
            )

        def strip_home(z):
            @pl.when(s != 0)
            def _():
                home_strip(z).start()

        def deliver_strips():
            for n, copy in enumerate(flight[0]):
                copy.wait_recv()
                strip_home(lax.rem(d + zones - 1 - n, zones))

            @pl.when(s == 0)
            def _():
                out[block(c * part, quarter, s), :] = final[0]
                relay(0, s).start()

        def home(k):
            owner = {"section": k, "seq": c, "dp": d}
            index = lax.rem(s + 2 * sections - k - 1, sections)
            place = out.at[block(c * part, quarter, s)]
            return remote(final.at[k], place, sems[8].at[k], sems[9].at[index], owner)

        def deliver(k):
            for copy in flight[k]:
                copy.wait_recv()

            @pl.when(s != k)
            def _():
                home(k).start()

            @pl.when(s == k)
            def _():
                out[block(c * part, quarter, s), :] = final[k]
                relay(0, s).start()

        def relay(n, source):
            piece = out.at[block(c * part, quarter, source)]
            return remote(piece, piece, sems[10].at[n], sems[11].at[n], partner)

        def hand(k):
            @pl.when(s == k)
            def _():
                for n, o in enumerate(order):
                    if k:
                        piece = out.at[block(c * part, quarter, o)]
                        remote(
                            final.at[k], piece, sems[8].at[k], sems[9].at[n], across[n]
                        ).wait_recv()
                    else:
                        for z in range(zones):
                            piece = out.at[block(c * part + o * quarter, strip, z)]
                            remote(
                                final.at[0, block(0, strip, z)],
                                piece,
                                sems[24].at[z],
                                sems[25].at[n * zones + z],
                                across[n],
                            ).wait_recv()
                    relay(n + 1, o).start()

        def settle(k):
            @pl.when(s != k)
            def _():
                if k:
                    home(k).wait_send()
                else:
                    for z in range(zones):
                        home_strip(z).wait_send()

            @pl.when(s == k)
            def _():
                for n, o in enumerate([s] + order):
                    relay(n, o).wait()

        def head_swap():
            far = head_ref.at[block(0, side, 1 - c)]
            flight["h"] = [launch(far, hmet, 6, 0, partner)]

        def head_climb(t):
            flight["h"][0].wait_recv()
            if t == 0:
                hsum[...] = hmet[...] + head_ref[block(0, side, c), :]
            else:
                mine = block(kept(side, t), side >> t, 0)
                hsum[mine, :] = hsum[mine, :] + hcame[landing(side, t - 1), :]
            away = block(kept(side, t), side >> (t + 1), 1 - bits[t])
            flight["h"] = [
                launch(hsum.at[away], hcame.at[landing(side, t)], 7, t, along[t])
            ]

        flight["r"] = []

        def pass_on(start, size):
            piece = head_out.at[block(c * side + start, size, 0)]
            flight["r"].append(launch(piece, piece, 9, len(flight["r"]), partner))

        def other(span, t):
            return kept(span, t) + (1 - bits[t]) * (span >> (t + 1))

        def head_level(t):
            flight["h"][0].wait_recv()
            start, size = kept(side, t + 1), side >> (t + 1)
            place = block(c * side + start, size, 0)
            if t == levels - 1:
                mine = block(start, size, 0)
                head_out[place, :] = hsum[mine, :] + hcame[landing(side, t), :]
                pass_on(start, size)
            else:
                pass_on(other(side, t + 1), side >> (t + 2))
            piece = head_out.at[place]
            flight["h"] = [launch(piece, piece, 8, t, along[t])]

        def head_hand():
            flight["h"][0].wait_recv()
            pass_on(other(side, 0), side // 2)

        head_swap()
        pull[pl.ds(0, most), :] = jnp.zeros((most, inner), bf16)
        pull[pl.ds(most + length, most), :] = jnp.zeros((most, inner), bf16)
        sums[...] = jnp.zeros_like(sums)

        top = sections - 1
        stages = {}
        for k in range(sections):
            line = [lambda k=k: swap(k), lambda k=k: spread(k)]
            if k:
                line += [lambda k=k, t=t: climb(k, t) for t in range(levels)]
                line += [lambda k=k, t=t: level(k, t) for t in reversed(range(levels))]
                line.append(lambda k=k: deliver(k))
            else:
                line += [climb_at_once, level_at_once, deliver_strips]
            stages[k] = line + [lambda k=k: hand(k)]
        line = [lambda t=t: head_climb(t) for t in range(levels)]
        line += [lambda t=t: head_level(t) for t in reversed(range(levels))]
        stages["h"] = line + [head_hand]
        marks = {}

        def plan(name, ticks):
            for at in ticks:
                if at <= 3 * sections - 1 and stages[name]:
                    marks.setdefault(at, []).append(stages[name].pop(0))

        for k in range(sections):
            plan(k, [3 * (top - k) + 2 + gap for gap in (0, 2, 3, 6, 9)])
        plan("h", (1, 5, 10))
        clock = [0]

        def tick():
            for stage in marks.get(clock[0], []):
                stage()
            clock[0] += 1

        for k in reversed(range(sections)):
            by = unit * 2**k
            slot = k % 2
            above = cot_ref if k == top else grad
            if k:
                prefetch(k - 1)
            for copy in bring[k][0]:
                copy.wait()

            def inward(i, k=k, slot=slot, above=above):
                place = i * tile
                here = above[pl.ds(place, tile), :]
                back = times_transposed(here, held[k, pl.ds(3 * inner, inner), :])
                back = back * bend[slot][pl.ds(place, tile), :].astype(f32)
                pull[pl.ds(most + place, tile), :] = back.astype(bf16)
                sums[k, pl.ds(3 * inner, inner), :] += contract_rows(
                    active[slot][pl.ds(place, tile), :], here
                )

            for i in range(length // tile):
                inward(i)
                tick()
            for copy in bring[k][1]:
                copy.wait()

            def outward(i, carry, k=k, by=by, slot=slot, above=above):
                place = pl.multiple_of(i * tile, 16)
                there = hidden[slot][pl.ds(place, tile), :]
                value = None
                for j in range(3):
                    piece = pull[pl.ds(pl.multiple_of(most + place + (1 - j) * by, 16), tile), :]
                    span = pl.ds(j * inner, inner)
                    sums[k, span, :] += contract_rows(piece, there)
                    if k:
                        term = jnp.dot(piece, held[k, span, :], preferred_element_type=f32)
                        value = term if value is None else value + term
                if k:
                    value = value * slope[slot][pl.ds(place, tile), :].astype(f32)
                    value = value + above[pl.ds(place, tile), :].astype(f32)
                    grad[pl.ds(place, tile), :] = value.astype(bf16)
                return carry

            lax.fori_loop(0, length // tile, outward, 0)
            tick()

        rounds = 0
        while any(stages.values()):
            for name in [*reversed(range(2, sections)), 0, 1, "h"]:
                if stages[name] and (name != "h" or rounds > 1):
                    stages[name].pop(0)()
            rounds += 1
        for copy in flight["r"]:
            copy.wait_recv()
        for k in range(sections):
            settle(k)
        for copy in sends:
            copy.wait_send()

    dma = pltpu.SemaphoreType.DMA

    def pair(count):
        return [dma((count,))] * 2

    long, thin = pltpu.VMEM((length, channels), bf16), pltpu.VMEM((length, inner), bf16)
    vmem = pl.BlockSpec(memory_space=pltpu.VMEM)
    return pl.pallas_call(
        kernel,
        out_shape=[
            jax.ShapeDtypeStruct((rows, channels), f32),
            jax.ShapeDtypeStruct(head_part.shape, f32),
        ],
        in_specs=[vmem, vmem] + [ANY] * (4 * sections),
        out_specs=[vmem, vmem],
        scratch_shapes=[long] * 4
        + [thin] * 4
        + [
            pltpu.VMEM(weights.shape, bf16),
            long,
            pltpu.VMEM((length + 2 * most, inner), bf16),
            pltpu.VMEM((sections, rows, channels), f32),
            dma((5 * sections,)),
            pltpu.VMEM((sections, part, channels), f32),
            pltpu.VMEM((sections, sections - 1, quarter, channels), bf16),
            pltpu.VMEM((sections, sections - 1, quarter, channels), bf16),
            pltpu.VMEM((sections, quarter, channels), f32),
            pltpu.VMEM((sections, quarter, channels), f32),
            pltpu.VMEM((sections, quarter, channels), f32),
            pltpu.VMEM((side, tracks), f32),
            pltpu.VMEM((side, tracks), f32),
            pltpu.VMEM((side, tracks), f32),
        ]
        + pair(sections)
        + pair(sections * (sections - 1))
        + pair(sections * levels)
        + pair(sections * levels)
        + [dma((sections,)), dma((sections,))]
        + pair(sections)
        + pair(1)
        + pair(levels)
        + pair(levels)
        + pair(levels + 1)
        + pair(zones - 1)
        + pair(zones - 1)
        + [dma((zones,)), dma((sections * zones,))],
        compiler_params=pltpu.CompilerParams(
            collective_id=2, has_side_effects=True, vmem_limit_bytes=48 * 2**20
        ),
        name="backward_tower",
    )(head_part, cot, weights, *hidden, *slope, *active, *bend)


def finish(total, head_sum, split):
    def kernel(total_ref, head_ref, conv_out, proj_out, head_out, sems):
        copies = [
            pltpu.make_async_copy(total_ref.at[pl.ds(0, split)], conv_out, sems.at[0]),
            pltpu.make_async_copy(
                total_ref.at[pl.ds(split, total.shape[0] - split)], proj_out, sems.at[1]
            ),
            pltpu.make_async_copy(head_ref, head_out, sems.at[2]),
        ]
        for copy in copies:
            copy.start()
        for copy in copies:
            copy.wait()

    width = total.shape[1]
    return pl.pallas_call(
        kernel,
        out_shape=[
            jax.ShapeDtypeStruct((split, width), total.dtype),
            jax.ShapeDtypeStruct((total.shape[0] - split, width), total.dtype),
            jax.ShapeDtypeStruct(head_sum.shape, head_sum.dtype),
        ],
        in_specs=[pl.BlockSpec(memory_space=pltpu.VMEM)] * 2,
        out_specs=[ANY] * 3,
        scratch_shapes=[pltpu.SemaphoreType.DMA((3,))],
        compiler_params=pltpu.CompilerParams(vmem_limit_bytes=8 * 2**20),
        name="finish",
    )(total, head_sum)


def plain_body(bases, targets, stem_weight, conv_weight, proj_weight, head_weight):
    sections = lax.axis_size("section")
    seqs = lax.axis_size("seq")
    section_number = lax.axis_index("section")
    batches, row_count, bin_width = bases.shape
    channels = stem_weight.shape[1]
    length = row_count * seqs
    factor = 1.0 / math.sqrt(batches * lax.axis_size("dp") * length)
    unit = length // 2**sections
    local_q = row_count // unit
    blocks = length // unit
    columns = batches * unit // (seqs * sections)

    conv_all = lax.all_gather(conv_weight, "section", axis=0, tiled=True)
    proj_all = lax.all_gather(proj_weight, "section", axis=0, tiled=True)

    def to_chains(value):
        value = lax.all_to_all(value, "seq", split_axis=1, concat_axis=0, tiled=True)
        return value.reshape(blocks * columns, value.shape[-1])

    own = bases.reshape(batches, local_q, unit, bin_width).transpose(1, 0, 2, 3)
    own = own.reshape(local_q, seqs, sections, columns, bin_width)
    own = lax.dynamic_index_in_dim(own, section_number, 2, keepdims=False)
    picked = to_chains(own.astype(jnp.bfloat16))
    onehot = jnp.concatenate([(picked == c).astype(jnp.bfloat16) for c in range(4)], 1)
    stem = stem_weight.reshape(bin_width, 4, channels).transpose(1, 0, 2).reshape(-1, channels)
    state = jnp.dot(onehot, stem, preferred_element_type=jnp.float32).astype(jnp.bfloat16)

    saved = []
    for layer in range(sections):
        by = columns * 2**layer
        taps = conv_all[layer].reshape(-1, conv_all.shape[-1])
        hidden = gelu_value(state.astype(jnp.float32)).astype(jnp.bfloat16)
        wide = jnp.concatenate([shift_rows(hidden, by), hidden, shift_rows(hidden, -by)], 1)
        inner_sum = jnp.dot(wide, taps, preferred_element_type=jnp.float32)
        active = gelu_value(inner_sum).astype(jnp.bfloat16)
        update = jnp.dot(active, proj_all[layer], preferred_element_type=jnp.float32)
        saved.append((state, wide, inner_sum, active))
        state = (state.astype(jnp.float32) + update).astype(jnp.bfloat16)

    lifted = gelu_value(state.astype(jnp.float32)).astype(jnp.bfloat16)
    lifted = lifted.reshape(seqs, local_q, 1, columns, channels)
    lifted = lax.all_to_all(lifted, "seq", split_axis=0, concat_axis=2, tiled=True)
    lifted = lifted.reshape(local_q, seqs, 1, columns, channels)
    lifted = lax.all_gather(lifted, "section", axis=2, tiled=True)
    lifted = lifted.reshape(local_q, batches, unit, channels).transpose(1, 0, 2, 3)
    lifted = lifted.reshape(batches * row_count, channels)

    logits = jnp.dot(lifted, head_weight, preferred_element_type=jnp.float32)
    counts = targets.reshape(batches * row_count, targets.shape[2]).astype(jnp.float32)
    slope = ((jnp.exp(logits) - counts) * factor).astype(jnp.bfloat16)
    head_sum = lax.psum(contract_rows(lifted, slope), ("seq", "dp"))
    lift_part = times_transposed(slope, head_weight)

    lift_part = lift_part.reshape(batches, local_q, unit, channels).transpose(1, 0, 2, 3)
    lift_part = lift_part.reshape(local_q, seqs, sections, columns, channels)
    lift_part = lax.psum_scatter(lift_part, "section", scatter_dimension=2, tiled=True)
    lift_grad = to_chains(lift_part.reshape(local_q, seqs, columns, channels))


    grad = (lift_grad * gelu_slope(state.astype(jnp.float32))).astype(jnp.bfloat16)
    parts = []
    for layer in reversed(range(sections)):
        by = columns * 2**layer
        start_state, wide, inner_sum, active = saved[layer]
        kernel = conv_all[layer]
        proj_part = contract_rows(active, grad)
        active_grad = times_transposed(grad, proj_all[layer])
        inner_grad = (active_grad * gelu_slope(inner_sum)).astype(jnp.bfloat16)
        parts.append(jnp.concatenate([contract_rows(inner_grad, wide), proj_part], 1))
        wide_grad = jnp.concatenate(
            [shift_rows(inner_grad, -by), inner_grad, shift_rows(inner_grad, by)], 1
        )
        turned = kernel.transpose(0, 2, 1).reshape(-1, channels)
        hidden_grad = jnp.dot(wide_grad, turned, preferred_element_type=jnp.float32)
        grad = (
            grad.astype(jnp.float32) + hidden_grad * gelu_slope(start_state.astype(jnp.float32))
        ).astype(jnp.bfloat16)
    parts = jnp.stack(parts[::-1])
    total = lax.psum_scatter(parts, "section", scatter_dimension=0, tiled=True)
    total = lax.psum(total[0], ("seq", "dp"))
    taps_width = total.shape[1] - channels
    conv_sum = total[:, :taps_width].T.reshape(conv_weight.shape)
    return conv_sum, total[:, taps_width:][None], head_sum


def paired_body(bases, targets, stem_weight, conv_weight, proj_weight, head_weight):
    sections = lax.axis_size("section")
    zones = lax.axis_size("dp")
    batches, half, bin_width = bases.shape
    channels = stem_weight.shape[1]
    inner = proj_weight.shape[1]
    length = batches * half
    unit = length // 2**sections
    factor = 1.0 / math.sqrt(batches * zones * length)
    stem = stem_weight.reshape(bin_width, 4, channels).transpose(1, 0, 2).reshape(-1, channels)
    taps = conv_weight[0].transpose(0, 2, 1).reshape(3 * inner, channels)
    top, weights, hidden, slope, active, bend = forward_tower(
        bases, stem, taps, proj_weight[0], sections, unit
    )
    head_part, cot = head(top, targets, head_weight, factor)
    cot = cot.reshape(length, channels)
    total, head_sum = backward_tower(
        head_part, cot, weights, hidden, slope, active, bend, sections, zones, unit
    )
    conv_sum, proj_sum, head_sum = finish(total, head_sum, 3 * inner)
    conv_sum = conv_sum.reshape(3, inner, channels).transpose(0, 2, 1)
    return conv_sum[None], proj_sum[None], head_sum


def body(bases, targets, stem_weight, conv_weight, proj_weight, head_weight):
    sections, zones = lax.axis_size("section"), lax.axis_size("dp")
    batches, half = bases.shape[:2]
    inner = proj_weight.shape[1]
    unit = batches * half // 2**sections
    paired = lax.axis_size("seq") == 2 and batches == 2 and zones > 1 and sections > 1
    paired = paired and unit % 16 == 0 and half % 16 == 0 and inner % 16 == 0
    paired = paired and (2 * inner) % (16 * sections) == 0
    paired = paired and (2 * inner) % (8 * sections * zones) == 0
    paired = paired and zones & (zones - 1) == 0
    paired = paired and stem_weight.shape[1] % (16 * zones) == 0
    run = paired_body if paired else plain_body
    return run(bases, targets, stem_weight, conv_weight, proj_weight, head_weight)


def solution(mesh):
    in_specs = (
        P("dp", "seq", None),
        P("dp", "seq", "section"),
        P(),
        P("section", None, None, None),
        P("section", None, None),
        P(None, "section"),
    )
    out_specs = (P("section", None, None, None), P("section", None, None), P(None, "section"))
    return jax.shard_map(body, mesh=mesh, in_specs=in_specs, out_specs=out_specs, check_vma=False)
```

```python
import math

import jax
import jax.numpy as jnp
from jax import lax
from jax.experimental import pallas as pl
from jax.experimental.pallas import tpu as pltpu
from jax.sharding import PartitionSpec as P

SQRT_TWO_OVER_PI = 0.7978845608028654
CUBIC_TERM = 0.044715


def gelu_value(inputs):
    return (
        0.5
        * inputs
        * (1.0 + jnp.tanh(SQRT_TWO_OVER_PI * (inputs + CUBIC_TERM * inputs * inputs * inputs)))
    )


def gelu_slope(inputs):
    tangent = jnp.tanh(SQRT_TWO_OVER_PI * (inputs + CUBIC_TERM * inputs * inputs * inputs))
    return 0.5 * (1.0 + tangent) + 0.5 * inputs * (1.0 - tangent * tangent) * SQRT_TWO_OVER_PI * (
        1.0 + 3.0 * CUBIC_TERM * inputs * inputs
    )


def contract_rows(left_side, right_side):
    return lax.dot_general(
        left_side, right_side, (((0,), (0,)), ((), ())), preferred_element_type=jnp.float32
    )


def times_transposed(left_side, right_side):
    return lax.dot_general(
        left_side, right_side, (((1,), (1,)), ((), ())), preferred_element_type=jnp.float32
    )


def shift_rows(value, by):
    if abs(by) >= value.shape[0]:
        return jnp.zeros_like(value)
    pad = jnp.zeros((abs(by),) + value.shape[1:], value.dtype)
    if by > 0:
        return jnp.concatenate([pad, value[:-by]], 0)
    return jnp.concatenate([value[-by:], pad], 0)


MESH = pl.DeviceIdType.MESH
ANY = pl.BlockSpec(memory_space=pl.ANY)


def greet(peers):
    barrier = pltpu.get_barrier_semaphore()
    for peer in peers:
        pl.semaphore_signal(barrier, inc=1, device_id=peer, device_id_type=MESH)
    pl.semaphore_wait(barrier, len(peers))


def remote(src, dst, send, recv, peer):
    return pltpu.make_async_remote_copy(
        src_ref=src, dst_ref=dst, send_sem=send, recv_sem=recv, device_id=peer, device_id_type=MESH
    )


def both_gelu(inputs):
    square = inputs * inputs
    tangent = jnp.tanh(
        inputs * (SQRT_TWO_OVER_PI + (SQRT_TWO_OVER_PI * CUBIC_TERM) * square)
    )
    gate = 0.5 + 0.5 * tangent
    value = inputs * gate
    inside = 2.0 * SQRT_TWO_OVER_PI + (6.0 * SQRT_TWO_OVER_PI * CUBIC_TERM) * square
    return value, gate + value * (1.0 - gate) * inside


def tile_of(rows):
    for size in (512, 384, 256, 192, 128, 96, 64, 48, 32, 16):
        if rows % size == 0:
            return size
    return rows


def forward_tower(bases, stem, taps, proj, sections, unit):
    seqs, half, width = bases.shape
    length = seqs * half
    channels = stem.shape[1]
    inner = proj.shape[0]
    rows = taps.shape[0] + inner
    part = rows // 2
    tile = tile_of(half)
    steps = half // tile
    team = 3 if steps % 3 == 0 else 1
    shifts = [unit * 2**k for k in range(sections)]

    def kernel(*refs):
        bases_ref, stem_ref, taps_ref, proj_ref = refs[:4]
        refs = refs[4:]
        top_ref, weights_ref = refs[:2]
        hidden_out, slope_out = refs[2 : 2 + sections], refs[2 + sections : 1 + 2 * sections]
        refs = refs[1 + 2 * sections :]
        active_out, bend_out = refs[:sections], refs[sections : 2 * sections]
        refs = refs[2 * sections :]
        full, held, turned, state, sorted_stem = refs[:5]
        refs = refs[5:]
        hidden, slope = refs[:sections], refs[sections : 2 * sections - 1]
        refs = refs[2 * sections - 1 :]
        active, bend = refs[:sections], refs[sections : 2 * sections]
        refs = refs[2 * sections :]
        bsend, brecv, send, recv, send2, recv2, tsend, trecv, own_sem, out_sem = refs

        s, c = lax.axis_index("section"), lax.axis_index("seq")
        partner = {"section": s, "seq": 1 - c}
        peers = [{"section": lax.rem(s + k, sections), "seq": c} for k in range(1, sections)]
        loads = [
            pltpu.make_async_copy(bases_ref.at[c], full.at[c], own_sem.at[0]),
            pltpu.make_async_copy(
                taps_ref, held.at[s, pl.ds(0, taps.shape[0])], own_sem.at[1]
            ),
            pltpu.make_async_copy(
                proj_ref, held.at[s, pl.ds(taps.shape[0], inner)], own_sem.at[2]
            ),
        ]
        for copy in loads:
            copy.start()
        greet(peers + [partner])
        across = remote(bases_ref.at[1 - c], full.at[c], bsend, brecv, partner)
        across.start()
        loads[1].wait()
        loads[2].wait()
        mine = held.at[s, pl.ds(pl.multiple_of(c * part, 16), part)]
        first = []
        for k, peer in enumerate(peers):
            first.append(remote(mine, mine, send.at[k], recv.at[k], peer))
            first[-1].start()
        for k in range(sections - 1):
            edge = jnp.zeros((shifts[k], channels), jnp.bfloat16)
            hidden[k][pl.ds(0, shifts[k]), :] = edge
            hidden[k][pl.ds(shifts[k] + length, shifts[k]), :] = edge

        across_rows = lax.broadcasted_iota(jnp.int32, (4 * width, 4 * width), 0)
        across_columns = lax.broadcasted_iota(jnp.int32, (4 * width, 4 * width), 1)
        place_of = 4 * lax.rem(across_rows, width) + across_rows // width
        chosen = (across_columns == place_of).astype(jnp.bfloat16)
        sorted_stem[...] = jnp.dot(
            chosen, stem_ref[...], preferred_element_type=jnp.float32
        ).astype(jnp.bfloat16)

        def begin(number):
            def step(i, carry):
                at = i * tile
                codes = full[number, pl.ds(pl.multiple_of(at, 16), tile), :]
                onehot = jnp.concatenate(
                    [(codes == k).astype(jnp.bfloat16) for k in range(4)], 1
                )
                start = jnp.dot(onehot, sorted_stem[...], preferred_element_type=jnp.float32)
                start = start.astype(jnp.bfloat16)
                place = pl.multiple_of(number * half + at, 16)
                state[pl.ds(place, tile), :] = start
                value = gelu_value(start.astype(jnp.float32)).astype(jnp.bfloat16)
                hidden[0][pl.ds(pl.multiple_of(shifts[0] + place, 16), tile), :] = value
                return carry

            lax.fori_loop(0, steps, step, 0)

        loads[0].wait()
        begin(c)
        across.wait_recv()
        begin(1 - c)

        second = []
        for k in range(sections - 1):
            first[k].wait_recv()
            source = lax.rem(s + sections - 1 - k, sections)
            piece = held.at[source, pl.ds(pl.multiple_of(c * part, 16), part)]
            second.append(remote(piece, piece, send2.at[k], recv2.at[k], partner))
            second[-1].start()
        for copy in second:
            copy.wait_recv()

        outs = []

        def keep(src, dst):
            outs.append(pltpu.make_async_copy(src, dst, out_sem.at[len(outs)]))
            outs[-1].start()

        keep(held, weights_ref)
        keep(hidden[0].at[pl.ds(shifts[0], length)], hidden_out[0])

        for k in range(sections):
            by = shifts[k]
            for j in range(3):
                tap = held[k, pl.ds(j * inner, inner), :]
                turned[pl.ds(j * channels, channels), :] = tap.T

            def group(places, lead, width, k=k, by=by):
                weight = turned[pl.ds(pl.multiple_of(lead * channels, 16), width * channels), :]
                inners = []
                for place in places:
                    wide = jnp.concatenate(
                        [
                            hidden[k][pl.ds(pl.multiple_of(place + (lead + j) * by, 16), tile), :]
                            for j in range(width)
                        ],
                        1,
                    )
                    inners.append(
                        jnp.dot(wide, weight, preferred_element_type=jnp.float32)
                    )
                olds = [state[pl.ds(place, tile), :].astype(jnp.float32) for place in places]
                results = []
                for inner_sum, old in zip(inners, olds):
                    value, bent = both_gelu(inner_sum)
                    value, bent = value.astype(jnp.bfloat16), bent.astype(jnp.bfloat16)
                    update = jnp.dot(
                        value,
                        held[k, pl.ds(3 * inner, inner), :],
                        preferred_element_type=jnp.float32,
                    )
                    results.append((value, bent, (old + update).astype(jnp.bfloat16)))
                for place, (value, bent, _) in zip(places, results):
                    active[k][pl.ds(place, tile), :] = value
                    bend[k][pl.ds(place, tile), :] = bent
                return [new for _, _, new in results]

            def spots(i, base):
                return [
                    pl.multiple_of(base + (i * team + g) * tile, 16) for g in range(team)
                ]

            if k < sections - 1:

                def step(i, carry, k=k):
                    places = spots(i, 0)
                    news = group(places, 0, 3)
                    pairs = [both_gelu(new.astype(jnp.float32)) for new in news]
                    for place, new, (value, bent) in zip(places, news, pairs):
                        state[pl.ds(place, tile), :] = new
                        ahead = pl.multiple_of(shifts[k + 1] + place, 16)
                        hidden[k + 1][pl.ds(ahead, tile), :] = value.astype(jnp.bfloat16)
                        slope[k][pl.ds(place, tile), :] = bent.astype(jnp.bfloat16)
                    return carry

                lax.fori_loop(0, length // (tile * team), step, 0)
                keep(hidden[k + 1].at[pl.ds(shifts[k + 1], length)], hidden_out[k + 1])
                keep(slope[k], slope_out[k])
            else:

                def finish_half(number):
                    def step(i, carry):
                        places = spots(i, number * half)
                        for place, new in zip(places, group(places, 1 - number, 2)):
                            state[pl.ds(place, tile), :] = new
                        return carry

                    lax.fori_loop(0, steps // team, step, 0)

                finish_half(1 - c)
                theirs = state.at[pl.ds(pl.multiple_of((1 - c) * half, 16), half)]
                last = remote(theirs, top_ref.at[c], tsend, trecv, partner)
                last.start()
                finish_half(c)
                top_ref[c] = state[pl.ds(pl.multiple_of(c * half, 16), half), :]
            keep(active[k], active_out[k])
            keep(bend[k], bend_out[k])
        for copy in outs:
            copy.wait()
        last.wait()
        across.wait_send()
        for copy in first + second:
            copy.wait_send()

    bf16 = jnp.bfloat16
    long = jax.ShapeDtypeStruct((length, channels), bf16)
    thin = jax.ShapeDtypeStruct((length, inner), bf16)
    dma = pltpu.SemaphoreType.DMA
    copies = 4 * sections
    out = pl.pallas_call(
        kernel,
        out_shape=[
            jax.ShapeDtypeStruct((seqs, half, channels), bf16),
            jax.ShapeDtypeStruct((sections, rows, channels), bf16),
        ]
        + [long] * (2 * sections - 1)
        + [thin] * (2 * sections),
        in_specs=[ANY, pl.BlockSpec(memory_space=pltpu.VMEM), ANY, ANY],
        out_specs=[pl.BlockSpec(memory_space=pltpu.VMEM)] + [ANY] * (4 * sections),
        scratch_shapes=[
            pltpu.VMEM((seqs, half, width), jnp.int32),
            pltpu.VMEM((sections, rows, channels), bf16),
            pltpu.VMEM((3 * channels, inner), bf16),
            pltpu.VMEM((length, channels), bf16),
            pltpu.VMEM(stem.shape, bf16),
        ]
        + [pltpu.VMEM((length + 2 * by, channels), bf16) for by in shifts]
        + [pltpu.VMEM((length, channels), bf16)] * (sections - 1)
        + [pltpu.VMEM((length, inner), bf16)] * (2 * sections)
        + [dma, dma]
        + [dma((sections - 1,))] * 4
        + [dma, dma, dma((3,)), dma((copies,))],
        compiler_params=pltpu.CompilerParams(
            collective_id=0, has_side_effects=True, vmem_limit_bytes=54 * 2**20
        ),
        name="forward_tower",
    )(bases, stem, taps, proj)
    top, weights = out[:2]
    hidden, slope = out[2 : 2 + sections], out[2 + sections : 1 + 2 * sections]
    active = out[1 + 2 * sections : 1 + 3 * sections]
    bend = out[1 + 3 * sections :]
    return top, weights, hidden, slope, active, bend


def head(top, targets, head_weight, factor):
    seqs, half, channels = top.shape
    tracks = head_weight.shape[1]
    tile = tile_of(half)
    if half % 512 == 0:
        tile = 512
    steps = half // tile

    def kernel(
        top_ref, targets_ref, weight_ref, grad_ref, cot_ref, counts, stage, load, send, recv
    ):
        s, c = lax.axis_index("section"), lax.axis_index("seq")
        partner = {"section": s, "seq": 1 - c}
        loads = []
        for n, b in enumerate((1 - c, c)):
            for i in range(steps):
                loads.append(
                    pltpu.make_async_copy(
                        targets_ref.at[b, pl.ds(i * tile, tile)],
                        counts.at[n * steps + i],
                        load.at[n * steps + i],
                    )
                )
                loads[-1].start()
        greet([partner])
        grad_ref[...] = jnp.zeros_like(grad_ref)

        def run(b, n, store):
            def step(i, carry):
                at = pl.multiple_of(i * tile, 16)
                pltpu.make_async_copy(
                    targets_ref.at[b, pl.ds(at, tile)], counts.at[n + i], load.at[n + i]
                ).wait()
                value, bent = both_gelu(top_ref[b, pl.ds(at, tile), :].astype(jnp.float32))
                lifted = value.astype(jnp.bfloat16)
                logits = jnp.dot(lifted, weight_ref[...], preferred_element_type=jnp.float32)
                drop = jnp.exp(logits) - counts[n + i].astype(jnp.float32)
                drop = (drop * factor).astype(jnp.bfloat16)
                grad_ref[...] += contract_rows(lifted, drop)
                lift = times_transposed(drop, weight_ref[...])
                store(at, (lift * bent).astype(jnp.bfloat16))
                return carry

            lax.fori_loop(0, steps, step, 0)

        def away(at, value):
            stage[pl.ds(at, tile), :] = value

        def here(at, value):
            cot_ref[c, pl.ds(at, tile), :] = value

        run(1 - c, 0, away)
        copy = remote(stage, cot_ref.at[c], send, recv, partner)
        copy.start()
        run(c, steps, here)
        copy.wait()

    vmem = pl.BlockSpec(memory_space=pltpu.VMEM)
    dma = pltpu.SemaphoreType.DMA
    return pl.pallas_call(
        kernel,
        out_shape=[
            jax.ShapeDtypeStruct((channels, tracks), jnp.float32),
            jax.ShapeDtypeStruct(top.shape, jnp.bfloat16),
        ],
        in_specs=[vmem, ANY, vmem],
        out_specs=[vmem, vmem],
        scratch_shapes=[
            pltpu.VMEM((seqs * steps, tile, tracks), jnp.int32),
            pltpu.VMEM((half, channels), jnp.bfloat16),
            dma((seqs * steps,)),
            dma,
            dma,
        ],
        compiler_params=pltpu.CompilerParams(
            collective_id=1, has_side_effects=True, vmem_limit_bytes=48 * 2**20
        ),
        name="head",
    )(top, targets, head_weight)


def backward_tower(head_part, cot, weights, hidden, slope, active, bend, sections, zones, unit):
    length, channels = hidden[0].shape
    inner = active[0].shape[1]
    rows = weights.shape[1]
    part = rows // 2
    quarter = part // sections
    levels = zones.bit_length() - 1
    tracks = head_part.shape[1]
    side = head_part.shape[0] // 2
    tile = length // 2
    most = unit * 2 ** (sections - 1)
    f32, bf16 = jnp.float32, jnp.bfloat16

    def kernel(*refs):
        head_ref, cot_ref, weights_ref = refs[:3]
        refs = refs[3:]
        hidden_in, slope_in = refs[:sections], refs[sections : 2 * sections - 1]
        refs = refs[2 * sections - 1 :]
        active_in, bend_in = refs[:sections], refs[sections : 2 * sections]
        refs = refs[2 * sections :]
        out, head_out = refs[:2]
        hidden, slope, active, bend = refs[2:4], refs[4:6], refs[6:8], refs[8:10]
        held, grad, pull, sums, load = refs[10:15]
        met, wire, came, total, zcame, final = refs[15:21]
        hmet, hsum, hcame = refs[21:24]
        sems = refs[24:]

        s, c, d = (lax.axis_index(name) for name in ("section", "seq", "dp"))
        partner = {"section": s, "seq": 1 - c, "dp": d}
        order = [lax.rem(s + k, sections) for k in range(1, sections)]
        across = [{"section": o, "seq": c, "dp": d} for o in order]
        bits = [lax.rem(d // 2**t, 2) for t in range(levels)]
        along = [
            {"section": s, "seq": c, "dp": d + 2**t * (1 - 2 * bits[t])} for t in range(levels)
        ]
        floors = [lax.rem(d + n, zones) for n in range(1, zones)]
        lifts = [{"section": s, "seq": c, "dp": z} for z in floors]
        count = [0]

        def fetch(src, dst):
            copy = pltpu.make_async_copy(src, dst, load.at[count[0]])
            count[0] += 1
            copy.start()
            return copy

        bring = {}

        def prefetch(k):
            slot = k % 2
            early = [
                fetch(weights_ref.at[k], held.at[k]),
                fetch(bend_in[k], bend[slot]),
                fetch(active_in[k], active[slot]),
            ]
            late = [fetch(hidden_in[k], hidden[slot])]
            if k:
                late.append(fetch(slope_in[k - 1], slope[slot]))
            bring[k] = (early, late)

        prefetch(sections - 1)
        greet([partner] + across + lifts)

        sends = []

        def launch(src, dst, pair, index, peer):
            copy = remote(src, dst, sems[2 * pair].at[index], sems[2 * pair + 1].at[index], peer)
            copy.start()
            sends.append(copy)
            return copy

        def block(base, size, number):
            return pl.ds(pl.multiple_of(base + number * size, 8), size)

        flight = {}

        def swap(k):
            far = sums.at[k, block(0, part, 1 - c)]
            flight[k] = [launch(far, met.at[k], 0, k, partner)]

        def spread(k):
            flight[k][0].wait_recv()
            flight[k] = []

            def both(o):
                return met[k, block(0, quarter, o), :] + sums[k, block(c * part, quarter, o), :]

            for n, o in enumerate(order):
                wire[k, n] = both(o).astype(bf16)
                flight[k].append(
                    launch(wire.at[k, n], came.at[k, n], 1, k * (sections - 1) + n, across[n])
                )
            total[k] = both(s)

        def kept(span, t):
            base = 0
            for step in range(t):
                base = base + bits[step] * (span >> (step + 1))
            return base

        def landing(span, t):
            return pl.ds(span - (span >> t), span >> (t + 1))

        def climb(k, t):
            for copy in flight[k]:
                copy.wait_recv()
            if t == 0:
                value = total[k]
                for n in range(sections - 1):
                    value = value + came[k, n].astype(f32)
                total[k] = value
            else:
                mine = block(kept(quarter, t), quarter >> t, 0)
                total[k, mine, :] = total[k, mine, :] + zcame[k, landing(quarter, t - 1), :]
            size = quarter >> (t + 1)
            away = block(kept(quarter, t), size, 1 - bits[t])
            flight[k] = [
                launch(
                    total.at[k, away],
                    zcame.at[k, landing(quarter, t)],
                    2,
                    k * levels + t,
                    along[t],
                )
            ]

        def level(k, t):
            for copy in flight[k]:
                copy.wait_recv()
            mine = block(kept(quarter, t + 1), quarter >> (t + 1), 0)
            if t == levels - 1:
                final[k, mine, :] = total[k, mine, :] + zcame[k, landing(quarter, t), :]
            piece = final.at[k, mine]
            flight[k] = [launch(piece, piece, 3, k * levels + t, along[t])]

        strip = quarter // zones

        def climb_at_once():
            for copy in flight[0]:
                copy.wait_recv()
            value = total[0]
            for n in range(sections - 1):
                value = value + came[0, n].astype(f32)
            total[0] = value
            flight[0] = [
                launch(
                    total.at[0, block(0, strip, z)],
                    zcame.at[0, pl.ds(n * strip, strip)],
                    10,
                    n,
                    lifts[n],
                )
                for n, z in enumerate(floors)
            ]

        def level_at_once():
            for copy in flight[0]:
                copy.wait_recv()
            value = total[0, block(0, strip, d), :]
            for n in range(zones - 1):
                value = value + zcame[0, pl.ds(n * strip, strip), :]
            final[0, block(0, strip, d), :] = value
            piece = final.at[0, block(0, strip, d)]
            flight[0] = [launch(piece, piece, 11, n, peer) for n, peer in enumerate(lifts)]
            strip_home(d)

        def home_strip(z):
            owner = {"section": 0, "seq": c, "dp": d}
            index = lax.rem(s + sections - 1, sections) * zones + z
            place = out.at[block(c * part + s * quarter, strip, z)]
            return remote(
                final.at[0, block(0, strip, z)],
                place,
                sems[24].at[z],
                sems[25].at[index],
                owner,
            )

        def strip_home(z):
            @pl.when(s != 0)
            def _():
                home_strip(z).start()

        def deliver_strips():
            for n, copy in enumerate(flight[0]):
                copy.wait_recv()
                strip_home(lax.rem(d + zones - 1 - n, zones))

            @pl.when(s == 0)
            def _():
                out[block(c * part, quarter, s), :] = final[0]
                relay(0, s).start()

        def home(k):
            owner = {"section": k, "seq": c, "dp": d}
            index = lax.rem(s + 2 * sections - k - 1, sections)
            place = out.at[block(c * part, quarter, s)]
            return remote(final.at[k], place, sems[8].at[k], sems[9].at[index], owner)

        def deliver(k):
            for copy in flight[k]:
                copy.wait_recv()

            @pl.when(s != k)
            def _():
                home(k).start()

            @pl.when(s == k)
            def _():
                out[block(c * part, quarter, s), :] = final[k]
                relay(0, s).start()

        def relay(n, source):
            piece = out.at[block(c * part, quarter, source)]
            return remote(piece, piece, sems[10].at[n], sems[11].at[n], partner)

        def hand(k):
            @pl.when(s == k)
            def _():
                for n, o in enumerate(order):
                    if k:
                        piece = out.at[block(c * part, quarter, o)]
                        remote(
                            final.at[k], piece, sems[8].at[k], sems[9].at[n], across[n]
                        ).wait_recv()
                    else:
                        for z in range(zones):
                            piece = out.at[block(c * part + o * quarter, strip, z)]
                            remote(
                                final.at[0, block(0, strip, z)],
                                piece,
                                sems[24].at[z],
                                sems[25].at[n * zones + z],
                                across[n],
                            ).wait_recv()
                    relay(n + 1, o).start()

        def settle(k):
            @pl.when(s != k)
            def _():
                if k:
                    home(k).wait_send()
                else:
                    for z in range(zones):
                        home_strip(z).wait_send()

            @pl.when(s == k)
            def _():
                for n, o in enumerate([s] + order):
                    relay(n, o).wait()

        def head_swap():
            far = head_ref.at[block(0, side, 1 - c)]
            flight["h"] = [launch(far, hmet, 6, 0, partner)]

        band = side // zones

        def head_climb():
            flight["h"][0].wait_recv()
            hsum[...] = hmet[...] + head_ref[block(0, side, c), :]
            flight["h"] = [
                launch(
                    hsum.at[block(0, band, z)], hcame.at[pl.ds(n * band, band)], 7, n, lifts[n]
                )
                for n, z in enumerate(floors)
            ]

        def head_level():
            for copy in flight["h"]:
                copy.wait_recv()
            value = hsum[block(0, band, d), :]
            for n in range(zones - 1):
                value = value + hcame[pl.ds(n * band, band), :]
            head_out[block(c * side, band, d), :] = value
            mine = head_out.at[block(c * side, band, d)]
            flight["h"] = [launch(mine, mine, 8, n, peer) for n, peer in enumerate(lifts)]
            flight["r"] = [launch(mine, mine, 9, 0, partner)]

        def head_hand():
            for n, copy in enumerate(flight["h"]):
                copy.wait_recv()
                source = lax.rem(d + zones - 1 - n, zones)
                piece = head_out.at[block(c * side, band, source)]
                flight["r"].append(launch(piece, piece, 9, n + 1, partner))

        head_swap()
        pull[pl.ds(0, most), :] = jnp.zeros((most, inner), bf16)
        pull[pl.ds(most + length, most), :] = jnp.zeros((most, inner), bf16)
        sums[...] = jnp.zeros_like(sums)

        top = sections - 1
        stages = {}
        for k in range(sections):
            line = [lambda k=k: swap(k), lambda k=k: spread(k)]
            if k:
                line += [lambda k=k, t=t: climb(k, t) for t in range(levels)]
                line += [lambda k=k, t=t: level(k, t) for t in reversed(range(levels))]
                line.append(lambda k=k: deliver(k))
            else:
                line += [climb_at_once, level_at_once, deliver_strips]
            stages[k] = line + [lambda k=k: hand(k)]
        stages["h"] = [head_climb, head_level, head_hand]
        marks = {}

        def plan(name, ticks):
            for at in ticks:
                if at <= 3 * sections - 1 and stages[name]:
                    marks.setdefault(at, []).append(stages[name].pop(0))

        for k in range(sections):
            plan(k, [3 * (top - k) + 2 + gap for gap in (0, 2, 3, 6, 9)])
        plan("h", (1, 8))
        clock = [0]

        def tick():
            for stage in marks.get(clock[0], []):
                stage()
            clock[0] += 1

        for k in reversed(range(sections)):
            by = unit * 2**k
            slot = k % 2
            above = cot_ref if k == top else grad
            if k:
                prefetch(k - 1)
            for copy in bring[k][0]:
                copy.wait()

            def inward(i, k=k, slot=slot, above=above):
                place = i * tile
                here = above[pl.ds(place, tile), :]
                back = times_transposed(here, held[k, pl.ds(3 * inner, inner), :])
                back = back * bend[slot][pl.ds(place, tile), :].astype(f32)
                pull[pl.ds(most + place, tile), :] = back.astype(bf16)
                sums[k, pl.ds(3 * inner, inner), :] += contract_rows(
                    active[slot][pl.ds(place, tile), :], here
                )

            for i in range(length // tile):
                inward(i)
                tick()
            for copy in bring[k][1]:
                copy.wait()

            def outward(i, carry, k=k, by=by, slot=slot, above=above):
                place = pl.multiple_of(i * tile, 16)
                there = hidden[slot][pl.ds(place, tile), :]
                value = None
                for j in range(3 if k < top else 2):
                    if k < top:
                        start = pl.multiple_of(most + place + (1 - j) * by, 16)
                        span = pl.ds(j * inner, inner)
                    else:
                        start = most + (1 - j) * by
                        span = pl.ds(pl.multiple_of((i + j) * inner, 16), inner)
                    piece = pull[pl.ds(start, tile), :]
                    sums[k, span, :] += contract_rows(piece, there)
                    if k:
                        term = jnp.dot(piece, held[k, span, :], preferred_element_type=f32)
                        value = term if value is None else value + term
                if k:
                    value = value * slope[slot][pl.ds(place, tile), :].astype(f32)
                    value = value + above[pl.ds(place, tile), :].astype(f32)
                    grad[pl.ds(place, tile), :] = value.astype(bf16)
                return carry

            lax.fori_loop(0, length // tile, outward, 0)
            tick()

        rounds = 0
        while any(stages.values()):
            for name in [*reversed(range(2, sections)), 0, 1, "h"]:
                if stages[name] and (name != "h" or rounds > 1):
                    stages[name].pop(0)()
            rounds += 1
        for copy in flight["r"]:
            copy.wait_recv()
        for k in range(sections):
            settle(k)
        for copy in sends:
            copy.wait_send()

    dma = pltpu.SemaphoreType.DMA

    def pair(count):
        return [dma((count,))] * 2

    long, thin = pltpu.VMEM((length, channels), bf16), pltpu.VMEM((length, inner), bf16)
    vmem = pl.BlockSpec(memory_space=pltpu.VMEM)
    return pl.pallas_call(
        kernel,
        out_shape=[
            jax.ShapeDtypeStruct((rows, channels), f32),
            jax.ShapeDtypeStruct(head_part.shape, f32),
        ],
        in_specs=[vmem, vmem] + [ANY] * (4 * sections),
        out_specs=[vmem, vmem],
        scratch_shapes=[long] * 4
        + [thin] * 4
        + [
            pltpu.VMEM(weights.shape, bf16),
            long,
            pltpu.VMEM((length + 2 * most, inner), bf16),
            pltpu.VMEM((sections, rows, channels), f32),
            dma((5 * sections,)),
            pltpu.VMEM((sections, part, channels), f32),
            pltpu.VMEM((sections, sections - 1, quarter, channels), bf16),
            pltpu.VMEM((sections, sections - 1, quarter, channels), bf16),
            pltpu.VMEM((sections, quarter, channels), f32),
            pltpu.VMEM((sections, quarter, channels), f32),
            pltpu.VMEM((sections, quarter, channels), f32),
            pltpu.VMEM((side, tracks), f32),
            pltpu.VMEM((side, tracks), f32),
            pltpu.VMEM((side, tracks), f32),
        ]
        + pair(sections)
        + pair(sections * (sections - 1))
        + pair(sections * levels)
        + pair(sections * levels)
        + [dma((sections,)), dma((sections,))]
        + pair(sections)
        + pair(1)
        + pair(zones - 1)
        + pair(zones - 1)
        + pair(zones)
        + pair(zones - 1)
        + pair(zones - 1)
        + [dma((zones,)), dma((sections * zones,))],
        compiler_params=pltpu.CompilerParams(
            collective_id=2, has_side_effects=True, vmem_limit_bytes=48 * 2**20
        ),
        name="backward_tower",
    )(head_part, cot, weights, *hidden, *slope, *active, *bend)


def finish(total, head_sum, split):
    def kernel(total_ref, head_ref, conv_out, proj_out, head_out, sems):
        copies = [
            pltpu.make_async_copy(total_ref.at[pl.ds(0, split)], conv_out, sems.at[0]),
            pltpu.make_async_copy(
                total_ref.at[pl.ds(split, total.shape[0] - split)], proj_out, sems.at[1]
            ),
            pltpu.make_async_copy(head_ref, head_out, sems.at[2]),
        ]
        for copy in copies:
            copy.start()
        for copy in copies:
            copy.wait()

    width = total.shape[1]
    return pl.pallas_call(
        kernel,
        out_shape=[
            jax.ShapeDtypeStruct((split, width), total.dtype),
            jax.ShapeDtypeStruct((total.shape[0] - split, width), total.dtype),
            jax.ShapeDtypeStruct(head_sum.shape, head_sum.dtype),
        ],
        in_specs=[pl.BlockSpec(memory_space=pltpu.VMEM)] * 2,
        out_specs=[ANY] * 3,
        scratch_shapes=[pltpu.SemaphoreType.DMA((3,))],
        compiler_params=pltpu.CompilerParams(vmem_limit_bytes=8 * 2**20),
        name="finish",
    )(total, head_sum)


def plain_body(bases, targets, stem_weight, conv_weight, proj_weight, head_weight):
    sections = lax.axis_size("section")
    seqs = lax.axis_size("seq")
    section_number = lax.axis_index("section")
    batches, row_count, bin_width = bases.shape
    channels = stem_weight.shape[1]
    length = row_count * seqs
    factor = 1.0 / math.sqrt(batches * lax.axis_size("dp") * length)
    unit = length // 2**sections
    local_q = row_count // unit
    blocks = length // unit
    columns = batches * unit // (seqs * sections)

    conv_all = lax.all_gather(conv_weight, "section", axis=0, tiled=True)
    proj_all = lax.all_gather(proj_weight, "section", axis=0, tiled=True)

    def to_chains(value):
        value = lax.all_to_all(value, "seq", split_axis=1, concat_axis=0, tiled=True)
        return value.reshape(blocks * columns, value.shape[-1])

    own = bases.reshape(batches, local_q, unit, bin_width).transpose(1, 0, 2, 3)
    own = own.reshape(local_q, seqs, sections, columns, bin_width)
    own = lax.dynamic_index_in_dim(own, section_number, 2, keepdims=False)
    picked = to_chains(own.astype(jnp.bfloat16))
    onehot = jnp.concatenate([(picked == c).astype(jnp.bfloat16) for c in range(4)], 1)
    stem = stem_weight.reshape(bin_width, 4, channels).transpose(1, 0, 2).reshape(-1, channels)
    state = jnp.dot(onehot, stem, preferred_element_type=jnp.float32).astype(jnp.bfloat16)

    saved = []
    for layer in range(sections):
        by = columns * 2**layer
        taps = conv_all[layer].reshape(-1, conv_all.shape[-1])
        hidden = gelu_value(state.astype(jnp.float32)).astype(jnp.bfloat16)
        wide = jnp.concatenate([shift_rows(hidden, by), hidden, shift_rows(hidden, -by)], 1)
        inner_sum = jnp.dot(wide, taps, preferred_element_type=jnp.float32)
        active = gelu_value(inner_sum).astype(jnp.bfloat16)
        update = jnp.dot(active, proj_all[layer], preferred_element_type=jnp.float32)
        saved.append((state, wide, inner_sum, active))
        state = (state.astype(jnp.float32) + update).astype(jnp.bfloat16)

    lifted = gelu_value(state.astype(jnp.float32)).astype(jnp.bfloat16)
    lifted = lifted.reshape(seqs, local_q, 1, columns, channels)
    lifted = lax.all_to_all(lifted, "seq", split_axis=0, concat_axis=2, tiled=True)
    lifted = lifted.reshape(local_q, seqs, 1, columns, channels)
    lifted = lax.all_gather(lifted, "section", axis=2, tiled=True)
    lifted = lifted.reshape(local_q, batches, unit, channels).transpose(1, 0, 2, 3)
    lifted = lifted.reshape(batches * row_count, channels)

    logits = jnp.dot(lifted, head_weight, preferred_element_type=jnp.float32)
    counts = targets.reshape(batches * row_count, targets.shape[2]).astype(jnp.float32)
    slope = ((jnp.exp(logits) - counts) * factor).astype(jnp.bfloat16)
    head_sum = lax.psum(contract_rows(lifted, slope), ("seq", "dp"))
    lift_part = times_transposed(slope, head_weight)

    lift_part = lift_part.reshape(batches, local_q, unit, channels).transpose(1, 0, 2, 3)
    lift_part = lift_part.reshape(local_q, seqs, sections, columns, channels)
    lift_part = lax.psum_scatter(lift_part, "section", scatter_dimension=2, tiled=True)
    lift_grad = to_chains(lift_part.reshape(local_q, seqs, columns, channels))


    grad = (lift_grad * gelu_slope(state.astype(jnp.float32))).astype(jnp.bfloat16)
    parts = []
    for layer in reversed(range(sections)):
        by = columns * 2**layer
        start_state, wide, inner_sum, active = saved[layer]
        kernel = conv_all[layer]
        proj_part = contract_rows(active, grad)
        active_grad = times_transposed(grad, proj_all[layer])
        inner_grad = (active_grad * gelu_slope(inner_sum)).astype(jnp.bfloat16)
        parts.append(jnp.concatenate([contract_rows(inner_grad, wide), proj_part], 1))
        wide_grad = jnp.concatenate(
            [shift_rows(inner_grad, -by), inner_grad, shift_rows(inner_grad, by)], 1
        )
        turned = kernel.transpose(0, 2, 1).reshape(-1, channels)
        hidden_grad = jnp.dot(wide_grad, turned, preferred_element_type=jnp.float32)
        grad = (
            grad.astype(jnp.float32) + hidden_grad * gelu_slope(start_state.astype(jnp.float32))
        ).astype(jnp.bfloat16)
    parts = jnp.stack(parts[::-1])
    total = lax.psum_scatter(parts, "section", scatter_dimension=0, tiled=True)
    total = lax.psum(total[0], ("seq", "dp"))
    taps_width = total.shape[1] - channels
    conv_sum = total[:, :taps_width].T.reshape(conv_weight.shape)
    return conv_sum, total[:, taps_width:][None], head_sum


def paired_body(bases, targets, stem_weight, conv_weight, proj_weight, head_weight):
    sections = lax.axis_size("section")
    zones = lax.axis_size("dp")
    batches, half, bin_width = bases.shape
    channels = stem_weight.shape[1]
    inner = proj_weight.shape[1]
    length = batches * half
    unit = length // 2**sections
    factor = 1.0 / math.sqrt(batches * zones * length)
    taps = conv_weight[0].transpose(0, 2, 1).reshape(3 * inner, channels)
    top, weights, hidden, slope, active, bend = forward_tower(
        bases, stem_weight, taps, proj_weight[0], sections, unit
    )
    head_part, cot = head(top, targets, head_weight, factor)
    cot = cot.reshape(length, channels)
    total, head_sum = backward_tower(
        head_part, cot, weights, hidden, slope, active, bend, sections, zones, unit
    )
    conv_sum, proj_sum, head_sum = finish(total, head_sum, 3 * inner)
    conv_sum = conv_sum.reshape(3, inner, channels).transpose(0, 2, 1)
    return conv_sum[None], proj_sum[None], head_sum


def body(bases, targets, stem_weight, conv_weight, proj_weight, head_weight):
    sections, zones = lax.axis_size("section"), lax.axis_size("dp")
    batches, half = bases.shape[:2]
    inner = proj_weight.shape[1]
    unit = batches * half // 2**sections
    paired = lax.axis_size("seq") == 2 and batches == 2 and zones > 1 and sections > 1
    paired = paired and unit % 16 == 0 and half % 16 == 0 and inner % 16 == 0
    paired = paired and (2 * inner) % (16 * sections) == 0
    paired = paired and (2 * inner) % (8 * sections * zones) == 0
    paired = paired and zones & (zones - 1) == 0
    paired = paired and stem_weight.shape[1] % (16 * zones) == 0
    run = paired_body if paired else plain_body
    return run(bases, targets, stem_weight, conv_weight, proj_weight, head_weight)


def solution(mesh):
    in_specs = (
        P("dp", "seq", None),
        P("dp", "seq", "section"),
        P(),
        P("section", None, None, None),
        P("section", None, None),
        P(None, "section"),
    )
    out_specs = (P("section", None, None, None), P("section", None, None), P(None, "section"))
    return jax.shard_map(body, mesh=mesh, in_specs=in_specs, out_specs=out_specs, check_vma=False)
```

```python
import math

import jax
import jax.numpy as jnp
from jax import lax
from jax.experimental import pallas as pl
from jax.experimental.pallas import tpu as pltpu
from jax.sharding import PartitionSpec as P

SQRT_TWO_OVER_PI = 0.7978845608028654
CUBIC_TERM = 0.044715


def gelu_value(inputs):
    return (
        0.5
        * inputs
        * (1.0 + jnp.tanh(SQRT_TWO_OVER_PI * (inputs + CUBIC_TERM * inputs * inputs * inputs)))
    )


def gelu_slope(inputs):
    tangent = jnp.tanh(SQRT_TWO_OVER_PI * (inputs + CUBIC_TERM * inputs * inputs * inputs))
    return 0.5 * (1.0 + tangent) + 0.5 * inputs * (1.0 - tangent * tangent) * SQRT_TWO_OVER_PI * (
        1.0 + 3.0 * CUBIC_TERM * inputs * inputs
    )


def contract_rows(left_side, right_side):
    return lax.dot_general(
        left_side, right_side, (((0,), (0,)), ((), ())), preferred_element_type=jnp.float32
    )


def times_transposed(left_side, right_side):
    return lax.dot_general(
        left_side, right_side, (((1,), (1,)), ((), ())), preferred_element_type=jnp.float32
    )


def shift_rows(value, by):
    if abs(by) >= value.shape[0]:
        return jnp.zeros_like(value)
    pad = jnp.zeros((abs(by),) + value.shape[1:], value.dtype)
    if by > 0:
        return jnp.concatenate([pad, value[:-by]], 0)
    return jnp.concatenate([value[-by:], pad], 0)


MESH = pl.DeviceIdType.MESH
ANY = pl.BlockSpec(memory_space=pl.ANY)


def greet(peers):
    barrier = pltpu.get_barrier_semaphore()
    for peer in peers:
        pl.semaphore_signal(barrier, inc=1, device_id=peer, device_id_type=MESH)
    pl.semaphore_wait(barrier, len(peers))


def remote(src, dst, send, recv, peer):
    return pltpu.make_async_remote_copy(
        src_ref=src, dst_ref=dst, send_sem=send, recv_sem=recv, device_id=peer, device_id_type=MESH
    )


def both_gelu(inputs):
    square = inputs * inputs
    tangent = jnp.tanh(
        inputs * (SQRT_TWO_OVER_PI + (SQRT_TWO_OVER_PI * CUBIC_TERM) * square)
    )
    gate = 0.5 + 0.5 * tangent
    value = inputs * gate
    inside = 2.0 * SQRT_TWO_OVER_PI + (6.0 * SQRT_TWO_OVER_PI * CUBIC_TERM) * square
    return value, gate + value * (1.0 - gate) * inside


def tile_of(rows):
    for size in (512, 384, 256, 192, 128, 96, 64, 48, 32, 16):
        if rows % size == 0:
            return size
    return rows


def forward_tower(bases, stem, taps, proj, sections, unit):
    seqs, half, width = bases.shape
    length = seqs * half
    channels = stem.shape[1]
    inner = proj.shape[0]
    rows = taps.shape[0] + inner
    part = rows // 2
    tile = tile_of(half)
    steps = half // tile
    team = 3 if steps % 3 == 0 else 1
    shifts = [unit * 2**k for k in range(sections)]

    def kernel(*refs):
        bases_ref, stem_ref, taps_ref, proj_ref = refs[:4]
        refs = refs[4:]
        top_ref, weights_ref = refs[:2]
        hidden_out, slope_out = refs[2 : 2 + sections], refs[2 + sections : 1 + 2 * sections]
        refs = refs[1 + 2 * sections :]
        active_out, bend_out = refs[:sections], refs[sections : 2 * sections]
        refs = refs[2 * sections :]
        full, held, turned, state, sorted_stem = refs[:5]
        refs = refs[5:]
        hidden, slope = refs[:sections], refs[sections : 2 * sections - 1]
        refs = refs[2 * sections - 1 :]
        active, bend = refs[:sections], refs[sections : 2 * sections]
        refs = refs[2 * sections :]
        bsend, brecv, send, recv, send2, recv2, tsend, trecv, own_sem, out_sem = refs

        s, c = lax.axis_index("section"), lax.axis_index("seq")
        partner = {"section": s, "seq": 1 - c}
        peers = [{"section": lax.rem(s + k, sections), "seq": c} for k in range(1, sections)]
        loads = [
            pltpu.make_async_copy(bases_ref.at[c], full.at[c], own_sem.at[0]),
            pltpu.make_async_copy(
                taps_ref, held.at[s, pl.ds(0, taps.shape[0])], own_sem.at[1]
            ),
            pltpu.make_async_copy(
                proj_ref, held.at[s, pl.ds(taps.shape[0], inner)], own_sem.at[2]
            ),
        ]
        for copy in loads:
            copy.start()
        greet(peers + [partner])
        across = remote(bases_ref.at[1 - c], full.at[c], bsend, brecv, partner)
        across.start()
        loads[1].wait()
        loads[2].wait()
        mine = held.at[s, pl.ds(pl.multiple_of(c * part, 16), part)]
        first = []
        for k, peer in enumerate(peers):
            first.append(remote(mine, mine, send.at[k], recv.at[k], peer))
            first[-1].start()
        for k in range(sections - 1):
            edge = jnp.zeros((shifts[k], channels), jnp.bfloat16)
            hidden[k][pl.ds(0, shifts[k]), :] = edge
            hidden[k][pl.ds(shifts[k] + length, shifts[k]), :] = edge

        across_rows = lax.broadcasted_iota(jnp.int32, (4 * width, 4 * width), 0)
        across_columns = lax.broadcasted_iota(jnp.int32, (4 * width, 4 * width), 1)
        place_of = 4 * lax.rem(across_rows, width) + across_rows // width
        chosen = (across_columns == place_of).astype(jnp.bfloat16)
        sorted_stem[...] = jnp.dot(
            chosen, stem_ref[...], preferred_element_type=jnp.float32
        ).astype(jnp.bfloat16)

        def begin(number):
            def step(i, carry):
                at = i * tile
                codes = full[number, pl.ds(pl.multiple_of(at, 16), tile), :]
                onehot = jnp.concatenate(
                    [(codes == k).astype(jnp.bfloat16) for k in range(4)], 1
                )
                start = jnp.dot(onehot, sorted_stem[...], preferred_element_type=jnp.float32)
                start = start.astype(jnp.bfloat16)
                place = pl.multiple_of(number * half + at, 16)
                state[pl.ds(place, tile), :] = start
                value = gelu_value(start.astype(jnp.float32)).astype(jnp.bfloat16)
                hidden[0][pl.ds(pl.multiple_of(shifts[0] + place, 16), tile), :] = value
                return carry

            lax.fori_loop(0, steps, step, 0)

        loads[0].wait()
        begin(c)
        across.wait_recv()
        begin(1 - c)

        second = []
        for k in range(sections - 1):
            first[k].wait_recv()
            source = lax.rem(s + sections - 1 - k, sections)
            piece = held.at[source, pl.ds(pl.multiple_of(c * part, 16), part)]
            second.append(remote(piece, piece, send2.at[k], recv2.at[k], partner))
            second[-1].start()
        for copy in second:
            copy.wait_recv()

        outs = []

        def keep(src, dst):
            outs.append(pltpu.make_async_copy(src, dst, out_sem.at[len(outs)]))
            outs[-1].start()

        keep(held, weights_ref)
        keep(hidden[0].at[pl.ds(shifts[0], length)], hidden_out[0])

        for k in range(sections):
            by = shifts[k]
            for j in range(3):
                tap = held[k, pl.ds(j * inner, inner), :]
                turned[pl.ds(j * channels, channels), :] = tap.T

            def group(places, lead, width, k=k, by=by):
                weight = turned[pl.ds(pl.multiple_of(lead * channels, 16), width * channels), :]
                inners = []
                for place in places:
                    wide = jnp.concatenate(
                        [
                            hidden[k][pl.ds(pl.multiple_of(place + (lead + j) * by, 16), tile), :]
                            for j in range(width)
                        ],
                        1,
                    )
                    inners.append(
                        jnp.dot(wide, weight, preferred_element_type=jnp.float32)
                    )
                olds = [state[pl.ds(place, tile), :].astype(jnp.float32) for place in places]
                results = []
                for inner_sum, old in zip(inners, olds):
                    value, bent = both_gelu(inner_sum)
                    value, bent = value.astype(jnp.bfloat16), bent.astype(jnp.bfloat16)
                    update = jnp.dot(
                        value,
                        held[k, pl.ds(3 * inner, inner), :],
                        preferred_element_type=jnp.float32,
                    )
                    results.append((value, bent, (old + update).astype(jnp.bfloat16)))
                for place, (value, bent, _) in zip(places, results):
                    active[k][pl.ds(place, tile), :] = value
                    bend[k][pl.ds(place, tile), :] = bent
                return [new for _, _, new in results]

            def spots(i, base):
                return [
                    pl.multiple_of(base + (i * team + g) * tile, 16) for g in range(team)
                ]

            if k < sections - 1:

                def step(i, carry, k=k):
                    places = spots(i, 0)
                    news = group(places, 0, 3)
                    pairs = [both_gelu(new.astype(jnp.float32)) for new in news]
                    for place, new, (value, bent) in zip(places, news, pairs):
                        state[pl.ds(place, tile), :] = new
                        ahead = pl.multiple_of(shifts[k + 1] + place, 16)
                        hidden[k + 1][pl.ds(ahead, tile), :] = value.astype(jnp.bfloat16)
                        slope[k][pl.ds(place, tile), :] = bent.astype(jnp.bfloat16)
                    return carry

                lax.fori_loop(0, length // (tile * team), step, 0)
                keep(hidden[k + 1].at[pl.ds(shifts[k + 1], length)], hidden_out[k + 1])
                keep(slope[k], slope_out[k])
            else:

                def finish_half(number):
                    def step(i, carry):
                        places = spots(i, number * half)
                        for place, new in zip(places, group(places, 1 - number, 2)):
                            state[pl.ds(place, tile), :] = new
                        return carry

                    lax.fori_loop(0, steps // team, step, 0)

                finish_half(1 - c)
                theirs = state.at[pl.ds(pl.multiple_of((1 - c) * half, 16), half)]
                last = remote(theirs, top_ref.at[c], tsend, trecv, partner)
                last.start()
                finish_half(c)
                top_ref[c] = state[pl.ds(pl.multiple_of(c * half, 16), half), :]
            keep(active[k], active_out[k])
            keep(bend[k], bend_out[k])
        for copy in outs:
            copy.wait()
        last.wait()
        across.wait_send()
        for copy in first + second:
            copy.wait_send()

    bf16 = jnp.bfloat16
    long = jax.ShapeDtypeStruct((length, channels), bf16)
    thin = jax.ShapeDtypeStruct((length, inner), bf16)
    dma = pltpu.SemaphoreType.DMA
    copies = 4 * sections
    out = pl.pallas_call(
        kernel,
        out_shape=[
            jax.ShapeDtypeStruct((seqs, half, channels), bf16),
            jax.ShapeDtypeStruct((sections, rows, channels), bf16),
        ]
        + [long] * (2 * sections - 1)
        + [thin] * (2 * sections),
        in_specs=[ANY, pl.BlockSpec(memory_space=pltpu.VMEM), ANY, ANY],
        out_specs=[pl.BlockSpec(memory_space=pltpu.VMEM)] + [ANY] * (4 * sections),
        scratch_shapes=[
            pltpu.VMEM((seqs, half, width), jnp.int32),
            pltpu.VMEM((sections, rows, channels), bf16),
            pltpu.VMEM((3 * channels, inner), bf16),
            pltpu.VMEM((length, channels), bf16),
            pltpu.VMEM(stem.shape, bf16),
        ]
        + [pltpu.VMEM((length + 2 * by, channels), bf16) for by in shifts]
        + [pltpu.VMEM((length, channels), bf16)] * (sections - 1)
        + [pltpu.VMEM((length, inner), bf16)] * (2 * sections)
        + [dma, dma]
        + [dma((sections - 1,))] * 4
        + [dma, dma, dma((3,)), dma((copies,))],
        compiler_params=pltpu.CompilerParams(
            collective_id=0, has_side_effects=True, vmem_limit_bytes=54 * 2**20
        ),
        name="forward_tower",
    )(bases, stem, taps, proj)
    top, weights = out[:2]
    hidden, slope = out[2 : 2 + sections], out[2 + sections : 1 + 2 * sections]
    active = out[1 + 2 * sections : 1 + 3 * sections]
    bend = out[1 + 3 * sections :]
    return top, weights, hidden, slope, active, bend


def head(top, targets, head_weight, factor):
    seqs, half, channels = top.shape
    tracks = head_weight.shape[1]
    tile = tile_of(half)
    if half % 512 == 0:
        tile = 512
    steps = half // tile

    def kernel(
        top_ref, targets_ref, weight_ref, grad_ref, cot_ref, counts, stage, load, send, recv
    ):
        s, c = lax.axis_index("section"), lax.axis_index("seq")
        partner = {"section": s, "seq": 1 - c}
        loads = []
        for n, b in enumerate((1 - c, c)):
            for i in range(steps):
                loads.append(
                    pltpu.make_async_copy(
                        targets_ref.at[b, pl.ds(i * tile, tile)],
                        counts.at[n * steps + i],
                        load.at[n * steps + i],
                    )
                )
                loads[-1].start()
        greet([partner])
        grad_ref[...] = jnp.zeros_like(grad_ref)

        def run(b, n, store):
            def step(i, carry):
                at = pl.multiple_of(i * tile, 16)
                pltpu.make_async_copy(
                    targets_ref.at[b, pl.ds(at, tile)], counts.at[n + i], load.at[n + i]
                ).wait()
                value, bent = both_gelu(top_ref[b, pl.ds(at, tile), :].astype(jnp.float32))
                lifted = value.astype(jnp.bfloat16)
                logits = jnp.dot(lifted, weight_ref[...], preferred_element_type=jnp.float32)
                drop = jnp.exp(logits) - counts[n + i].astype(jnp.float32)
                drop = (drop * factor).astype(jnp.bfloat16)
                grad_ref[...] += contract_rows(lifted, drop)
                lift = times_transposed(drop, weight_ref[...])
                store(at, (lift * bent).astype(jnp.bfloat16))
                return carry

            lax.fori_loop(0, steps, step, 0)

        def away(at, value):
            stage[pl.ds(at, tile), :] = value

        def here(at, value):
            cot_ref[c, pl.ds(at, tile), :] = value

        run(1 - c, 0, away)
        copy = remote(stage, cot_ref.at[c], send, recv, partner)
        copy.start()
        run(c, steps, here)
        copy.wait()

    vmem = pl.BlockSpec(memory_space=pltpu.VMEM)
    dma = pltpu.SemaphoreType.DMA
    return pl.pallas_call(
        kernel,
        out_shape=[
            jax.ShapeDtypeStruct((channels, tracks), jnp.float32),
            jax.ShapeDtypeStruct(top.shape, jnp.bfloat16),
        ],
        in_specs=[vmem, ANY, vmem],
        out_specs=[vmem, vmem],
        scratch_shapes=[
            pltpu.VMEM((seqs * steps, tile, tracks), jnp.int32),
            pltpu.VMEM((half, channels), jnp.bfloat16),
            dma((seqs * steps,)),
            dma,
            dma,
        ],
        compiler_params=pltpu.CompilerParams(
            collective_id=1, has_side_effects=True, vmem_limit_bytes=48 * 2**20
        ),
        name="head",
    )(top, targets, head_weight)


def backward_tower(head_part, cot, weights, hidden, slope, active, bend, sections, zones, unit):
    length, channels = hidden[0].shape
    inner = active[0].shape[1]
    rows = weights.shape[1]
    part = rows // 2
    quarter = part // sections
    levels = zones.bit_length() - 1
    tracks = head_part.shape[1]
    side = head_part.shape[0] // 2
    tile = length // 2
    most = unit * 2 ** (sections - 1)
    f32, bf16 = jnp.float32, jnp.bfloat16

    def kernel(*refs):
        head_ref, cot_ref, weights_ref = refs[:3]
        refs = refs[3:]
        hidden_in, slope_in = refs[:sections], refs[sections : 2 * sections - 1]
        refs = refs[2 * sections - 1 :]
        active_in, bend_in = refs[:sections], refs[sections : 2 * sections]
        refs = refs[2 * sections :]
        out, head_out = refs[:2]
        hidden, slope, active, bend = refs[2:4], refs[4:6], refs[6:8], refs[8:10]
        held, grad, pull, sums, load = refs[10:15]
        met, wire, came, total, zcame, final = refs[15:21]
        hmet, hsum, hcame = refs[21:24]
        sems = refs[24:]

        s, c, d = (lax.axis_index(name) for name in ("section", "seq", "dp"))
        partner = {"section": s, "seq": 1 - c, "dp": d}
        order = [lax.rem(s + k, sections) for k in range(1, sections)]
        across = [{"section": o, "seq": c, "dp": d} for o in order]
        bits = [lax.rem(d // 2**t, 2) for t in range(levels)]
        along = [
            {"section": s, "seq": c, "dp": d + 2**t * (1 - 2 * bits[t])} for t in range(levels)
        ]
        floors = [lax.rem(d + n, zones) for n in range(1, zones)]
        lifts = [{"section": s, "seq": c, "dp": z} for z in floors]
        count = [0]

        def fetch(src, dst):
            copy = pltpu.make_async_copy(src, dst, load.at[count[0]])
            count[0] += 1
            copy.start()
            return copy

        bring = {}

        def prefetch(k):
            slot = k % 2
            early = [
                fetch(weights_ref.at[k], held.at[k]),
                fetch(bend_in[k], bend[slot]),
                fetch(active_in[k], active[slot]),
            ]
            late = [fetch(hidden_in[k], hidden[slot])]
            if k:
                late.append(fetch(slope_in[k - 1], slope[slot]))
            bring[k] = (early, late)

        prefetch(sections - 1)
        greet([partner] + across + lifts)

        sends = []

        def launch(src, dst, pair, index, peer):
            copy = remote(src, dst, sems[2 * pair].at[index], sems[2 * pair + 1].at[index], peer)
            copy.start()
            sends.append(copy)
            return copy

        def block(base, size, number):
            return pl.ds(pl.multiple_of(base + number * size, 8), size)

        flight = {}

        def swap(k):
            far = sums.at[k, block(0, part, 1 - c)]
            flight[k] = [launch(far, met.at[k], 0, k, partner)]

        def spread(k):
            flight[k][0].wait_recv()
            flight[k] = []

            def both(o):
                return met[k, block(0, quarter, o), :] + sums[k, block(c * part, quarter, o), :]

            for n, o in enumerate(order):
                wire[k, n] = both(o).astype(bf16)
                flight[k].append(
                    launch(wire.at[k, n], came.at[k, n], 1, k * (sections - 1) + n, across[n])
                )
            total[k] = both(s)

        def kept(span, t):
            base = 0
            for step in range(t):
                base = base + bits[step] * (span >> (step + 1))
            return base

        def landing(span, t):
            return pl.ds(span - (span >> t), span >> (t + 1))

        def climb(k, t):
            for copy in flight[k]:
                copy.wait_recv()
            if t == 0:
                value = total[k]
                for n in range(sections - 1):
                    value = value + came[k, n].astype(f32)
                total[k] = value
            else:
                mine = block(kept(quarter, t), quarter >> t, 0)
                total[k, mine, :] = total[k, mine, :] + zcame[k, landing(quarter, t - 1), :]
            size = quarter >> (t + 1)
            away = block(kept(quarter, t), size, 1 - bits[t])
            flight[k] = [
                launch(
                    total.at[k, away],
                    zcame.at[k, landing(quarter, t)],
                    2,
                    k * levels + t,
                    along[t],
                )
            ]

        def level(k, t):
            for copy in flight[k]:
                copy.wait_recv()
            mine = block(kept(quarter, t + 1), quarter >> (t + 1), 0)
            if t == levels - 1:
                final[k, mine, :] = total[k, mine, :] + zcame[k, landing(quarter, t), :]
            piece = final.at[k, mine]
            flight[k] = [launch(piece, piece, 3, k * levels + t, along[t])]

        strip = quarter // zones
        brisk = 0

        def climb_at_once(k):
            for copy in flight[k]:
                copy.wait_recv()
            value = total[k]
            for n in range(sections - 1):
                value = value + came[k, n].astype(f32)
            total[k] = value
            flight[k] = [
                launch(
                    total.at[k, block(0, strip, z)],
                    zcame.at[k, pl.ds(n * strip, strip)],
                    10,
                    k * (zones - 1) + n,
                    lifts[n],
                )
                for n, z in enumerate(floors)
            ]

        def level_at_once(k):
            for copy in flight[k]:
                copy.wait_recv()
            value = total[k, block(0, strip, d), :]
            for n in range(zones - 1):
                value = value + zcame[k, pl.ds(n * strip, strip), :]
            final[k, block(0, strip, d), :] = value
            piece = final.at[k, block(0, strip, d)]
            flight[k] = [launch(piece, piece, 11, k * (zones - 1) + n, peer) for n, peer in enumerate(lifts)]
            strip_home(k, d)

        def home_strip(k, z):
            owner = {"section": k, "seq": c, "dp": d}
            index = lax.rem(s + 2 * sections - k - 1, sections) * zones + z
            place = out.at[block(c * part + s * quarter, strip, z)]
            return remote(
                final.at[k, block(0, strip, z)],
                place,
                sems[24].at[k * zones + z],
                sems[25].at[index],
                owner,
            )

        def strip_home(k, z):
            @pl.when(s != k)
            def _():
                home_strip(k, z).start()

        def deliver_strips(k):
            for n, copy in enumerate(flight[k]):
                copy.wait_recv()
                strip_home(k, lax.rem(d + zones - 1 - n, zones))

            @pl.when(s == k)
            def _():
                out[block(c * part, quarter, s), :] = final[k]
                relay(0, s).start()

        def home(k):
            owner = {"section": k, "seq": c, "dp": d}
            index = lax.rem(s + 2 * sections - k - 1, sections)
            place = out.at[block(c * part, quarter, s)]
            return remote(final.at[k], place, sems[8].at[k], sems[9].at[index], owner)

        def deliver(k):
            for copy in flight[k]:
                copy.wait_recv()

            @pl.when(s != k)
            def _():
                home(k).start()

            @pl.when(s == k)
            def _():
                out[block(c * part, quarter, s), :] = final[k]
                relay(0, s).start()

        def relay(n, source):
            piece = out.at[block(c * part, quarter, source)]
            return remote(piece, piece, sems[10].at[n], sems[11].at[n], partner)

        def hand(k):
            @pl.when(s == k)
            def _():
                for n, o in enumerate(order):
                    if k > brisk:
                        piece = out.at[block(c * part, quarter, o)]
                        remote(
                            final.at[k], piece, sems[8].at[k], sems[9].at[n], across[n]
                        ).wait_recv()
                    else:
                        for z in range(zones):
                            piece = out.at[block(c * part + o * quarter, strip, z)]
                            remote(
                                final.at[k, block(0, strip, z)],
                                piece,
                                sems[24].at[k * zones + z],
                                sems[25].at[n * zones + z],
                                across[n],
                            ).wait_recv()
                    relay(n + 1, o).start()

        def settle(k):
            @pl.when(s != k)
            def _():
                if k > brisk:
                    home(k).wait_send()
                else:
                    for z in range(zones):
                        home_strip(k, z).wait_send()

            @pl.when(s == k)
            def _():
                for n, o in enumerate([s] + order):
                    relay(n, o).wait()

        def head_swap():
            far = head_ref.at[block(0, side, 1 - c)]
            flight["h"] = [launch(far, hmet, 6, 0, partner)]

        def head_climb(t):
            flight["h"][0].wait_recv()
            if t == 0:
                hsum[...] = hmet[...] + head_ref[block(0, side, c), :]
            else:
                mine = block(kept(side, t), side >> t, 0)
                hsum[mine, :] = hsum[mine, :] + hcame[landing(side, t - 1), :]
            away = block(kept(side, t), side >> (t + 1), 1 - bits[t])
            flight["h"] = [
                launch(hsum.at[away], hcame.at[landing(side, t)], 7, t, along[t])
            ]

        flight["r"] = []

        def pass_on(start, size):
            piece = head_out.at[block(c * side + start, size, 0)]
            flight["r"].append(launch(piece, piece, 9, len(flight["r"]), partner))

        def other(span, t):
            return kept(span, t) + (1 - bits[t]) * (span >> (t + 1))

        def head_level(t):
            flight["h"][0].wait_recv()
            start, size = kept(side, t + 1), side >> (t + 1)
            place = block(c * side + start, size, 0)
            if t == levels - 1:
                mine = block(start, size, 0)
                head_out[place, :] = hsum[mine, :] + hcame[landing(side, t), :]
                pass_on(start, size)
            else:
                pass_on(other(side, t + 1), side >> (t + 2))
            piece = head_out.at[place]
            flight["h"] = [launch(piece, piece, 8, t, along[t])]

        def head_hand():
            flight["h"][0].wait_recv()
            pass_on(other(side, 0), side // 2)

        head_swap()
        pull[pl.ds(0, most), :] = jnp.zeros((most, inner), bf16)
        pull[pl.ds(most + length, most), :] = jnp.zeros((most, inner), bf16)
        sums[...] = jnp.zeros_like(sums)

        top = sections - 1
        stages = {}
        for k in range(sections):
            line = [lambda k=k: swap(k), lambda k=k: spread(k)]
            if k > brisk:
                line += [lambda k=k, t=t: climb(k, t) for t in range(levels)]
                line += [lambda k=k, t=t: level(k, t) for t in reversed(range(levels))]
                line.append(lambda k=k: deliver(k))
            else:
                for stage in (climb_at_once, level_at_once, deliver_strips):
                    line.append(lambda k=k, stage=stage: stage(k))
            stages[k] = line + [lambda k=k: hand(k)]
        line = [lambda t=t: head_climb(t) for t in range(levels)]
        line += [lambda t=t: head_level(t) for t in reversed(range(levels))]
        stages["h"] = line + [head_hand]
        marks = {}

        def plan(name, ticks):
            for at in ticks:
                if at <= 3 * sections - 1 and stages[name]:
                    marks.setdefault(at, []).append(stages[name].pop(0))

        for k in range(sections):
            plan(k, [3 * (top - k) + 2 + gap for gap in (0, 2, 3, 6, 9)])
        plan("h", (1, 5, 10))
        clock = [0]

        def tick():
            for stage in marks.get(clock[0], []):
                stage()
            clock[0] += 1

        for k in reversed(range(sections)):
            by = unit * 2**k
            slot = k % 2
            above = cot_ref if k == top else grad
            if k:
                prefetch(k - 1)
            for copy in bring[k][0]:
                copy.wait()

            def inward(i, k=k, slot=slot, above=above):
                place = i * tile
                here = above[pl.ds(place, tile), :]
                back = times_transposed(here, held[k, pl.ds(3 * inner, inner), :])
                back = back * bend[slot][pl.ds(place, tile), :].astype(f32)
                pull[pl.ds(most + place, tile), :] = back.astype(bf16)
                sums[k, pl.ds(3 * inner, inner), :] += contract_rows(
                    active[slot][pl.ds(place, tile), :], here
                )

            for i in range(length // tile):
                inward(i)
                tick()
            for copy in bring[k][1]:
                copy.wait()

            def outward(i, carry, k=k, by=by, slot=slot, above=above):
                place = pl.multiple_of(i * tile, 16)
                there = hidden[slot][pl.ds(place, tile), :]
                value = None
                for j in range(3 if k < top else 2):
                    if k < top:
                        start = pl.multiple_of(most + place + (1 - j) * by, 16)
                        span = pl.ds(j * inner, inner)
                    else:
                        start = most + (1 - j) * by
                        span = pl.ds(pl.multiple_of((i + j) * inner, 16), inner)
                    piece = pull[pl.ds(start, tile), :]
                    sums[k, span, :] += contract_rows(piece, there)
                    if k:
                        term = jnp.dot(piece, held[k, span, :], preferred_element_type=f32)
                        value = term if value is None else value + term
                if k:
                    value = value * slope[slot][pl.ds(place, tile), :].astype(f32)
                    value = value + above[pl.ds(place, tile), :].astype(f32)
                    grad[pl.ds(place, tile), :] = value.astype(bf16)
                return carry

            lax.fori_loop(0, length // tile, outward, 0)
            tick()

        rounds = 0
        while any(stages.values()):
            for name in [0, *reversed(range(1, sections)), "h"]:
                if stages[name] and (name != "h" or rounds > 1):
                    stages[name].pop(0)()
            rounds += 1
        for copy in flight["r"]:
            copy.wait_recv()
        for k in range(sections):
            settle(k)
        for copy in sends:
            copy.wait_send()

    dma = pltpu.SemaphoreType.DMA

    def pair(count):
        return [dma((count,))] * 2

    long, thin = pltpu.VMEM((length, channels), bf16), pltpu.VMEM((length, inner), bf16)
    vmem = pl.BlockSpec(memory_space=pltpu.VMEM)
    return pl.pallas_call(
        kernel,
        out_shape=[
            jax.ShapeDtypeStruct((rows, channels), f32),
            jax.ShapeDtypeStruct(head_part.shape, f32),
        ],
        in_specs=[vmem, vmem] + [ANY] * (4 * sections),
        out_specs=[vmem, vmem],
        scratch_shapes=[long] * 4
        + [thin] * 4
        + [
            pltpu.VMEM(weights.shape, bf16),
            long,
            pltpu.VMEM((length + 2 * most, inner), bf16),
            pltpu.VMEM((sections, rows, channels), f32),
            dma((5 * sections,)),
            pltpu.VMEM((sections, part, channels), f32),
            pltpu.VMEM((sections, sections - 1, quarter, channels), bf16),
            pltpu.VMEM((sections, sections - 1, quarter, channels), bf16),
            pltpu.VMEM((sections, quarter, channels), f32),
            pltpu.VMEM((sections, quarter, channels), f32),
            pltpu.VMEM((sections, quarter, channels), f32),
            pltpu.VMEM((side, tracks), f32),
            pltpu.VMEM((side, tracks), f32),
            pltpu.VMEM((side, tracks), f32),
        ]
        + pair(sections)
        + pair(sections * (sections - 1))
        + pair(sections * levels)
        + pair(sections * levels)
        + [dma((sections,)), dma((sections,))]
        + pair(sections)
        + pair(1)
        + pair(levels)
        + pair(levels)
        + pair(levels + 1)
        + pair(sections * (zones - 1))
        + pair(sections * (zones - 1))
        + [dma((sections * zones,)), dma((sections * zones,))],
        compiler_params=pltpu.CompilerParams(
            collective_id=2, has_side_effects=True, vmem_limit_bytes=48 * 2**20
        ),
        name="backward_tower",
    )(head_part, cot, weights, *hidden, *slope, *active, *bend)


def finish(total, head_sum, split):
    def kernel(total_ref, head_ref, conv_out, proj_out, head_out, sems):
        copies = [
            pltpu.make_async_copy(total_ref.at[pl.ds(0, split)], conv_out, sems.at[0]),
            pltpu.make_async_copy(
                total_ref.at[pl.ds(split, total.shape[0] - split)], proj_out, sems.at[1]
            ),
            pltpu.make_async_copy(head_ref, head_out, sems.at[2]),
        ]
        for copy in copies:
            copy.start()
        for copy in copies:
            copy.wait()

    width = total.shape[1]
    return pl.pallas_call(
        kernel,
        out_shape=[
            jax.ShapeDtypeStruct((split, width), total.dtype),
            jax.ShapeDtypeStruct((total.shape[0] - split, width), total.dtype),
            jax.ShapeDtypeStruct(head_sum.shape, head_sum.dtype),
        ],
        in_specs=[pl.BlockSpec(memory_space=pltpu.VMEM)] * 2,
        out_specs=[ANY] * 3,
        scratch_shapes=[pltpu.SemaphoreType.DMA((3,))],
        compiler_params=pltpu.CompilerParams(vmem_limit_bytes=8 * 2**20),
        name="finish",
    )(total, head_sum)


def plain_body(bases, targets, stem_weight, conv_weight, proj_weight, head_weight):
    sections = lax.axis_size("section")
    seqs = lax.axis_size("seq")
    section_number = lax.axis_index("section")
    batches, row_count, bin_width = bases.shape
    channels = stem_weight.shape[1]
    length = row_count * seqs
    factor = 1.0 / math.sqrt(batches * lax.axis_size("dp") * length)
    unit = length // 2**sections
    local_q = row_count // unit
    blocks = length // unit
    columns = batches * unit // (seqs * sections)

    conv_all = lax.all_gather(conv_weight, "section", axis=0, tiled=True)
    proj_all = lax.all_gather(proj_weight, "section", axis=0, tiled=True)

    def to_chains(value):
        value = lax.all_to_all(value, "seq", split_axis=1, concat_axis=0, tiled=True)
        return value.reshape(blocks * columns, value.shape[-1])

    own = bases.reshape(batches, local_q, unit, bin_width).transpose(1, 0, 2, 3)
    own = own.reshape(local_q, seqs, sections, columns, bin_width)
    own = lax.dynamic_index_in_dim(own, section_number, 2, keepdims=False)
    picked = to_chains(own.astype(jnp.bfloat16))
    onehot = jnp.concatenate([(picked == c).astype(jnp.bfloat16) for c in range(4)], 1)
    stem = stem_weight.reshape(bin_width, 4, channels).transpose(1, 0, 2).reshape(-1, channels)
    state = jnp.dot(onehot, stem, preferred_element_type=jnp.float32).astype(jnp.bfloat16)

    saved = []
    for layer in range(sections):
        by = columns * 2**layer
        taps = conv_all[layer].reshape(-1, conv_all.shape[-1])
        hidden = gelu_value(state.astype(jnp.float32)).astype(jnp.bfloat16)
        wide = jnp.concatenate([shift_rows(hidden, by), hidden, shift_rows(hidden, -by)], 1)
        inner_sum = jnp.dot(wide, taps, preferred_element_type=jnp.float32)
        active = gelu_value(inner_sum).astype(jnp.bfloat16)
        update = jnp.dot(active, proj_all[layer], preferred_element_type=jnp.float32)
        saved.append((state, wide, inner_sum, active))
        state = (state.astype(jnp.float32) + update).astype(jnp.bfloat16)

    lifted = gelu_value(state.astype(jnp.float32)).astype(jnp.bfloat16)
    lifted = lifted.reshape(seqs, local_q, 1, columns, channels)
    lifted = lax.all_to_all(lifted, "seq", split_axis=0, concat_axis=2, tiled=True)
    lifted = lifted.reshape(local_q, seqs, 1, columns, channels)
    lifted = lax.all_gather(lifted, "section", axis=2, tiled=True)
    lifted = lifted.reshape(local_q, batches, unit, channels).transpose(1, 0, 2, 3)
    lifted = lifted.reshape(batches * row_count, channels)

    logits = jnp.dot(lifted, head_weight, preferred_element_type=jnp.float32)
    counts = targets.reshape(batches * row_count, targets.shape[2]).astype(jnp.float32)
    slope = ((jnp.exp(logits) - counts) * factor).astype(jnp.bfloat16)
    head_sum = lax.psum(contract_rows(lifted, slope), ("seq", "dp"))
    lift_part = times_transposed(slope, head_weight)

    lift_part = lift_part.reshape(batches, local_q, unit, channels).transpose(1, 0, 2, 3)
    lift_part = lift_part.reshape(local_q, seqs, sections, columns, channels)
    lift_part = lax.psum_scatter(lift_part, "section", scatter_dimension=2, tiled=True)
    lift_grad = to_chains(lift_part.reshape(local_q, seqs, columns, channels))


    grad = (lift_grad * gelu_slope(state.astype(jnp.float32))).astype(jnp.bfloat16)
    parts = []
    for layer in reversed(range(sections)):
        by = columns * 2**layer
        start_state, wide, inner_sum, active = saved[layer]
        kernel = conv_all[layer]
        proj_part = contract_rows(active, grad)
        active_grad = times_transposed(grad, proj_all[layer])
        inner_grad = (active_grad * gelu_slope(inner_sum)).astype(jnp.bfloat16)
        parts.append(jnp.concatenate([contract_rows(inner_grad, wide), proj_part], 1))
        wide_grad = jnp.concatenate(
            [shift_rows(inner_grad, -by), inner_grad, shift_rows(inner_grad, by)], 1
        )
        turned = kernel.transpose(0, 2, 1).reshape(-1, channels)
        hidden_grad = jnp.dot(wide_grad, turned, preferred_element_type=jnp.float32)
        grad = (
            grad.astype(jnp.float32) + hidden_grad * gelu_slope(start_state.astype(jnp.float32))
        ).astype(jnp.bfloat16)
    parts = jnp.stack(parts[::-1])
    total = lax.psum_scatter(parts, "section", scatter_dimension=0, tiled=True)
    total = lax.psum(total[0], ("seq", "dp"))
    taps_width = total.shape[1] - channels
    conv_sum = total[:, :taps_width].T.reshape(conv_weight.shape)
    return conv_sum, total[:, taps_width:][None], head_sum


def paired_body(bases, targets, stem_weight, conv_weight, proj_weight, head_weight):
    sections = lax.axis_size("section")
    zones = lax.axis_size("dp")
    batches, half, bin_width = bases.shape
    channels = stem_weight.shape[1]
    inner = proj_weight.shape[1]
    length = batches * half
    unit = length // 2**sections
    factor = 1.0 / math.sqrt(batches * zones * length)
    taps = conv_weight[0].transpose(0, 2, 1).reshape(3 * inner, channels)
    top, weights, hidden, slope, active, bend = forward_tower(
        bases, stem_weight, taps, proj_weight[0], sections, unit
    )
    head_part, cot = head(top, targets, head_weight, factor)
    cot = cot.reshape(length, channels)
    total, head_sum = backward_tower(
        head_part, cot, weights, hidden, slope, active, bend, sections, zones, unit
    )
    conv_sum, proj_sum, head_sum = finish(total, head_sum, 3 * inner)
    conv_sum = conv_sum.reshape(3, inner, channels).transpose(0, 2, 1)
    return conv_sum[None], proj_sum[None], head_sum


def body(bases, targets, stem_weight, conv_weight, proj_weight, head_weight):
    sections, zones = lax.axis_size("section"), lax.axis_size("dp")
    batches, half = bases.shape[:2]
    inner = proj_weight.shape[1]
    unit = batches * half // 2**sections
    paired = lax.axis_size("seq") == 2 and batches == 2 and zones > 1 and sections > 1
    paired = paired and unit % 16 == 0 and half % 16 == 0 and inner % 16 == 0
    paired = paired and (2 * inner) % (16 * sections) == 0
    paired = paired and (2 * inner) % (8 * sections * zones) == 0
    paired = paired and zones & (zones - 1) == 0
    paired = paired and stem_weight.shape[1] % (16 * zones) == 0
    run = paired_body if paired else plain_body
    return run(bases, targets, stem_weight, conv_weight, proj_weight, head_weight)


def solution(mesh):
    in_specs = (
        P("dp", "seq", None),
        P("dp", "seq", "section"),
        P(),
        P("section", None, None, None),
        P("section", None, None),
        P(None, "section"),
    )
    out_specs = (P("section", None, None, None), P("section", None, None), P(None, "section"))
    return jax.shard_map(body, mesh=mesh, in_specs=in_specs, out_specs=out_specs, check_vma=False)
```

```python
import math

import jax
import jax.numpy as jnp
from jax import lax
from jax.experimental import pallas as pl
from jax.experimental.pallas import tpu as pltpu
from jax.sharding import PartitionSpec as P

SQRT_TWO_OVER_PI = 0.7978845608028654
CUBIC_TERM = 0.044715


def gelu_value(inputs):
    return (
        0.5
        * inputs
        * (1.0 + jnp.tanh(SQRT_TWO_OVER_PI * (inputs + CUBIC_TERM * inputs * inputs * inputs)))
    )


def gelu_slope(inputs):
    tangent = jnp.tanh(SQRT_TWO_OVER_PI * (inputs + CUBIC_TERM * inputs * inputs * inputs))
    return 0.5 * (1.0 + tangent) + 0.5 * inputs * (1.0 - tangent * tangent) * SQRT_TWO_OVER_PI * (
        1.0 + 3.0 * CUBIC_TERM * inputs * inputs
    )


def contract_rows(left_side, right_side):
    return lax.dot_general(
        left_side, right_side, (((0,), (0,)), ((), ())), preferred_element_type=jnp.float32
    )


def times_transposed(left_side, right_side):
    return lax.dot_general(
        left_side, right_side, (((1,), (1,)), ((), ())), preferred_element_type=jnp.float32
    )


def shift_rows(value, by):
    if abs(by) >= value.shape[0]:
        return jnp.zeros_like(value)
    pad = jnp.zeros((abs(by),) + value.shape[1:], value.dtype)
    if by > 0:
        return jnp.concatenate([pad, value[:-by]], 0)
    return jnp.concatenate([value[-by:], pad], 0)


MESH = pl.DeviceIdType.MESH
ANY = pl.BlockSpec(memory_space=pl.ANY)


def greet(peers):
    barrier = pltpu.get_barrier_semaphore()
    for peer in peers:
        pl.semaphore_signal(barrier, inc=1, device_id=peer, device_id_type=MESH)
    pl.semaphore_wait(barrier, len(peers))


def remote(src, dst, send, recv, peer):
    return pltpu.make_async_remote_copy(
        src_ref=src, dst_ref=dst, send_sem=send, recv_sem=recv, device_id=peer, device_id_type=MESH
    )


def both_gelu(inputs):
    square = inputs * inputs
    tangent = jnp.tanh(
        inputs * (SQRT_TWO_OVER_PI + (SQRT_TWO_OVER_PI * CUBIC_TERM) * square)
    )
    gate = 0.5 + 0.5 * tangent
    value = inputs * gate
    inside = 2.0 * SQRT_TWO_OVER_PI + (6.0 * SQRT_TWO_OVER_PI * CUBIC_TERM) * square
    return value, gate + value * (1.0 - gate) * inside


def tile_of(rows):
    for size in (512, 384, 256, 192, 128, 96, 64, 48, 32, 16):
        if rows % size == 0:
            return size
    return rows


def forward_tower(bases, stem, taps, proj, sections, unit):
    seqs, half, width = bases.shape
    length = seqs * half
    channels = stem.shape[1]
    inner = proj.shape[0]
    rows = taps.shape[0] + inner
    part = rows // 2
    tile = tile_of(half)
    steps = half // tile
    team = 3 if steps % 3 == 0 else 1
    shifts = [unit * 2**k for k in range(sections)]

    def kernel(*refs):
        bases_ref, stem_ref, taps_ref, proj_ref = refs[:4]
        refs = refs[4:]
        top_ref, weights_ref = refs[:2]
        hidden_out, slope_out = refs[2 : 2 + sections], refs[2 + sections : 1 + 2 * sections]
        refs = refs[1 + 2 * sections :]
        active_out, bend_out = refs[:sections], refs[sections : 2 * sections]
        refs = refs[2 * sections :]
        full, held, turned, state, sorted_stem = refs[:5]
        refs = refs[5:]
        hidden, slope = refs[:sections], refs[sections : 2 * sections - 1]
        refs = refs[2 * sections - 1 :]
        active, bend = refs[:sections], refs[sections : 2 * sections]
        refs = refs[2 * sections :]
        bsend, brecv, send, recv, send2, recv2, tsend, trecv, own_sem, out_sem = refs

        s, c = lax.axis_index("section"), lax.axis_index("seq")
        partner = {"section": s, "seq": 1 - c}
        peers = [{"section": lax.rem(s + k, sections), "seq": c} for k in range(1, sections)]
        loads = [
            pltpu.make_async_copy(bases_ref.at[c], full.at[c], own_sem.at[0]),
            pltpu.make_async_copy(
                taps_ref, held.at[s, pl.ds(0, taps.shape[0])], own_sem.at[1]
            ),
            pltpu.make_async_copy(
                proj_ref, held.at[s, pl.ds(taps.shape[0], inner)], own_sem.at[2]
            ),
        ]
        for copy in loads:
            copy.start()
        greet(peers + [partner])
        across = remote(bases_ref.at[1 - c], full.at[c], bsend, brecv, partner)
        across.start()
        loads[1].wait()
        loads[2].wait()
        mine = held.at[s, pl.ds(pl.multiple_of(c * part, 16), part)]
        first = []
        for k, peer in enumerate(peers):
            first.append(remote(mine, mine, send.at[k], recv.at[k], peer))
            first[-1].start()
        for k in range(sections - 1):
            edge = jnp.zeros((shifts[k], channels), jnp.bfloat16)
            hidden[k][pl.ds(0, shifts[k]), :] = edge
            hidden[k][pl.ds(shifts[k] + length, shifts[k]), :] = edge

        across_rows = lax.broadcasted_iota(jnp.int32, (4 * width, 4 * width), 0)
        across_columns = lax.broadcasted_iota(jnp.int32, (4 * width, 4 * width), 1)
        place_of = 4 * lax.rem(across_rows, width) + across_rows // width
        chosen = (across_columns == place_of).astype(jnp.bfloat16)
        sorted_stem[...] = jnp.dot(
            chosen, stem_ref[...], preferred_element_type=jnp.float32
        ).astype(jnp.bfloat16)

        def begin(number):
            def step(i, carry):
                at = i * tile
                codes = full[number, pl.ds(pl.multiple_of(at, 16), tile), :]
                onehot = jnp.concatenate(
                    [(codes == k).astype(jnp.bfloat16) for k in range(4)], 1
                )
                start = jnp.dot(onehot, sorted_stem[...], preferred_element_type=jnp.float32)
                start = start.astype(jnp.bfloat16)
                place = pl.multiple_of(number * half + at, 16)
                state[pl.ds(place, tile), :] = start
                value = gelu_value(start.astype(jnp.float32)).astype(jnp.bfloat16)
                hidden[0][pl.ds(pl.multiple_of(shifts[0] + place, 16), tile), :] = value
                return carry

            lax.fori_loop(0, steps, step, 0)

        loads[0].wait()
        begin(c)
        across.wait_recv()
        begin(1 - c)

        second = []
        for k in range(sections - 1):
            first[k].wait_recv()
            source = lax.rem(s + sections - 1 - k, sections)
            piece = held.at[source, pl.ds(pl.multiple_of(c * part, 16), part)]
            second.append(remote(piece, piece, send2.at[k], recv2.at[k], partner))
            second[-1].start()
        for copy in second:
            copy.wait_recv()

        outs = []

        def keep(src, dst):
            outs.append(pltpu.make_async_copy(src, dst, out_sem.at[len(outs)]))
            outs[-1].start()

        keep(held, weights_ref)
        keep(hidden[0].at[pl.ds(shifts[0], length)], hidden_out[0])

        for k in range(sections):
            by = shifts[k]
            for j in range(3):
                tap = held[k, pl.ds(j * inner, inner), :]
                turned[pl.ds(j * channels, channels), :] = tap.T

            def group(places, lead, width, k=k, by=by):
                weight = turned[pl.ds(pl.multiple_of(lead * channels, 16), width * channels), :]
                inners = []
                for place in places:
                    wide = jnp.concatenate(
                        [
                            hidden[k][pl.ds(pl.multiple_of(place + (lead + j) * by, 16), tile), :]
                            for j in range(width)
                        ],
                        1,
                    )
                    inners.append(
                        jnp.dot(wide, weight, preferred_element_type=jnp.float32)
                    )
                olds = [state[pl.ds(place, tile), :].astype(jnp.float32) for place in places]
                results = []
                for inner_sum, old in zip(inners, olds):
                    value, bent = both_gelu(inner_sum)
                    value, bent = value.astype(jnp.bfloat16), bent.astype(jnp.bfloat16)
                    update = jnp.dot(
                        value,
                        held[k, pl.ds(3 * inner, inner), :],
                        preferred_element_type=jnp.float32,
                    )
                    results.append((value, bent, (old + update).astype(jnp.bfloat16)))
                for place, (value, bent, _) in zip(places, results):
                    active[k][pl.ds(place, tile), :] = value
                    bend[k][pl.ds(place, tile), :] = bent
                return [new for _, _, new in results]

            def spots(i, base):
                return [
                    pl.multiple_of(base + (i * team + g) * tile, 16) for g in range(team)
                ]

            if k < sections - 1:

                def step(i, carry, k=k):
                    places = spots(i, 0)
                    news = group(places, 0, 3)
                    pairs = [both_gelu(new.astype(jnp.float32)) for new in news]
                    for place, new, (value, bent) in zip(places, news, pairs):
                        state[pl.ds(place, tile), :] = new
                        ahead = pl.multiple_of(shifts[k + 1] + place, 16)
                        hidden[k + 1][pl.ds(ahead, tile), :] = value.astype(jnp.bfloat16)
                        slope[k][pl.ds(place, tile), :] = bent.astype(jnp.bfloat16)
                    return carry

                lax.fori_loop(0, length // (tile * team), step, 0)
                keep(hidden[k + 1].at[pl.ds(shifts[k + 1], length)], hidden_out[k + 1])
                keep(slope[k], slope_out[k])
            else:

                def finish_half(number):
                    def step(i, carry):
                        places = spots(i, number * half)
                        for place, new in zip(places, group(places, 1 - number, 2)):
                            state[pl.ds(place, tile), :] = new
                        return carry

                    lax.fori_loop(0, steps // team, step, 0)

                finish_half(1 - c)
                theirs = state.at[pl.ds(pl.multiple_of((1 - c) * half, 16), half)]
                last = remote(theirs, top_ref.at[c], tsend, trecv, partner)
                last.start()
                finish_half(c)
                top_ref[c] = state[pl.ds(pl.multiple_of(c * half, 16), half), :]
            keep(active[k], active_out[k])
            keep(bend[k], bend_out[k])
        for copy in outs:
            copy.wait()
        last.wait()
        across.wait_send()
        for copy in first + second:
            copy.wait_send()

    bf16 = jnp.bfloat16
    long = jax.ShapeDtypeStruct((length, channels), bf16)
    thin = jax.ShapeDtypeStruct((length, inner), bf16)
    dma = pltpu.SemaphoreType.DMA
    copies = 4 * sections
    out = pl.pallas_call(
        kernel,
        out_shape=[
            jax.ShapeDtypeStruct((seqs, half, channels), bf16),
            jax.ShapeDtypeStruct((sections, rows, channels), bf16),
        ]
        + [long] * (2 * sections - 1)
        + [thin] * (2 * sections),
        in_specs=[ANY, pl.BlockSpec(memory_space=pltpu.VMEM), ANY, ANY],
        out_specs=[pl.BlockSpec(memory_space=pltpu.VMEM)] + [ANY] * (4 * sections),
        scratch_shapes=[
            pltpu.VMEM((seqs, half, width), jnp.int32),
            pltpu.VMEM((sections, rows, channels), bf16),
            pltpu.VMEM((3 * channels, inner), bf16),
            pltpu.VMEM((length, channels), bf16),
            pltpu.VMEM(stem.shape, bf16),
        ]
        + [pltpu.VMEM((length + 2 * by, channels), bf16) for by in shifts]
        + [pltpu.VMEM((length, channels), bf16)] * (sections - 1)
        + [pltpu.VMEM((length, inner), bf16)] * (2 * sections)
        + [dma, dma]
        + [dma((sections - 1,))] * 4
        + [dma, dma, dma((3,)), dma((copies,))],
        compiler_params=pltpu.CompilerParams(
            collective_id=0, has_side_effects=True, vmem_limit_bytes=54 * 2**20
        ),
        name="forward_tower",
    )(bases, stem, taps, proj)
    top, weights = out[:2]
    hidden, slope = out[2 : 2 + sections], out[2 + sections : 1 + 2 * sections]
    active = out[1 + 2 * sections : 1 + 3 * sections]
    bend = out[1 + 3 * sections :]
    return top, weights, hidden, slope, active, bend


def head(top, targets, head_weight, factor):
    seqs, half, channels = top.shape
    tracks = head_weight.shape[1]
    tile = tile_of(half)
    if half % 512 == 0:
        tile = 512
    steps = half // tile

    def kernel(
        top_ref, targets_ref, weight_ref, grad_ref, cot_ref, counts, stage, load, send, recv
    ):
        s, c = lax.axis_index("section"), lax.axis_index("seq")
        partner = {"section": s, "seq": 1 - c}
        loads = []
        for n, b in enumerate((1 - c, c)):
            for i in range(steps):
                loads.append(
                    pltpu.make_async_copy(
                        targets_ref.at[b, pl.ds(i * tile, tile)],
                        counts.at[n * steps + i],
                        load.at[n * steps + i],
                    )
                )
                loads[-1].start()
        greet([partner])
        grad_ref[...] = jnp.zeros_like(grad_ref)

        def run(b, n, store):
            def step(i, carry):
                at = pl.multiple_of(i * tile, 16)
                pltpu.make_async_copy(
                    targets_ref.at[b, pl.ds(at, tile)], counts.at[n + i], load.at[n + i]
                ).wait()
                value, bent = both_gelu(top_ref[b, pl.ds(at, tile), :].astype(jnp.float32))
                lifted = value.astype(jnp.bfloat16)
                logits = jnp.dot(lifted, weight_ref[...], preferred_element_type=jnp.float32)
                drop = jnp.exp(logits) - counts[n + i].astype(jnp.float32)
                drop = (drop * factor).astype(jnp.bfloat16)
                grad_ref[...] += contract_rows(lifted, drop)
                lift = times_transposed(drop, weight_ref[...])
                store(at, (lift * bent).astype(jnp.bfloat16))
                return carry

            lax.fori_loop(0, steps, step, 0)

        def away(at, value):
            stage[pl.ds(at, tile), :] = value

        def here(at, value):
            cot_ref[c, pl.ds(at, tile), :] = value

        run(1 - c, 0, away)
        copy = remote(stage, cot_ref.at[c], send, recv, partner)
        copy.start()
        run(c, steps, here)
        copy.wait()

    vmem = pl.BlockSpec(memory_space=pltpu.VMEM)
    dma = pltpu.SemaphoreType.DMA
    return pl.pallas_call(
        kernel,
        out_shape=[
            jax.ShapeDtypeStruct((channels, tracks), jnp.float32),
            jax.ShapeDtypeStruct(top.shape, jnp.bfloat16),
        ],
        in_specs=[vmem, ANY, vmem],
        out_specs=[vmem, vmem],
        scratch_shapes=[
            pltpu.VMEM((seqs * steps, tile, tracks), jnp.int32),
            pltpu.VMEM((half, channels), jnp.bfloat16),
            dma((seqs * steps,)),
            dma,
            dma,
        ],
        compiler_params=pltpu.CompilerParams(
            collective_id=1, has_side_effects=True, vmem_limit_bytes=48 * 2**20
        ),
        name="head",
    )(top, targets, head_weight)


def backward_tower(head_part, cot, weights, hidden, slope, active, bend, sections, zones, unit):
    length, channels = hidden[0].shape
    inner = active[0].shape[1]
    rows = weights.shape[1]
    part = rows // 2
    quarter = part // sections
    levels = zones.bit_length() - 1
    tracks = head_part.shape[1]
    side = head_part.shape[0] // 2
    tile = length // 2
    most = unit * 2 ** (sections - 1)
    f32, bf16 = jnp.float32, jnp.bfloat16

    def kernel(*refs):
        head_ref, cot_ref, weights_ref = refs[:3]
        refs = refs[3:]
        hidden_in, slope_in = refs[:sections], refs[sections : 2 * sections - 1]
        refs = refs[2 * sections - 1 :]
        active_in, bend_in = refs[:sections], refs[sections : 2 * sections]
        refs = refs[2 * sections :]
        out, head_out = refs[:2]
        hidden, slope, active, bend = refs[2:4], refs[4:6], refs[6:8], refs[8:10]
        held, grad, pull, sums, load = refs[10:15]
        met, wire, came, total, zcame, final = refs[15:21]
        hmet, hsum, hcame = refs[21:24]
        sems = refs[24:]

        s, c, d = (lax.axis_index(name) for name in ("section", "seq", "dp"))
        partner = {"section": s, "seq": 1 - c, "dp": d}
        order = [lax.rem(s + k, sections) for k in range(1, sections)]
        across = [{"section": o, "seq": c, "dp": d} for o in order]
        bits = [lax.rem(d // 2**t, 2) for t in range(levels)]
        along = [
            {"section": s, "seq": c, "dp": d + 2**t * (1 - 2 * bits[t])} for t in range(levels)
        ]
        floors = [lax.rem(d + n, zones) for n in range(1, zones)]
        lifts = [{"section": s, "seq": c, "dp": z} for z in floors]
        count = [0]

        def fetch(src, dst):
            copy = pltpu.make_async_copy(src, dst, load.at[count[0]])
            count[0] += 1
            copy.start()
            return copy

        bring = {}

        def prefetch(k):
            slot = k % 2
            early = [
                fetch(weights_ref.at[k], held.at[k]),
                fetch(bend_in[k], bend[slot]),
                fetch(active_in[k], active[slot]),
            ]
            late = [fetch(hidden_in[k], hidden[slot])]
            if k:
                late.append(fetch(slope_in[k - 1], slope[slot]))
            bring[k] = (early, late)

        prefetch(sections - 1)
        greet([partner] + across + lifts)

        sends = []

        def launch(src, dst, pair, index, peer):
            copy = remote(src, dst, sems[2 * pair].at[index], sems[2 * pair + 1].at[index], peer)
            copy.start()
            sends.append(copy)
            return copy

        def block(base, size, number):
            return pl.ds(pl.multiple_of(base + number * size, 8), size)

        flight = {}

        def swap(k):
            far = sums.at[k, block(0, part, 1 - c)]
            flight[k] = [launch(far, met.at[k], 0, k, partner)]

        def spread(k):
            flight[k][0].wait_recv()
            flight[k] = []

            def both(o):
                return met[k, block(0, quarter, o), :] + sums[k, block(c * part, quarter, o), :]

            for n, o in enumerate(order):
                wire[k, n] = both(o).astype(bf16)
                flight[k].append(
                    launch(wire.at[k, n], came.at[k, n], 1, k * (sections - 1) + n, across[n])
                )
            total[k] = both(s)

        def kept(span, t):
            base = 0
            for step in range(t):
                base = base + bits[step] * (span >> (step + 1))
            return base

        def landing(span, t):
            return pl.ds(span - (span >> t), span >> (t + 1))

        def climb(k, t):
            for copy in flight[k]:
                copy.wait_recv()
            if t == 0:
                value = total[k]
                for n in range(sections - 1):
                    value = value + came[k, n].astype(f32)
                total[k] = value
            else:
                mine = block(kept(quarter, t), quarter >> t, 0)
                total[k, mine, :] = total[k, mine, :] + zcame[k, landing(quarter, t - 1), :]
            size = quarter >> (t + 1)
            away = block(kept(quarter, t), size, 1 - bits[t])
            flight[k] = [
                launch(
                    total.at[k, away],
                    zcame.at[k, landing(quarter, t)],
                    2,
                    k * levels + t,
                    along[t],
                )
            ]

        def level(k, t):
            for copy in flight[k]:
                copy.wait_recv()
            mine = block(kept(quarter, t + 1), quarter >> (t + 1), 0)
            if t == levels - 1:
                final[k, mine, :] = total[k, mine, :] + zcame[k, landing(quarter, t), :]
            piece = final.at[k, mine]
            flight[k] = [launch(piece, piece, 3, k * levels + t, along[t])]

        strip = quarter // zones
        brisk = 0

        def climb_at_once(k):
            for copy in flight[k]:
                copy.wait_recv()
            value = total[k]
            for n in range(sections - 1):
                value = value + came[k, n].astype(f32)
            total[k] = value
            flight[k] = [
                launch(
                    total.at[k, block(0, strip, z)],
                    zcame.at[k, pl.ds(n * strip, strip)],
                    10,
                    k * (zones - 1) + n,
                    lifts[n],
                )
                for n, z in enumerate(floors)
            ]

        def level_at_once(k):
            for copy in flight[k]:
                copy.wait_recv()
            value = total[k, block(0, strip, d), :]
            for n in range(zones - 1):
                value = value + zcame[k, pl.ds(n * strip, strip), :]
            final[k, block(0, strip, d), :] = value
            piece = final.at[k, block(0, strip, d)]
            flight[k] = [launch(piece, piece, 11, k * (zones - 1) + n, peer) for n, peer in enumerate(lifts)]
            strip_home(k, d)

        def home_strip(k, z):
            owner = {"section": k, "seq": c, "dp": d}
            index = lax.rem(s + 2 * sections - k - 1, sections) * zones + z
            place = out.at[block(c * part + s * quarter, strip, z)]
            return remote(
                final.at[k, block(0, strip, z)],
                place,
                sems[24].at[k * zones + z],
                sems[25].at[index],
                owner,
            )

        def strip_home(k, z):
            @pl.when(s != k)
            def _():
                home_strip(k, z).start()

        def deliver_strips(k):
            for n, copy in enumerate(flight[k]):
                copy.wait_recv()
                strip_home(k, lax.rem(d + zones - 1 - n, zones))

            @pl.when(s == k)
            def _():
                out[block(c * part, quarter, s), :] = final[k]
                relay(0, s).start()

        def home(k):
            owner = {"section": k, "seq": c, "dp": d}
            index = lax.rem(s + 2 * sections - k - 1, sections)
            place = out.at[block(c * part, quarter, s)]
            return remote(final.at[k], place, sems[8].at[k], sems[9].at[index], owner)

        def deliver(k):
            for copy in flight[k]:
                copy.wait_recv()

            @pl.when(s != k)
            def _():
                home(k).start()

            @pl.when(s == k)
            def _():
                out[block(c * part, quarter, s), :] = final[k]
                relay(0, s).start()

        def relay(n, source):
            piece = out.at[block(c * part, quarter, source)]
            return remote(piece, piece, sems[10].at[n], sems[11].at[n], partner)

        def hand(k):
            @pl.when(s == k)
            def _():
                for n, o in enumerate(order):
                    if k > brisk:
                        piece = out.at[block(c * part, quarter, o)]
                        remote(
                            final.at[k], piece, sems[8].at[k], sems[9].at[n], across[n]
                        ).wait_recv()
                    else:
                        for z in range(zones):
                            piece = out.at[block(c * part + o * quarter, strip, z)]
                            remote(
                                final.at[k, block(0, strip, z)],
                                piece,
                                sems[24].at[k * zones + z],
                                sems[25].at[n * zones + z],
                                across[n],
                            ).wait_recv()
                    relay(n + 1, o).start()

        def settle(k):
            @pl.when(s != k)
            def _():
                if k > brisk:
                    home(k).wait_send()
                else:
                    for z in range(zones):
                        home_strip(k, z).wait_send()

            @pl.when(s == k)
            def _():
                for n, o in enumerate([s] + order):
                    relay(n, o).wait()

        def head_swap():
            far = head_ref.at[block(0, side, 1 - c)]
            flight["h"] = [launch(far, hmet, 6, 0, partner)]

        def head_climb(t):
            flight["h"][0].wait_recv()
            if t == 0:
                hsum[...] = hmet[...] + head_ref[block(0, side, c), :]
            else:
                mine = block(kept(side, t), side >> t, 0)
                hsum[mine, :] = hsum[mine, :] + hcame[landing(side, t - 1), :]
            away = block(kept(side, t), side >> (t + 1), 1 - bits[t])
            flight["h"] = [
                launch(hsum.at[away], hcame.at[landing(side, t)], 7, t, along[t])
            ]

        flight["r"] = []

        def pass_on(start, size):
            piece = head_out.at[block(c * side + start, size, 0)]
            flight["r"].append(launch(piece, piece, 9, len(flight["r"]), partner))

        def other(span, t):
            return kept(span, t) + (1 - bits[t]) * (span >> (t + 1))

        def head_level(t):
            flight["h"][0].wait_recv()
            start, size = kept(side, t + 1), side >> (t + 1)
            place = block(c * side + start, size, 0)
            if t == levels - 1:
                mine = block(start, size, 0)
                head_out[place, :] = hsum[mine, :] + hcame[landing(side, t), :]
                pass_on(start, size)
            else:
                pass_on(other(side, t + 1), side >> (t + 2))
            piece = head_out.at[place]
            flight["h"] = [launch(piece, piece, 8, t, along[t])]

        def head_hand():
            flight["h"][0].wait_recv()
            pass_on(other(side, 0), side // 2)

        head_swap()
        pull[pl.ds(0, most), :] = jnp.zeros((most, inner), bf16)
        pull[pl.ds(most + length, most), :] = jnp.zeros((most, inner), bf16)
        sums[...] = jnp.zeros_like(sums)

        top = sections - 1
        stages = {}
        for k in range(sections):
            line = [lambda k=k: swap(k), lambda k=k: spread(k)]
            if k > brisk:
                line += [lambda k=k, t=t: climb(k, t) for t in range(levels)]
                line += [lambda k=k, t=t: level(k, t) for t in reversed(range(levels))]
                line.append(lambda k=k: deliver(k))
            else:
                for stage in (climb_at_once, level_at_once, deliver_strips):
                    line.append(lambda k=k, stage=stage: stage(k))
            stages[k] = line + [lambda k=k: hand(k)]
        line = [lambda t=t: head_climb(t) for t in range(levels)]
        line += [lambda t=t: head_level(t) for t in reversed(range(levels))]
        stages["h"] = line + [head_hand]
        marks = {}

        def plan(name, ticks):
            for at in ticks:
                if at <= 3 * sections - 1 and stages[name]:
                    marks.setdefault(at, []).append(stages[name].pop(0))

        for k in range(sections):
            plan(k, [3 * (top - k) + 2 + gap for gap in (0, 2, 3, 6)])
        plan("h", (1, 5, 10))
        clock = [0]

        def tick():
            for stage in marks.get(clock[0], []):
                stage()
            clock[0] += 1

        for k in reversed(range(sections)):
            by = unit * 2**k
            slot = k % 2
            above = cot_ref if k == top else grad
            if k:
                prefetch(k - 1)
            for copy in bring[k][0]:
                copy.wait()

            def inward(i, k=k, slot=slot, above=above):
                place = i * tile
                here = above[pl.ds(place, tile), :]
                back = times_transposed(here, held[k, pl.ds(3 * inner, inner), :])
                back = back * bend[slot][pl.ds(place, tile), :].astype(f32)
                pull[pl.ds(most + place, tile), :] = back.astype(bf16)
                sums[k, pl.ds(3 * inner, inner), :] += contract_rows(
                    active[slot][pl.ds(place, tile), :], here
                )

            for i in range(length // tile):
                inward(i)
                tick()
            for copy in bring[k][1]:
                copy.wait()

            def outward(i, carry, k=k, by=by, slot=slot, above=above):
                place = pl.multiple_of(i * tile, 16)
                there = hidden[slot][pl.ds(place, tile), :]
                value = None
                for j in range(3 if k < top else 2):
                    if k < top:
                        start = pl.multiple_of(most + place + (1 - j) * by, 16)
                        span = pl.ds(j * inner, inner)
                    else:
                        start = most + (1 - j) * by
                        span = pl.ds(pl.multiple_of((i + j) * inner, 16), inner)
                    piece = pull[pl.ds(start, tile), :]
                    sums[k, span, :] += contract_rows(piece, there)
                    if k:
                        term = jnp.dot(piece, held[k, span, :], preferred_element_type=f32)
                        value = term if value is None else value + term
                if k:
                    value = value * slope[slot][pl.ds(place, tile), :].astype(f32)
                    value = value + above[pl.ds(place, tile), :].astype(f32)
                    grad[pl.ds(place, tile), :] = value.astype(bf16)
                return carry

            lax.fori_loop(0, length // tile, outward, 0)
            tick()

        rounds = 0
        while any(stages.values()):
            for name in [0, *reversed(range(1, sections)), "h"]:
                if stages[name] and (name != "h" or rounds > 1):
                    stages[name].pop(0)()
            rounds += 1
        for copy in flight["r"]:
            copy.wait_recv()
        for k in range(sections):
            settle(k)
        for copy in sends:
            copy.wait_send()

    dma = pltpu.SemaphoreType.DMA

    def pair(count):
        return [dma((count,))] * 2

    long, thin = pltpu.VMEM((length, channels), bf16), pltpu.VMEM((length, inner), bf16)
    vmem = pl.BlockSpec(memory_space=pltpu.VMEM)
    return pl.pallas_call(
        kernel,
        out_shape=[
            jax.ShapeDtypeStruct((rows, channels), f32),
            jax.ShapeDtypeStruct(head_part.shape, f32),
        ],
        in_specs=[vmem, vmem] + [ANY] * (4 * sections),
        out_specs=[vmem, vmem],
        scratch_shapes=[long] * 4
        + [thin] * 4
        + [
            pltpu.VMEM(weights.shape, bf16),
            long,
            pltpu.VMEM((length + 2 * most, inner), bf16),
            pltpu.VMEM((sections, rows, channels), f32),
            dma((5 * sections,)),
            pltpu.VMEM((sections, part, channels), f32),
            pltpu.VMEM((sections, sections - 1, quarter, channels), bf16),
            pltpu.VMEM((sections, sections - 1, quarter, channels), bf16),
            pltpu.VMEM((sections, quarter, channels), f32),
            pltpu.VMEM((sections, quarter, channels), f32),
            pltpu.VMEM((sections, quarter, channels), f32),
            pltpu.VMEM((side, tracks), f32),
            pltpu.VMEM((side, tracks), f32),
            pltpu.VMEM((side, tracks), f32),
        ]
        + pair(sections)
        + pair(sections * (sections - 1))
        + pair(sections * levels)
        + pair(sections * levels)
        + [dma((sections,)), dma((sections,))]
        + pair(sections)
        + pair(1)
        + pair(levels)
        + pair(levels)
        + pair(levels + 1)
        + pair(sections * (zones - 1))
        + pair(sections * (zones - 1))
        + [dma((sections * zones,)), dma((sections * zones,))],
        compiler_params=pltpu.CompilerParams(
            collective_id=2, has_side_effects=True, vmem_limit_bytes=48 * 2**20
        ),
        name="backward_tower",
    )(head_part, cot, weights, *hidden, *slope, *active, *bend)


def finish(total, head_sum, split):
    def kernel(total_ref, head_ref, conv_out, proj_out, head_out, sems):
        copies = [
            pltpu.make_async_copy(total_ref.at[pl.ds(0, split)], conv_out, sems.at[0]),
            pltpu.make_async_copy(
                total_ref.at[pl.ds(split, total.shape[0] - split)], proj_out, sems.at[1]
            ),
            pltpu.make_async_copy(head_ref, head_out, sems.at[2]),
        ]
        for copy in copies:
            copy.start()
        for copy in copies:
            copy.wait()

    width = total.shape[1]
    return pl.pallas_call(
        kernel,
        out_shape=[
            jax.ShapeDtypeStruct((split, width), total.dtype),
            jax.ShapeDtypeStruct((total.shape[0] - split, width), total.dtype),
            jax.ShapeDtypeStruct(head_sum.shape, head_sum.dtype),
        ],
        in_specs=[pl.BlockSpec(memory_space=pltpu.VMEM)] * 2,
        out_specs=[ANY] * 3,
        scratch_shapes=[pltpu.SemaphoreType.DMA((3,))],
        compiler_params=pltpu.CompilerParams(vmem_limit_bytes=8 * 2**20),
        name="finish",
    )(total, head_sum)


def plain_body(bases, targets, stem_weight, conv_weight, proj_weight, head_weight):
    sections = lax.axis_size("section")
    seqs = lax.axis_size("seq")
    section_number = lax.axis_index("section")
    batches, row_count, bin_width = bases.shape
    channels = stem_weight.shape[1]
    length = row_count * seqs
    factor = 1.0 / math.sqrt(batches * lax.axis_size("dp") * length)
    unit = length // 2**sections
    local_q = row_count // unit
    blocks = length // unit
    columns = batches * unit // (seqs * sections)

    conv_all = lax.all_gather(conv_weight, "section", axis=0, tiled=True)
    proj_all = lax.all_gather(proj_weight, "section", axis=0, tiled=True)

    def to_chains(value):
        value = lax.all_to_all(value, "seq", split_axis=1, concat_axis=0, tiled=True)
        return value.reshape(blocks * columns, value.shape[-1])

    own = bases.reshape(batches, local_q, unit, bin_width).transpose(1, 0, 2, 3)
    own = own.reshape(local_q, seqs, sections, columns, bin_width)
    own = lax.dynamic_index_in_dim(own, section_number, 2, keepdims=False)
    picked = to_chains(own.astype(jnp.bfloat16))
    onehot = jnp.concatenate([(picked == c).astype(jnp.bfloat16) for c in range(4)], 1)
    stem = stem_weight.reshape(bin_width, 4, channels).transpose(1, 0, 2).reshape(-1, channels)
    state = jnp.dot(onehot, stem, preferred_element_type=jnp.float32).astype(jnp.bfloat16)

    saved = []
    for layer in range(sections):
        by = columns * 2**layer
        taps = conv_all[layer].reshape(-1, conv_all.shape[-1])
        hidden = gelu_value(state.astype(jnp.float32)).astype(jnp.bfloat16)
        wide = jnp.concatenate([shift_rows(hidden, by), hidden, shift_rows(hidden, -by)], 1)
        inner_sum = jnp.dot(wide, taps, preferred_element_type=jnp.float32)
        active = gelu_value(inner_sum).astype(jnp.bfloat16)
        update = jnp.dot(active, proj_all[layer], preferred_element_type=jnp.float32)
        saved.append((state, wide, inner_sum, active))
        state = (state.astype(jnp.float32) + update).astype(jnp.bfloat16)

    lifted = gelu_value(state.astype(jnp.float32)).astype(jnp.bfloat16)
    lifted = lifted.reshape(seqs, local_q, 1, columns, channels)
    lifted = lax.all_to_all(lifted, "seq", split_axis=0, concat_axis=2, tiled=True)
    lifted = lifted.reshape(local_q, seqs, 1, columns, channels)
    lifted = lax.all_gather(lifted, "section", axis=2, tiled=True)
    lifted = lifted.reshape(local_q, batches, unit, channels).transpose(1, 0, 2, 3)
    lifted = lifted.reshape(batches * row_count, channels)

    logits = jnp.dot(lifted, head_weight, preferred_element_type=jnp.float32)
    counts = targets.reshape(batches * row_count, targets.shape[2]).astype(jnp.float32)
    slope = ((jnp.exp(logits) - counts) * factor).astype(jnp.bfloat16)
    head_sum = lax.psum(contract_rows(lifted, slope), ("seq", "dp"))
    lift_part = times_transposed(slope, head_weight)

    lift_part = lift_part.reshape(batches, local_q, unit, channels).transpose(1, 0, 2, 3)
    lift_part = lift_part.reshape(local_q, seqs, sections, columns, channels)
    lift_part = lax.psum_scatter(lift_part, "section", scatter_dimension=2, tiled=True)
    lift_grad = to_chains(lift_part.reshape(local_q, seqs, columns, channels))


    grad = (lift_grad * gelu_slope(state.astype(jnp.float32))).astype(jnp.bfloat16)
    parts = []
    for layer in reversed(range(sections)):
        by = columns * 2**layer
        start_state, wide, inner_sum, active = saved[layer]
        kernel = conv_all[layer]
        proj_part = contract_rows(active, grad)
        active_grad = times_transposed(grad, proj_all[layer])
        inner_grad = (active_grad * gelu_slope(inner_sum)).astype(jnp.bfloat16)
        parts.append(jnp.concatenate([contract_rows(inner_grad, wide), proj_part], 1))
        wide_grad = jnp.concatenate(
            [shift_rows(inner_grad, -by), inner_grad, shift_rows(inner_grad, by)], 1
        )
        turned = kernel.transpose(0, 2, 1).reshape(-1, channels)
        hidden_grad = jnp.dot(wide_grad, turned, preferred_element_type=jnp.float32)
        grad = (
            grad.astype(jnp.float32) + hidden_grad * gelu_slope(start_state.astype(jnp.float32))
        ).astype(jnp.bfloat16)
    parts = jnp.stack(parts[::-1])
    total = lax.psum_scatter(parts, "section", scatter_dimension=0, tiled=True)
    total = lax.psum(total[0], ("seq", "dp"))
    taps_width = total.shape[1] - channels
    conv_sum = total[:, :taps_width].T.reshape(conv_weight.shape)
    return conv_sum, total[:, taps_width:][None], head_sum


def paired_body(bases, targets, stem_weight, conv_weight, proj_weight, head_weight):
    sections = lax.axis_size("section")
    zones = lax.axis_size("dp")
    batches, half, bin_width = bases.shape
    channels = stem_weight.shape[1]
    inner = proj_weight.shape[1]
    length = batches * half
    unit = length // 2**sections
    factor = 1.0 / math.sqrt(batches * zones * length)
    taps = conv_weight[0].transpose(0, 2, 1).reshape(3 * inner, channels)
    top, weights, hidden, slope, active, bend = forward_tower(
        bases, stem_weight, taps, proj_weight[0], sections, unit
    )
    head_part, cot = head(top, targets, head_weight, factor)
    cot = cot.reshape(length, channels)
    total, head_sum = backward_tower(
        head_part, cot, weights, hidden, slope, active, bend, sections, zones, unit
    )
    conv_sum, proj_sum, head_sum = finish(total, head_sum, 3 * inner)
    conv_sum = conv_sum.reshape(3, inner, channels).transpose(0, 2, 1)
    return conv_sum[None], proj_sum[None], head_sum


def body(bases, targets, stem_weight, conv_weight, proj_weight, head_weight):
    sections, zones = lax.axis_size("section"), lax.axis_size("dp")
    batches, half = bases.shape[:2]
    inner = proj_weight.shape[1]
    unit = batches * half // 2**sections
    paired = lax.axis_size("seq") == 2 and batches == 2 and zones > 1 and sections > 1
    paired = paired and unit % 16 == 0 and half % 16 == 0 and inner % 16 == 0
    paired = paired and (2 * inner) % (16 * sections) == 0
    paired = paired and (2 * inner) % (8 * sections * zones) == 0
    paired = paired and zones & (zones - 1) == 0
    paired = paired and stem_weight.shape[1] % (16 * zones) == 0
    run = paired_body if paired else plain_body
    return run(bases, targets, stem_weight, conv_weight, proj_weight, head_weight)


def solution(mesh):
    in_specs = (
        P("dp", "seq", None),
        P("dp", "seq", "section"),
        P(),
        P("section", None, None, None),
        P("section", None, None),
        P(None, "section"),
    )
    out_specs = (P("section", None, None, None), P("section", None, None), P(None, "section"))
    return jax.shard_map(body, mesh=mesh, in_specs=in_specs, out_specs=out_specs, check_vma=False)
```

```python
import math

import jax
import jax.numpy as jnp
from jax import lax
from jax.experimental import pallas as pl
from jax.experimental.pallas import tpu as pltpu
from jax.sharding import PartitionSpec as P

SQRT_TWO_OVER_PI = 0.7978845608028654
CUBIC_TERM = 0.044715


def gelu_value(inputs):
    return (
        0.5
        * inputs
        * (1.0 + jnp.tanh(SQRT_TWO_OVER_PI * (inputs + CUBIC_TERM * inputs * inputs * inputs)))
    )


def gelu_slope(inputs):
    tangent = jnp.tanh(SQRT_TWO_OVER_PI * (inputs + CUBIC_TERM * inputs * inputs * inputs))
    return 0.5 * (1.0 + tangent) + 0.5 * inputs * (1.0 - tangent * tangent) * SQRT_TWO_OVER_PI * (
        1.0 + 3.0 * CUBIC_TERM * inputs * inputs
    )


def contract_rows(left_side, right_side):
    return lax.dot_general(
        left_side, right_side, (((0,), (0,)), ((), ())), preferred_element_type=jnp.float32
    )


def times_transposed(left_side, right_side):
    return lax.dot_general(
        left_side, right_side, (((1,), (1,)), ((), ())), preferred_element_type=jnp.float32
    )


def shift_rows(value, by):
    if abs(by) >= value.shape[0]:
        return jnp.zeros_like(value)
    pad = jnp.zeros((abs(by),) + value.shape[1:], value.dtype)
    if by > 0:
        return jnp.concatenate([pad, value[:-by]], 0)
    return jnp.concatenate([value[-by:], pad], 0)


MESH = pl.DeviceIdType.MESH
ANY = pl.BlockSpec(memory_space=pl.ANY)


def greet(peers):
    barrier = pltpu.get_barrier_semaphore()
    for peer in peers:
        pl.semaphore_signal(barrier, inc=1, device_id=peer, device_id_type=MESH)
    pl.semaphore_wait(barrier, len(peers))


def remote(src, dst, send, recv, peer):
    return pltpu.make_async_remote_copy(
        src_ref=src, dst_ref=dst, send_sem=send, recv_sem=recv, device_id=peer, device_id_type=MESH
    )


def both_gelu(inputs):
    square = inputs * inputs
    tangent = jnp.tanh(
        inputs * (SQRT_TWO_OVER_PI + (SQRT_TWO_OVER_PI * CUBIC_TERM) * square)
    )
    gate = 0.5 + 0.5 * tangent
    value = inputs * gate
    inside = 2.0 * SQRT_TWO_OVER_PI + (6.0 * SQRT_TWO_OVER_PI * CUBIC_TERM) * square
    return value, gate + value * (1.0 - gate) * inside


def tile_of(rows):
    for size in (512, 384, 256, 192, 128, 96, 64, 48, 32, 16):
        if rows % size == 0:
            return size
    return rows


def forward_tower(bases, stem, taps, proj, sections, unit):
    seqs, half, width = bases.shape
    length = seqs * half
    channels = stem.shape[1]
    inner = proj.shape[0]
    rows = taps.shape[0] + inner
    part = rows // 2
    tile = tile_of(half)
    steps = half // tile
    team = 3 if steps % 3 == 0 else 1
    shifts = [unit * 2**k for k in range(sections)]

    def kernel(*refs):
        bases_ref, stem_ref, taps_ref, proj_ref = refs[:4]
        refs = refs[4:]
        top_ref, weights_ref = refs[:2]
        hidden_out, slope_out = refs[2 : 2 + sections], refs[2 + sections : 1 + 2 * sections]
        refs = refs[1 + 2 * sections :]
        active_out, bend_out = refs[:sections], refs[sections : 2 * sections]
        refs = refs[2 * sections :]
        full, held, turned, state, sorted_stem = refs[:5]
        refs = refs[5:]
        hidden, slope = refs[:sections], refs[sections : 2 * sections - 1]
        refs = refs[2 * sections - 1 :]
        active, bend = refs[:sections], refs[sections : 2 * sections]
        refs = refs[2 * sections :]
        bsend, brecv, send, recv, send2, recv2, tsend, trecv, own_sem, out_sem = refs

        s, c = lax.axis_index("section"), lax.axis_index("seq")
        partner = {"section": s, "seq": 1 - c}
        peers = [{"section": lax.rem(s + k, sections), "seq": c} for k in range(1, sections)]
        loads = [
            pltpu.make_async_copy(bases_ref.at[c], full.at[c], own_sem.at[0]),
            pltpu.make_async_copy(
                taps_ref, held.at[s, pl.ds(0, taps.shape[0])], own_sem.at[1]
            ),
            pltpu.make_async_copy(
                proj_ref, held.at[s, pl.ds(taps.shape[0], inner)], own_sem.at[2]
            ),
        ]
        for copy in loads:
            copy.start()
        greet(peers + [partner])
        across = remote(bases_ref.at[1 - c], full.at[c], bsend, brecv, partner)
        across.start()
        loads[1].wait()
        loads[2].wait()
        mine = held.at[s, pl.ds(pl.multiple_of(c * part, 16), part)]
        first = []
        for k, peer in enumerate(peers):
            first.append(remote(mine, mine, send.at[k], recv.at[k], peer))
            first[-1].start()
        for k in range(sections - 1):
            edge = jnp.zeros((shifts[k], channels), jnp.bfloat16)
            hidden[k][pl.ds(0, shifts[k]), :] = edge
            hidden[k][pl.ds(shifts[k] + length, shifts[k]), :] = edge

        across_rows = lax.broadcasted_iota(jnp.int32, (4 * width, 4 * width), 0)
        across_columns = lax.broadcasted_iota(jnp.int32, (4 * width, 4 * width), 1)
        place_of = 4 * lax.rem(across_rows, width) + across_rows // width
        chosen = (across_columns == place_of).astype(jnp.bfloat16)
        sorted_stem[...] = jnp.dot(
            chosen, stem_ref[...], preferred_element_type=jnp.float32
        ).astype(jnp.bfloat16)

        def begin(number):
            def step(i, carry):
                at = i * tile
                codes = full[number, pl.ds(pl.multiple_of(at, 16), tile), :]
                onehot = jnp.concatenate(
                    [(codes == k).astype(jnp.bfloat16) for k in range(4)], 1
                )
                start = jnp.dot(onehot, sorted_stem[...], preferred_element_type=jnp.float32)
                start = start.astype(jnp.bfloat16)
                place = pl.multiple_of(number * half + at, 16)
                state[pl.ds(place, tile), :] = start
                value = gelu_value(start.astype(jnp.float32)).astype(jnp.bfloat16)
                hidden[0][pl.ds(pl.multiple_of(shifts[0] + place, 16), tile), :] = value
                return carry

            lax.fori_loop(0, steps, step, 0)

        loads[0].wait()
        begin(c)
        across.wait_recv()
        begin(1 - c)

        second = []
        for k in range(sections - 1):
            first[k].wait_recv()
            source = lax.rem(s + sections - 1 - k, sections)
            piece = held.at[source, pl.ds(pl.multiple_of(c * part, 16), part)]
            second.append(remote(piece, piece, send2.at[k], recv2.at[k], partner))
            second[-1].start()
        for copy in second:
            copy.wait_recv()

        outs = []

        def keep(src, dst):
            outs.append(pltpu.make_async_copy(src, dst, out_sem.at[len(outs)]))
            outs[-1].start()

        keep(held, weights_ref)
        keep(hidden[0].at[pl.ds(shifts[0], length)], hidden_out[0])

        for k in range(sections):
            by = shifts[k]
            for j in range(3):
                tap = held[k, pl.ds(j * inner, inner), :]
                turned[pl.ds(j * channels, channels), :] = tap.T

            def group(places, lead, width, k=k, by=by):
                weight = turned[pl.ds(pl.multiple_of(lead * channels, 16), width * channels), :]
                inners = []
                for place in places:
                    wide = jnp.concatenate(
                        [
                            hidden[k][pl.ds(pl.multiple_of(place + (lead + j) * by, 16), tile), :]
                            for j in range(width)
                        ],
                        1,
                    )
                    inners.append(
                        jnp.dot(wide, weight, preferred_element_type=jnp.float32)
                    )
                olds = [state[pl.ds(place, tile), :].astype(jnp.float32) for place in places]
                results = []
                for inner_sum, old in zip(inners, olds):
                    value, bent = both_gelu(inner_sum)
                    value, bent = value.astype(jnp.bfloat16), bent.astype(jnp.bfloat16)
                    update = jnp.dot(
                        value,
                        held[k, pl.ds(3 * inner, inner), :],
                        preferred_element_type=jnp.float32,
                    )
                    results.append((value, bent, (old + update).astype(jnp.bfloat16)))
                for place, (value, bent, _) in zip(places, results):
                    active[k][pl.ds(place, tile), :] = value
                    bend[k][pl.ds(place, tile), :] = bent
                return [new for _, _, new in results]

            def spots(i, base):
                return [
                    pl.multiple_of(base + (i * team + g) * tile, 16) for g in range(team)
                ]

            if k < sections - 1:

                def step(i, carry, k=k):
                    places = spots(i, 0)
                    news = group(places, 0, 3)
                    pairs = [both_gelu(new.astype(jnp.float32)) for new in news]
                    for place, new, (value, bent) in zip(places, news, pairs):
                        state[pl.ds(place, tile), :] = new
                        ahead = pl.multiple_of(shifts[k + 1] + place, 16)
                        hidden[k + 1][pl.ds(ahead, tile), :] = value.astype(jnp.bfloat16)
                        slope[k][pl.ds(place, tile), :] = bent.astype(jnp.bfloat16)
                    return carry

                lax.fori_loop(0, length // (tile * team), step, 0)
                keep(hidden[k + 1].at[pl.ds(shifts[k + 1], length)], hidden_out[k + 1])
                keep(slope[k], slope_out[k])
            else:

                def finish_half(number, store):
                    def step(i, carry):
                        places = spots(i, number * half)
                        for place, new in zip(places, group(places, 1 - number, 2)):
                            store(place, new)
                        return carry

                    lax.fori_loop(0, steps // team, step, 0)

                def away(place, new):
                    state[pl.ds(place, tile), :] = new

                def here(place, new):
                    start = pl.multiple_of(place - c * half, 16)
                    top_ref[c, pl.ds(start, tile), :] = new

                finish_half(1 - c, away)
                theirs = state.at[pl.ds(pl.multiple_of((1 - c) * half, 16), half)]
                last = remote(theirs, top_ref.at[c], tsend, trecv, partner)
                last.start()
                finish_half(c, here)
            keep(active[k], active_out[k])
            keep(bend[k], bend_out[k])
        for copy in outs:
            copy.wait()
        last.wait()
        across.wait_send()
        for copy in first + second:
            copy.wait_send()

    bf16 = jnp.bfloat16
    long = jax.ShapeDtypeStruct((length, channels), bf16)
    thin = jax.ShapeDtypeStruct((length, inner), bf16)
    dma = pltpu.SemaphoreType.DMA
    copies = 4 * sections
    out = pl.pallas_call(
        kernel,
        out_shape=[
            jax.ShapeDtypeStruct((seqs, half, channels), bf16),
            jax.ShapeDtypeStruct((sections, rows, channels), bf16),
        ]
        + [long] * (2 * sections - 1)
        + [thin] * (2 * sections),
        in_specs=[ANY, pl.BlockSpec(memory_space=pltpu.VMEM), ANY, ANY],
        out_specs=[pl.BlockSpec(memory_space=pltpu.VMEM)] + [ANY] * (4 * sections),
        scratch_shapes=[
            pltpu.VMEM((seqs, half, width), jnp.int32),
            pltpu.VMEM((sections, rows, channels), bf16),
            pltpu.VMEM((3 * channels, inner), bf16),
            pltpu.VMEM((length, channels), bf16),
            pltpu.VMEM(stem.shape, bf16),
        ]
        + [pltpu.VMEM((length + 2 * by, channels), bf16) for by in shifts]
        + [pltpu.VMEM((length, channels), bf16)] * (sections - 1)
        + [pltpu.VMEM((length, inner), bf16)] * (2 * sections)
        + [dma, dma]
        + [dma((sections - 1,))] * 4
        + [dma, dma, dma((3,)), dma((copies,))],
        compiler_params=pltpu.CompilerParams(
            collective_id=0, has_side_effects=True, vmem_limit_bytes=54 * 2**20
        ),
        name="forward_tower",
    )(bases, stem, taps, proj)
    top, weights = out[:2]
    hidden, slope = out[2 : 2 + sections], out[2 + sections : 1 + 2 * sections]
    active = out[1 + 2 * sections : 1 + 3 * sections]
    bend = out[1 + 3 * sections :]
    return top, weights, hidden, slope, active, bend


def head(top, targets, head_weight, factor):
    seqs, half, channels = top.shape
    tracks = head_weight.shape[1]
    tile = tile_of(half)
    if half % 512 == 0:
        tile = 512
    steps = half // tile

    def kernel(
        top_ref, targets_ref, weight_ref, grad_ref, cot_ref, counts, stage, load, send, recv
    ):
        s, c = lax.axis_index("section"), lax.axis_index("seq")
        partner = {"section": s, "seq": 1 - c}
        loads = []
        for n, b in enumerate((1 - c, c)):
            for i in range(steps):
                loads.append(
                    pltpu.make_async_copy(
                        targets_ref.at[b, pl.ds(i * tile, tile)],
                        counts.at[n * steps + i],
                        load.at[n * steps + i],
                    )
                )
                loads[-1].start()
        greet([partner])
        grad_ref[...] = jnp.zeros_like(grad_ref)

        def run(b, n, store):
            def step(i, carry):
                at = pl.multiple_of(i * tile, 16)
                pltpu.make_async_copy(
                    targets_ref.at[b, pl.ds(at, tile)], counts.at[n + i], load.at[n + i]
                ).wait()
                value, bent = both_gelu(top_ref[b, pl.ds(at, tile), :].astype(jnp.float32))
                lifted = value.astype(jnp.bfloat16)
                logits = jnp.dot(lifted, weight_ref[...], preferred_element_type=jnp.float32)
                drop = jnp.exp(logits) - counts[n + i].astype(jnp.float32)
                drop = (drop * factor).astype(jnp.bfloat16)
                grad_ref[...] += contract_rows(lifted, drop)
                lift = times_transposed(drop, weight_ref[...])
                store(at, (lift * bent).astype(jnp.bfloat16))
                return carry

            lax.fori_loop(0, steps, step, 0)

        def away(at, value):
            stage[pl.ds(at, tile), :] = value

        def here(at, value):
            cot_ref[c, pl.ds(at, tile), :] = value

        run(1 - c, 0, away)
        copy = remote(stage, cot_ref.at[c], send, recv, partner)
        copy.start()
        run(c, steps, here)
        copy.wait()

    vmem = pl.BlockSpec(memory_space=pltpu.VMEM)
    dma = pltpu.SemaphoreType.DMA
    return pl.pallas_call(
        kernel,
        out_shape=[
            jax.ShapeDtypeStruct((channels, tracks), jnp.float32),
            jax.ShapeDtypeStruct(top.shape, jnp.bfloat16),
        ],
        in_specs=[vmem, ANY, vmem],
        out_specs=[vmem, vmem],
        scratch_shapes=[
            pltpu.VMEM((seqs * steps, tile, tracks), jnp.int32),
            pltpu.VMEM((half, channels), jnp.bfloat16),
            dma((seqs * steps,)),
            dma,
            dma,
        ],
        compiler_params=pltpu.CompilerParams(
            collective_id=1, has_side_effects=True, vmem_limit_bytes=48 * 2**20
        ),
        name="head",
    )(top, targets, head_weight)


def backward_tower(head_part, cot, weights, hidden, slope, active, bend, sections, zones, unit):
    length, channels = hidden[0].shape
    inner = active[0].shape[1]
    rows = weights.shape[1]
    part = rows // 2
    quarter = part // sections
    levels = zones.bit_length() - 1
    tracks = head_part.shape[1]
    side = head_part.shape[0] // 2
    tile = length // 2
    most = unit * 2 ** (sections - 1)
    f32, bf16 = jnp.float32, jnp.bfloat16

    def kernel(*refs):
        head_ref, cot_ref, weights_ref = refs[:3]
        refs = refs[3:]
        hidden_in, slope_in = refs[:sections], refs[sections : 2 * sections - 1]
        refs = refs[2 * sections - 1 :]
        active_in, bend_in = refs[:sections], refs[sections : 2 * sections]
        refs = refs[2 * sections :]
        out, head_out = refs[:2]
        hidden, slope, active, bend = refs[2:4], refs[4:6], refs[6:8], refs[8:10]
        held, grad, pull, sums, load = refs[10:15]
        met, wire, came, total, zcame, final = refs[15:21]
        hmet, hsum, hcame = refs[21:24]
        sems = refs[24:]

        s, c, d = (lax.axis_index(name) for name in ("section", "seq", "dp"))
        partner = {"section": s, "seq": 1 - c, "dp": d}
        order = [lax.rem(s + k, sections) for k in range(1, sections)]
        across = [{"section": o, "seq": c, "dp": d} for o in order]
        bits = [lax.rem(d // 2**t, 2) for t in range(levels)]
        along = [
            {"section": s, "seq": c, "dp": d + 2**t * (1 - 2 * bits[t])} for t in range(levels)
        ]
        floors = [lax.rem(d + n, zones) for n in range(1, zones)]
        lifts = [{"section": s, "seq": c, "dp": z} for z in floors]
        count = [0]

        def fetch(src, dst):
            copy = pltpu.make_async_copy(src, dst, load.at[count[0]])
            count[0] += 1
            copy.start()
            return copy

        bring = {}

        def prefetch(k):
            slot = k % 2
            early = [
                fetch(weights_ref.at[k], held.at[k]),
                fetch(bend_in[k], bend[slot]),
                fetch(active_in[k], active[slot]),
            ]
            late = [fetch(hidden_in[k], hidden[slot])]
            if k:
                late.append(fetch(slope_in[k - 1], slope[slot]))
            bring[k] = (early, late)

        prefetch(sections - 1)
        greet([partner] + across + lifts)

        sends = []

        def launch(src, dst, pair, index, peer):
            copy = remote(src, dst, sems[2 * pair].at[index], sems[2 * pair + 1].at[index], peer)
            copy.start()
            sends.append(copy)
            return copy

        def block(base, size, number):
            return pl.ds(pl.multiple_of(base + number * size, 8), size)

        flight = {}

        def swap(k):
            far = sums.at[k, block(0, part, 1 - c)]
            flight[k] = [launch(far, met.at[k], 0, k, partner)]

        def spread(k):
            flight[k][0].wait_recv()
            flight[k] = []

            def both(o):
                return met[k, block(0, quarter, o), :] + sums[k, block(c * part, quarter, o), :]

            for n, o in enumerate(order):
                wire[k, n] = both(o).astype(bf16)
                flight[k].append(
                    launch(wire.at[k, n], came.at[k, n], 1, k * (sections - 1) + n, across[n])
                )
            total[k] = both(s)

        def kept(span, t):
            base = 0
            for step in range(t):
                base = base + bits[step] * (span >> (step + 1))
            return base

        def landing(span, t):
            return pl.ds(span - (span >> t), span >> (t + 1))

        def climb(k, t):
            for copy in flight[k]:
                copy.wait_recv()
            if t == 0:
                value = total[k]
                for n in range(sections - 1):
                    value = value + came[k, n].astype(f32)
                total[k] = value
            else:
                mine = block(kept(quarter, t), quarter >> t, 0)
                total[k, mine, :] = total[k, mine, :] + zcame[k, landing(quarter, t - 1), :]
            size = quarter >> (t + 1)
            away = block(kept(quarter, t), size, 1 - bits[t])
            flight[k] = [
                launch(
                    total.at[k, away],
                    zcame.at[k, landing(quarter, t)],
                    2,
                    k * levels + t,
                    along[t],
                )
            ]

        def level(k, t):
            for copy in flight[k]:
                copy.wait_recv()
            mine = block(kept(quarter, t + 1), quarter >> (t + 1), 0)
            if t == levels - 1:
                final[k, mine, :] = total[k, mine, :] + zcame[k, landing(quarter, t), :]
            piece = final.at[k, mine]
            flight[k] = [launch(piece, piece, 3, k * levels + t, along[t])]

        strip = quarter // zones
        brisk = 0

        def climb_at_once(k):
            for copy in flight[k]:
                copy.wait_recv()
            value = total[k]
            for n in range(sections - 1):
                value = value + came[k, n].astype(f32)
            total[k] = value
            flight[k] = [
                launch(
                    total.at[k, block(0, strip, z)],
                    zcame.at[k, pl.ds(n * strip, strip)],
                    10,
                    k * (zones - 1) + n,
                    lifts[n],
                )
                for n, z in enumerate(floors)
            ]

        def level_at_once(k):
            for copy in flight[k]:
                copy.wait_recv()
            value = total[k, block(0, strip, d), :]
            for n in range(zones - 1):
                value = value + zcame[k, pl.ds(n * strip, strip), :]
            final[k, block(0, strip, d), :] = value
            piece = final.at[k, block(0, strip, d)]
            flight[k] = [launch(piece, piece, 11, k * (zones - 1) + n, peer) for n, peer in enumerate(lifts)]
            strip_home(k, d)

        def home_strip(k, z):
            owner = {"section": k, "seq": c, "dp": d}
            index = lax.rem(s + 2 * sections - k - 1, sections) * zones + z
            place = out.at[block(c * part + s * quarter, strip, z)]
            return remote(
                final.at[k, block(0, strip, z)],
                place,
                sems[24].at[k * zones + z],
                sems[25].at[index],
                owner,
            )

        def strip_home(k, z):
            @pl.when(s != k)
            def _():
                home_strip(k, z).start()

        def deliver_strips(k):
            for n, copy in enumerate(flight[k]):
                copy.wait_recv()
                strip_home(k, lax.rem(d + zones - 1 - n, zones))

            @pl.when(s == k)
            def _():
                out[block(c * part, quarter, s), :] = final[k]
                relay(0, s).start()

        def home(k):
            owner = {"section": k, "seq": c, "dp": d}
            index = lax.rem(s + 2 * sections - k - 1, sections)
            place = out.at[block(c * part, quarter, s)]
            return remote(final.at[k], place, sems[8].at[k], sems[9].at[index], owner)

        def deliver(k):
            for copy in flight[k]:
                copy.wait_recv()

            @pl.when(s != k)
            def _():
                home(k).start()

            @pl.when(s == k)
            def _():
                out[block(c * part, quarter, s), :] = final[k]
                relay(0, s).start()

        def relay(n, source):
            piece = out.at[block(c * part, quarter, source)]
            return remote(piece, piece, sems[10].at[n], sems[11].at[n], partner)

        def hand(k):
            @pl.when(s == k)
            def _():
                for n, o in enumerate(order):
                    if k > brisk:
                        piece = out.at[block(c * part, quarter, o)]
                        remote(
                            final.at[k], piece, sems[8].at[k], sems[9].at[n], across[n]
                        ).wait_recv()
                    else:
                        for z in range(zones):
                            piece = out.at[block(c * part + o * quarter, strip, z)]
                            remote(
                                final.at[k, block(0, strip, z)],
                                piece,
                                sems[24].at[k * zones + z],
                                sems[25].at[n * zones + z],
                                across[n],
                            ).wait_recv()
                    relay(n + 1, o).start()

        def settle(k):
            @pl.when(s != k)
            def _():
                if k > brisk:
                    home(k).wait_send()
                else:
                    for z in range(zones):
                        home_strip(k, z).wait_send()

            @pl.when(s == k)
            def _():
                for n, o in enumerate([s] + order):
                    relay(n, o).wait()

        def head_swap():
            far = head_ref.at[block(0, side, 1 - c)]
            flight["h"] = [launch(far, hmet, 6, 0, partner)]

        def head_climb(t):
            flight["h"][0].wait_recv()
            if t == 0:
                hsum[...] = hmet[...] + head_ref[block(0, side, c), :]
            else:
                mine = block(kept(side, t), side >> t, 0)
                hsum[mine, :] = hsum[mine, :] + hcame[landing(side, t - 1), :]
            away = block(kept(side, t), side >> (t + 1), 1 - bits[t])
            flight["h"] = [
                launch(hsum.at[away], hcame.at[landing(side, t)], 7, t, along[t])
            ]

        flight["r"] = []

        def pass_on(start, size):
            piece = head_out.at[block(c * side + start, size, 0)]
            flight["r"].append(launch(piece, piece, 9, len(flight["r"]), partner))

        def other(span, t):
            return kept(span, t) + (1 - bits[t]) * (span >> (t + 1))

        def head_level(t):
            flight["h"][0].wait_recv()
            start, size = kept(side, t + 1), side >> (t + 1)
            place = block(c * side + start, size, 0)
            if t == levels - 1:
                mine = block(start, size, 0)
                head_out[place, :] = hsum[mine, :] + hcame[landing(side, t), :]
                pass_on(start, size)
            else:
                pass_on(other(side, t + 1), side >> (t + 2))
            piece = head_out.at[place]
            flight["h"] = [launch(piece, piece, 8, t, along[t])]

        def head_hand():
            flight["h"][0].wait_recv()
            pass_on(other(side, 0), side // 2)

        head_swap()
        pull[pl.ds(0, most), :] = jnp.zeros((most, inner), bf16)
        pull[pl.ds(most + length, most), :] = jnp.zeros((most, inner), bf16)
        sums[...] = jnp.zeros_like(sums)

        top = sections - 1
        stages = {}
        for k in range(sections):
            line = [lambda k=k: swap(k), lambda k=k: spread(k)]
            if k > brisk:
                line += [lambda k=k, t=t: climb(k, t) for t in range(levels)]
                line += [lambda k=k, t=t: level(k, t) for t in reversed(range(levels))]
                line.append(lambda k=k: deliver(k))
            else:
                for stage in (climb_at_once, level_at_once, deliver_strips):
                    line.append(lambda k=k, stage=stage: stage(k))
            stages[k] = line + [lambda k=k: hand(k)]
        line = [lambda t=t: head_climb(t) for t in range(levels)]
        line += [lambda t=t: head_level(t) for t in reversed(range(levels))]
        stages["h"] = line + [head_hand]
        marks = {}

        def plan(name, ticks):
            for at in ticks:
                if at <= 3 * sections - 1 and stages[name]:
                    marks.setdefault(at, []).append(stages[name].pop(0))

        for k in range(sections):
            plan(k, [3 * (top - k) + 2 + gap for gap in (0, 2, 3, 6)])
        plan("h", (1, 5, 10))
        clock = [0]

        def tick():
            for stage in marks.get(clock[0], []):
                stage()
            clock[0] += 1

        for k in reversed(range(sections)):
            by = unit * 2**k
            slot = k % 2
            above = cot_ref if k == top else grad
            for copy in bring[k][0]:
                copy.wait()

            def inward(i, k=k, slot=slot, above=above):
                place = i * tile
                here = above[pl.ds(place, tile), :]
                back = times_transposed(here, held[k, pl.ds(3 * inner, inner), :])
                back = back * bend[slot][pl.ds(place, tile), :].astype(f32)
                pull[pl.ds(most + place, tile), :] = back.astype(bf16)
                sums[k, pl.ds(3 * inner, inner), :] += contract_rows(
                    active[slot][pl.ds(place, tile), :], here
                )

            for i in range(length // tile):
                inward(i)
                tick()
            for copy in bring[k][1]:
                copy.wait()
            if k:
                prefetch(k - 1)

            def outward(i, carry, k=k, by=by, slot=slot, above=above):
                place = pl.multiple_of(i * tile, 16)
                there = hidden[slot][pl.ds(place, tile), :]
                value = None
                for j in range(3 if k < top else 2):
                    if k < top:
                        start = pl.multiple_of(most + place + (1 - j) * by, 16)
                        span = pl.ds(j * inner, inner)
                    else:
                        start = most + (1 - j) * by
                        span = pl.ds(pl.multiple_of((i + j) * inner, 16), inner)
                    piece = pull[pl.ds(start, tile), :]
                    sums[k, span, :] += contract_rows(piece, there)
                    if k:
                        term = jnp.dot(piece, held[k, span, :], preferred_element_type=f32)
                        value = term if value is None else value + term
                if k:
                    value = value * slope[slot][pl.ds(place, tile), :].astype(f32)
                    value = value + above[pl.ds(place, tile), :].astype(f32)
                    grad[pl.ds(place, tile), :] = value.astype(bf16)
                return carry

            lax.fori_loop(0, length // tile, outward, 0)
            tick()

        rounds = 0
        while any(stages.values()):
            for name in [0, *reversed(range(1, sections)), "h"]:
                if stages[name] and (name != "h" or rounds > 1):
                    stages[name].pop(0)()
            rounds += 1
        for copy in flight["r"]:
            copy.wait_recv()
        for k in range(sections):
            settle(k)
        for copy in sends:
            copy.wait_send()

    dma = pltpu.SemaphoreType.DMA

    def pair(count):
        return [dma((count,))] * 2

    long, thin = pltpu.VMEM((length, channels), bf16), pltpu.VMEM((length, inner), bf16)
    vmem = pl.BlockSpec(memory_space=pltpu.VMEM)
    return pl.pallas_call(
        kernel,
        out_shape=[
            jax.ShapeDtypeStruct((rows, channels), f32),
            jax.ShapeDtypeStruct(head_part.shape, f32),
        ],
        in_specs=[vmem, vmem] + [ANY] * (4 * sections),
        out_specs=[vmem, vmem],
        scratch_shapes=[long] * 4
        + [thin] * 4
        + [
            pltpu.VMEM(weights.shape, bf16),
            long,
            pltpu.VMEM((length + 2 * most, inner), bf16),
            pltpu.VMEM((sections, rows, channels), f32),
            dma((5 * sections,)),
            pltpu.VMEM((sections, part, channels), f32),
            pltpu.VMEM((sections, sections - 1, quarter, channels), bf16),
            pltpu.VMEM((sections, sections - 1, quarter, channels), bf16),
            pltpu.VMEM((sections, quarter, channels), f32),
            pltpu.VMEM((sections, quarter, channels), f32),
            pltpu.VMEM((sections, quarter, channels), f32),
            pltpu.VMEM((side, tracks), f32),
            pltpu.VMEM((side, tracks), f32),
            pltpu.VMEM((side, tracks), f32),
        ]
        + pair(sections)
        + pair(sections * (sections - 1))
        + pair(sections * levels)
        + pair(sections * levels)
        + [dma((sections,)), dma((sections,))]
        + pair(sections)
        + pair(1)
        + pair(levels)
        + pair(levels)
        + pair(levels + 1)
        + pair(sections * (zones - 1))
        + pair(sections * (zones - 1))
        + [dma((sections * zones,)), dma((sections * zones,))],
        compiler_params=pltpu.CompilerParams(
            collective_id=2, has_side_effects=True, vmem_limit_bytes=48 * 2**20
        ),
        name="backward_tower",
    )(head_part, cot, weights, *hidden, *slope, *active, *bend)


def finish(total, head_sum, split):
    def kernel(total_ref, head_ref, conv_out, proj_out, head_out, sems):
        copies = [
            pltpu.make_async_copy(total_ref.at[pl.ds(0, split)], conv_out, sems.at[0]),
            pltpu.make_async_copy(
                total_ref.at[pl.ds(split, total.shape[0] - split)], proj_out, sems.at[1]
            ),
            pltpu.make_async_copy(head_ref, head_out, sems.at[2]),
        ]
        for copy in copies:
            copy.start()
        for copy in copies:
            copy.wait()

    width = total.shape[1]
    return pl.pallas_call(
        kernel,
        out_shape=[
            jax.ShapeDtypeStruct((split, width), total.dtype),
            jax.ShapeDtypeStruct((total.shape[0] - split, width), total.dtype),
            jax.ShapeDtypeStruct(head_sum.shape, head_sum.dtype),
        ],
        in_specs=[pl.BlockSpec(memory_space=pltpu.VMEM)] * 2,
        out_specs=[ANY] * 3,
        scratch_shapes=[pltpu.SemaphoreType.DMA((3,))],
        compiler_params=pltpu.CompilerParams(vmem_limit_bytes=8 * 2**20),
        name="finish",
    )(total, head_sum)


def plain_body(bases, targets, stem_weight, conv_weight, proj_weight, head_weight):
    sections = lax.axis_size("section")
    seqs = lax.axis_size("seq")
    section_number = lax.axis_index("section")
    batches, row_count, bin_width = bases.shape
    channels = stem_weight.shape[1]
    length = row_count * seqs
    factor = 1.0 / math.sqrt(batches * lax.axis_size("dp") * length)
    unit = length // 2**sections
    local_q = row_count // unit
    blocks = length // unit
    columns = batches * unit // (seqs * sections)

    conv_all = lax.all_gather(conv_weight, "section", axis=0, tiled=True)
    proj_all = lax.all_gather(proj_weight, "section", axis=0, tiled=True)

    def to_chains(value):
        value = lax.all_to_all(value, "seq", split_axis=1, concat_axis=0, tiled=True)
        return value.reshape(blocks * columns, value.shape[-1])

    own = bases.reshape(batches, local_q, unit, bin_width).transpose(1, 0, 2, 3)
    own = own.reshape(local_q, seqs, sections, columns, bin_width)
    own = lax.dynamic_index_in_dim(own, section_number, 2, keepdims=False)
    picked = to_chains(own.astype(jnp.bfloat16))
    onehot = jnp.concatenate([(picked == c).astype(jnp.bfloat16) for c in range(4)], 1)
    stem = stem_weight.reshape(bin_width, 4, channels).transpose(1, 0, 2).reshape(-1, channels)
    state = jnp.dot(onehot, stem, preferred_element_type=jnp.float32).astype(jnp.bfloat16)

    saved = []
    for layer in range(sections):
        by = columns * 2**layer
        taps = conv_all[layer].reshape(-1, conv_all.shape[-1])
        hidden = gelu_value(state.astype(jnp.float32)).astype(jnp.bfloat16)
        wide = jnp.concatenate([shift_rows(hidden, by), hidden, shift_rows(hidden, -by)], 1)
        inner_sum = jnp.dot(wide, taps, preferred_element_type=jnp.float32)
        active = gelu_value(inner_sum).astype(jnp.bfloat16)
        update = jnp.dot(active, proj_all[layer], preferred_element_type=jnp.float32)
        saved.append((state, wide, inner_sum, active))
        state = (state.astype(jnp.float32) + update).astype(jnp.bfloat16)

    lifted = gelu_value(state.astype(jnp.float32)).astype(jnp.bfloat16)
    lifted = lifted.reshape(seqs, local_q, 1, columns, channels)
    lifted = lax.all_to_all(lifted, "seq", split_axis=0, concat_axis=2, tiled=True)
    lifted = lifted.reshape(local_q, seqs, 1, columns, channels)
    lifted = lax.all_gather(lifted, "section", axis=2, tiled=True)
    lifted = lifted.reshape(local_q, batches, unit, channels).transpose(1, 0, 2, 3)
    lifted = lifted.reshape(batches * row_count, channels)

    logits = jnp.dot(lifted, head_weight, preferred_element_type=jnp.float32)
    counts = targets.reshape(batches * row_count, targets.shape[2]).astype(jnp.float32)
    slope = ((jnp.exp(logits) - counts) * factor).astype(jnp.bfloat16)
    head_sum = lax.psum(contract_rows(lifted, slope), ("seq", "dp"))
    lift_part = times_transposed(slope, head_weight)

    lift_part = lift_part.reshape(batches, local_q, unit, channels).transpose(1, 0, 2, 3)
    lift_part = lift_part.reshape(local_q, seqs, sections, columns, channels)
    lift_part = lax.psum_scatter(lift_part, "section", scatter_dimension=2, tiled=True)
    lift_grad = to_chains(lift_part.reshape(local_q, seqs, columns, channels))


    grad = (lift_grad * gelu_slope(state.astype(jnp.float32))).astype(jnp.bfloat16)
    parts = []
    for layer in reversed(range(sections)):
        by = columns * 2**layer
        start_state, wide, inner_sum, active = saved[layer]
        kernel = conv_all[layer]
        proj_part = contract_rows(active, grad)
        active_grad = times_transposed(grad, proj_all[layer])
        inner_grad = (active_grad * gelu_slope(inner_sum)).astype(jnp.bfloat16)
        parts.append(jnp.concatenate([contract_rows(inner_grad, wide), proj_part], 1))
        wide_grad = jnp.concatenate(
            [shift_rows(inner_grad, -by), inner_grad, shift_rows(inner_grad, by)], 1
        )
        turned = kernel.transpose(0, 2, 1).reshape(-1, channels)
        hidden_grad = jnp.dot(wide_grad, turned, preferred_element_type=jnp.float32)
        grad = (
            grad.astype(jnp.float32) + hidden_grad * gelu_slope(start_state.astype(jnp.float32))
        ).astype(jnp.bfloat16)
    parts = jnp.stack(parts[::-1])
    total = lax.psum_scatter(parts, "section", scatter_dimension=0, tiled=True)
    total = lax.psum(total[0], ("seq", "dp"))
    taps_width = total.shape[1] - channels
    conv_sum = total[:, :taps_width].T.reshape(conv_weight.shape)
    return conv_sum, total[:, taps_width:][None], head_sum


def paired_body(bases, targets, stem_weight, conv_weight, proj_weight, head_weight):
    sections = lax.axis_size("section")
    zones = lax.axis_size("dp")
    batches, half, bin_width = bases.shape
    channels = stem_weight.shape[1]
    inner = proj_weight.shape[1]
    length = batches * half
    unit = length // 2**sections
    factor = 1.0 / math.sqrt(batches * zones * length)
    taps = conv_weight[0].transpose(0, 2, 1).reshape(3 * inner, channels)
    top, weights, hidden, slope, active, bend = forward_tower(
        bases, stem_weight, taps, proj_weight[0], sections, unit
    )
    head_part, cot = head(top, targets, head_weight, factor)
    cot = cot.reshape(length, channels)
    total, head_sum = backward_tower(
        head_part, cot, weights, hidden, slope, active, bend, sections, zones, unit
    )
    conv_sum, proj_sum, head_sum = finish(total, head_sum, 3 * inner)
    conv_sum = conv_sum.reshape(3, inner, channels).transpose(0, 2, 1)
    return conv_sum[None], proj_sum[None], head_sum


def body(bases, targets, stem_weight, conv_weight, proj_weight, head_weight):
    sections, zones = lax.axis_size("section"), lax.axis_size("dp")
    batches, half = bases.shape[:2]
    inner = proj_weight.shape[1]
    unit = batches * half // 2**sections
    paired = lax.axis_size("seq") == 2 and batches == 2 and zones > 1 and sections > 1
    paired = paired and unit % 16 == 0 and half % 16 == 0 and inner % 16 == 0
    paired = paired and (2 * inner) % (16 * sections) == 0
    paired = paired and (2 * inner) % (8 * sections * zones) == 0
    paired = paired and zones & (zones - 1) == 0
    paired = paired and stem_weight.shape[1] % (16 * zones) == 0
    run = paired_body if paired else plain_body
    return run(bases, targets, stem_weight, conv_weight, proj_weight, head_weight)


def solution(mesh):
    in_specs = (
        P("dp", "seq", None),
        P("dp", "seq", "section"),
        P(),
        P("section", None, None, None),
        P("section", None, None),
        P(None, "section"),
    )
    out_specs = (P("section", None, None, None), P("section", None, None), P(None, "section"))
    return jax.shard_map(body, mesh=mesh, in_specs=in_specs, out_specs=out_specs, check_vma=False)
```
